128 devices in a mesh: expert: 8 (over x, z_lo), fsdp: 16 (over y, z_hi, core).
Axes of the slice: x: 4, y: 4, z: 4 (z_hi: 2, z_lo: 2; z = z_hi * 2 + z_lo), core: 2. Of those that a mesh axis runs over, the one named last changes fastest.
Arguments:
- tokens: bfloat16 [16, 1024, 1536], P('fsdp', 'expert'), may hold values from -6 to 6
- seg_ids: int32 [16, 1024], P('fsdp'), may hold values from 0 to 1023, as said below
- routes: int32 [16, 1024, 8], P('fsdp', 'expert'), may hold values from 0 to 39, all different within a row; in each aligned block of 128 rows (0 to 127, 128 to 255, ..., all dimensions but the last counted through in order) at most 48 rows name the same one
- gain_attn: bfloat16 [1536], P('fsdp'), may hold values from 0.5 to 1.5
- query_key_value_weight: bfloat16 [1536, 2560], P('fsdp'), may hold values from -0.15625 to 0.15625
- w_out: bfloat16 [1536, 1536], P('fsdp'), may hold values from -0.875 to 0.875
- gain_moe: bfloat16 [1536], P('fsdp'), may hold values from 0.5 to 1.5
- w_router: bfloat16 [1536, 40], P('fsdp'), may hold values from -0.078125 to 0.078125
- w_gate_up: bfloat16 [40, 1536, 1024], P('expert', 'fsdp'), may hold values from -0.15625 to 0.15625
- w_down: bfloat16 [40, 512, 1536], P('expert', 'fsdp'), may hold values from -1.5 to 1.5
- cotangent: bfloat16 [16, 1024, 1536], P('fsdp', 'expert'), may hold values from -6 to 6
Outputs:
- output: bfloat16 [16, 1024, 1536], P('fsdp', 'expert')
- grad_tokens: bfloat16 [16, 1024, 1536], P('fsdp', 'expert')
- grad_gain_attn: float32 [1536], P('fsdp')
- grad_w_qkv: float32 [1536, 2560], P('fsdp')
- grad_w_out: float32 [1536, 1536], P('fsdp')
- grad_gain_moe: float32 [1536], P('fsdp')
- grad_w_router: float32 [1536, 40], P('fsdp')
- grad_w_gate_up: float32 [40, 1536, 1024], P('expert', 'fsdp')
- grad_w_down: float32 [40, 512, 1536], P('expert', 'fsdp')
The draws below stay inside these ranges and needn't reach their ends.
Inputs may be any that keep to these rules, and one draw needn't show every extreme that they name: `seg_ids`: never falls along a sequence; a document's number is the position of its first token, so equal numbers mark one document of consecutive positions; in one sequence, drawn from the seed, a single document covers all 1024 positions, and some other sequence ends in a document of one token. `routes`: A token's 8 experts are distinct. Within each aligned block of 128 tokens (the tokens of one device) no expert is named by more than 48 tokens, and in some block some expert is named by exactly 48.
All inputs are finite; a program needn't handle non-finite values.
Results may differ from the reference program's by a relative error of at most 0.03.
Values may be sent and summed in bfloat16 or wider, within the bound.
No kernel may reach another device: no remote copies, remote signals or barrier semaphores. Data moves between devices by JAX's collectives and lax.ppermute only.
A program may use at most 192 MiB of HBM per device.

```python
import math
from functools import partial
import jax
import jax.numpy as jnp
import numpy as np
from jax import lax

MODEL_WIDTH = 1536
QUERY_HEADS = 24
KEY_VALUE_HEADS = 8
HEAD_SIZE = 64
FFE = 512
TOP = 8
SEQUENCE_TOKENS = 1024
EXPERTS = 40
TOK_DEV = 128
SEQS = 16
CAP = 48
N_EXPERT = 8


def draw_seg_ids(key, part):
    key = jax.random.fold_in(key, 11)
    key_flags, key_row = jax.random.split(key)
    mean_length = max(SEQUENCE_TOKENS // 4, 2)
    flags = (jax.random.randint(key_flags, (SEQS, SEQUENCE_TOKENS), 0, mean_length) == 0).astype(jnp.int32)
    flags = flags.at[:, 0].set(0)
    whole_row = jax.random.randint(key_row, (), 0, SEQS)
    end_row = (whole_row + 1) % SEQS
    row_numbers = jnp.arange(SEQS, dtype=jnp.int32)[:, None]
    column_numbers = jnp.arange(SEQUENCE_TOKENS, dtype=jnp.int32)[None, :]
    flags = jnp.where((row_numbers == end_row) & (column_numbers == SEQUENCE_TOKENS - 1), 1, flags)
    flags = jnp.where(row_numbers == whole_row, 0, flags)
    starts = jnp.where(flags == 1, column_numbers, 0).astype(jnp.int32)
    return lax.cummax(starts, axis=1).astype(jnp.int32)


def levels(key, extent, shards, least, high):
    factor_of = 1.0
    for position, parts in shards:
        heights = jax.random.uniform(jax.random.fold_in(jax.random.fold_in(key, 6), position), (parts,), jnp.float32, least / len(shards), high / len(shards))
        factor_of = factor_of * jnp.repeat(jnp.exp(heights), extent[position] // parts).reshape((-1,) + (1,) * (len(extent) - 1 - position))
    return factor_of


def shared_out(rng, own, number, rows, count, top, most, lean):
    ranking = jax.random.permutation(rng, count)
    heavy_load, common = load_shares(count, rows * top, most, lean, True), load_shares(count, rows * top, most, lean, False)
    places = jnp.arange(count)

    def named(lengths, offset_by):
        used = int((lengths > 0).sum())
        fixed = max(1, used // 4)
        passed = fixed + (places - fixed + offset_by * (used - fixed)) % max(1, count - fixed)
        return jnp.zeros((count,), jnp.int32).at[ranking[jnp.where(places < fixed, places, passed)]].set(jnp.asarray(lengths, jnp.int32))

    lengths = jnp.where(number % 4 == 0, named(heavy_load, number // 4), named(common, number - number // 4 - 1))
    mixed = jax.random.permutation(jax.random.fold_in(own, 3), count)
    donor, taker = mixed[0:count // 2 * 2:2], mixed[1:count // 2 * 2:2]
    slack = jnp.minimum(lengths[donor] - 1, most - lengths[taker]) // 2
    slack = jnp.where((donor == ranking[0]) | (taker == ranking[0]) | (lengths[taker] == 0), 0, jnp.maximum(slack, 0))
    passed = jax.random.randint(jax.random.fold_in(own, 4), (count // 2,), 0, 1 << 20) % (slack + 1)
    lengths = lengths.at[donor].add(-passed).at[taker].add(passed)
    items = jnp.searchsorted(jnp.cumsum(lengths), jnp.arange(rows * top), side="right").astype(jnp.int32)
    grid = items.reshape(top, rows).T
    grid = grid[jax.random.permutation(jax.random.fold_in(own, 1), rows)]
    offset_by = jax.random.randint(jax.random.fold_in(own, 2), (rows, 1), 0, top)
    return jnp.take_along_axis(grid, (jnp.arange(top)[None, :] + offset_by) % top, axis=1)


def load_shares(number_of, total, most, slope, full):
    weights = [(1 << 20) // math.isqrt(grade ** slope) + 1 for grade in range(1, number_of + 1)]
    largest = most if full else min(most, max(-(-total // number_of), total * weights[0] // sum(weights)))
    least = 1 if total - largest >= number_of - 1 else 0
    given, surplus = [largest] + [least] * (number_of - 1), total - largest - least * (number_of - 1)
    while surplus > 0:
        free = [i for i in range(1, number_of) if given[i] < largest] or [i for i in range(1, number_of) if given[i] < most]
        pool, left = sum([weights[i] for i in free]), surplus
        for i in free:
            more = min(most - given[i], max(1, left * weights[i] // pool), surplus)
            given[i] = given[i] + more
            surplus = surplus - more
    return np.array(given)


def gaussian(stream_key, extent, width, reach, pieces=(), held_as=jnp.bfloat16):
    entries = jax.random.normal(stream_key, extent, jnp.float32) * width
    if len(pieces) > 0:
        entries = levels(stream_key, extent, pieces, -0.22, 0.18) * entries
    return jnp.clip(entries, min=-reach, max=reach).astype(held_as)


def setup_inputs(seed: int = 0) -> dict:
    streams_of = jax.random.split(jax.random.key(seed), 12)
    tokens = gaussian(streams_of[0], (SEQS, SEQUENCE_TOKENS, MODEL_WIDTH), 1.0, 6.0, ((0, 16), (1, 8)))
    seg_ids = draw_seg_ids(jax.random.fold_in(streams_of[11], 71), 0)
    routes_keys = jax.random.split(jax.random.fold_in(streams_of[2], 1), SEQS * SEQUENCE_TOKENS // TOK_DEV)
    routes_turns = jax.random.permutation(jax.random.fold_in(streams_of[2], 3), SEQS * SEQUENCE_TOKENS // TOK_DEV)
    routes = jax.vmap(lambda own, number: shared_out(jax.random.fold_in(streams_of[2], 2), own, number, TOK_DEV, EXPERTS, TOP, CAP, 1))(routes_keys, routes_turns).reshape((SEQS, SEQUENCE_TOKENS, TOP))
    gain_attn = jnp.clip(1.0 + 0.1 * jax.random.normal(streams_of[3], (MODEL_WIDTH,), jnp.float32), 0.5, 1.5).astype(jnp.bfloat16)
    query_key_value_weight = gaussian(streams_of[4], (MODEL_WIDTH, (QUERY_HEADS + 2 * KEY_VALUE_HEADS) * HEAD_SIZE), MODEL_WIDTH ** -0.5, 0.15625, ((0, 16),))
    w_out = gaussian(streams_of[5], (QUERY_HEADS * HEAD_SIZE, MODEL_WIDTH), (QUERY_HEADS * HEAD_SIZE // 32) ** -0.5, 0.875, ((0, 16),))
    gain_moe = jnp.clip(1.0 + 0.1 * jax.random.normal(streams_of[6], (MODEL_WIDTH,), jnp.float32), 0.5, 1.5).astype(jnp.bfloat16)
    w_router = gaussian(streams_of[7], (MODEL_WIDTH, EXPERTS), (4 * MODEL_WIDTH) ** -0.5, 0.078125, ((0, 16),))
    w_gate_up = gaussian(streams_of[8], (EXPERTS, MODEL_WIDTH, 2 * FFE), MODEL_WIDTH ** -0.5, 0.15625, ((0, 8), (1, 16)))
    w_down = gaussian(streams_of[9], (EXPERTS, FFE, MODEL_WIDTH), (FFE // 32) ** -0.5, 1.5, ((0, 8), (1, 16)))
    cotangent = gaussian(streams_of[10], (SEQS, SEQUENCE_TOKENS, MODEL_WIDTH), 1.0, 6.0, ((0, 16), (1, 8)))
    return {"tokens": tokens, "seg_ids": seg_ids, "routes": routes, "gain_attn": gain_attn, "query_key_value_weight": query_key_value_weight, "w_out": w_out, "gain_moe": gain_moe, "w_router": w_router, "w_gate_up": w_gate_up, "w_down": w_down, "cotangent": cotangent}


@jax.custom_vjp
def lower_precision(v):
    return lax.optimization_barrier(v.astype(jnp.bfloat16)).astype(jnp.float32)

@jax.custom_vjp
def low_back(v):
    return v

def low_keep(v):
    return (lower_precision(v), None)

def low_pass(kept, grad):
    return (grad,)

def back_keep(v):
    return (v, None)

def back_low(kept, grad):
    return (lower_precision(grad),)
lower_precision.defvjp(low_keep, low_pass)
low_back.defvjp(back_keep, back_low)
EPS = 1e-06
THETA = 10000.0
LARGE_NEGATIVE = -1e+30

def rms_scale(features, gain_vec):
    inverse = lax.rsqrt(lax.optimization_barrier(jnp.mean(features * features, axis=-1, keepdims=True)) + EPS)
    return features * inverse * gain_vec

def apply_rotary(features, cosine_table, sine_table):
    half_width = features.shape[-1] // 2
    low_half = features[..., :half_width]
    high_half = features[..., half_width:]
    return jnp.concatenate([low_half * cosine_table - high_half * sine_table, high_half * cosine_table + low_half * sine_table], axis=-1)

def slot_tables(chosen):
    flat_ids = chosen.reshape(N_EXPERT, TOK_DEV * TOP).astype(jnp.int32)
    id_hot = (flat_ids[:, :, None] == jnp.arange(EXPERTS, dtype=jnp.int32)).astype(jnp.int32)
    ranks = lax.optimization_barrier(jnp.sum((jnp.cumsum(id_hot, axis=1).astype(jnp.int32) - id_hot) * id_hot, axis=2)).astype(jnp.int32)
    slot_pos = (flat_ids * CAP + ranks).astype(jnp.int32)
    row_numbers = jnp.broadcast_to(jnp.arange(TOK_DEV * TOP, dtype=jnp.int32), flat_ids.shape)

    def fill_slots(places, row_ids):
        return jnp.full((EXPERTS * CAP,), TOK_DEV * TOP, jnp.int32).at[places].set(row_ids)
    slot_src = jax.vmap(fill_slots)(slot_pos, row_numbers)
    return (slot_pos, slot_src)

def one_sequence(params, packed):
    gain_a, qkv_w, out_w, gain_m, router_w, gate_up_w, down_w = params
    inputs, segments, chosen, slot_pos, slot_src = packed
    highest = lax.Precision.HIGHEST
    score_scale = 1.0 / math.sqrt(HEAD_SIZE)
    query_total_width = QUERY_HEADS * HEAD_SIZE
    key_value_width = KEY_VALUE_HEADS * HEAD_SIZE
    normed_one = lower_precision(rms_scale(inputs, gain_a))
    projected_rows = low_back(jnp.dot(normed_one, qkv_w, precision=highest))
    positions = jnp.arange(SEQUENCE_TOKENS, dtype=jnp.int32)
    inv_freq = THETA ** (-jnp.arange(0, HEAD_SIZE, 2, dtype=jnp.float32) / HEAD_SIZE)
    angles = positions.astype(jnp.float32)[:, None] * inv_freq[None, :]
    cosine_table = jnp.cos(angles)[:, None, :]
    sine_table = jnp.sin(angles)[:, None, :]
    query_rows = lower_precision(apply_rotary(projected_rows[:, :query_total_width].reshape(SEQUENCE_TOKENS, QUERY_HEADS, HEAD_SIZE), cosine_table, sine_table))
    gathered_keys = lower_precision(apply_rotary(projected_rows[:, query_total_width:query_total_width + key_value_width].reshape(SEQUENCE_TOKENS, KEY_VALUE_HEADS, HEAD_SIZE), cosine_table, sine_table))
    gathered_values = lower_precision(projected_rows[:, query_total_width + key_value_width:].reshape(SEQUENCE_TOKENS, KEY_VALUE_HEADS, HEAD_SIZE))
    query_tile = min(512, SEQUENCE_TOKENS)

    def attend(block_in):
        query_block_size, block_pos, block_seg = block_in
        grouped_queries = query_block_size.reshape(query_tile, KEY_VALUE_HEADS, QUERY_HEADS // KEY_VALUE_HEADS, HEAD_SIZE)
        scores = low_back(jnp.einsum('qkgd,skd->kgqs', grouped_queries, gathered_keys, precision=highest) * score_scale)
        visible = (positions[None, :] <= block_pos[:, None]) & (segments[None, :] == block_seg[:, None])
        masked = jnp.where(visible, scores, LARGE_NEGATIVE)
        row_max = lax.optimization_barrier(jnp.max(masked, axis=-1, keepdims=True))
        exponent = jnp.where(visible, jnp.exp(masked - row_max), 0.0)
        row_sum = lax.optimization_barrier(jnp.sum(exponent, axis=-1, keepdims=True))
        probs = lower_precision(exponent / row_sum)
        attended_blk = jnp.einsum('kgqs,skd->qkgd', probs, gathered_values, precision=highest)
        return attended_blk.reshape(query_tile, query_total_width)
    attended = lax.map(jax.checkpoint(attend), (query_rows.reshape(-1, query_tile, QUERY_HEADS, HEAD_SIZE), positions.reshape(-1, query_tile), segments.reshape(-1, query_tile)))
    attended = low_back(lower_precision(attended.reshape(SEQUENCE_TOKENS, query_total_width)))
    resid = inputs + low_back(jnp.dot(attended, out_w, precision=highest))
    normed_two = lower_precision(rms_scale(resid, gain_m))
    logits = low_back(jnp.dot(normed_two, router_w, precision=highest))
    picked = jnp.take_along_axis(logits, chosen, axis=1)
    gates = jax.nn.softmax(picked, axis=-1)
    routed = low_back(jnp.repeat(normed_two, TOP, axis=0)).reshape(N_EXPERT, TOK_DEV * TOP, MODEL_WIDTH)
    padded = jnp.concatenate([routed, jnp.zeros((N_EXPERT, 1, MODEL_WIDTH), jnp.float32)], axis=1)
    dispatched = jax.vmap(lambda table_rows, indices: table_rows[indices])(padded, slot_src)
    dispatched = dispatched.reshape(N_EXPERT, EXPERTS, CAP, MODEL_WIDTH)
    pre_act = low_back(jnp.einsum('becd,edf->becf', dispatched, gate_up_w, precision=highest))
    hidden = lower_precision(jax.nn.silu(pre_act[..., :FFE]) * pre_act[..., FFE:])
    expert_out = low_back(lower_precision(jnp.einsum('becf,efd->becd', hidden, down_w, precision=highest)))
    flat_out = expert_out.reshape(N_EXPERT, EXPERTS * CAP, MODEL_WIDTH)
    returned = jax.vmap(lambda table_rows, indices: table_rows[indices])(flat_out, slot_pos)
    returned = returned.reshape(SEQUENCE_TOKENS, TOP, MODEL_WIDTH)
    return resid + lax.optimization_barrier(jnp.sum(gates[:, :, None] * returned, axis=1))

def forward(tables, tokens_f, gain_a, qkv_w, out_w, gain_m, router_w, gate_up_w, down_w):
    params = (gain_a, qkv_w, out_w, gain_m, router_w, gate_up_w, down_w)
    segments, chosen, slot_pos, slot_src = tables
    step_fn = jax.checkpoint(partial(one_sequence, params))
    return lax.map(step_fn, (tokens_f, segments, chosen, slot_pos, slot_src))

def reference(tokens, seg_ids, routes, gain_attn, query_key_value_weight, w_out, gain_moe, w_router, w_gate_up, w_down, cotangent):
    slot_pos, slot_src = jax.vmap(slot_tables)(routes)
    tables = (seg_ids, routes, slot_pos, slot_src)
    floats = (tokens.astype(jnp.float32), gain_attn.astype(jnp.float32), query_key_value_weight.astype(jnp.float32), w_out.astype(jnp.float32), gain_moe.astype(jnp.float32), w_router.astype(jnp.float32), w_gate_up.astype(jnp.float32), w_down.astype(jnp.float32))

    def wrapped(tokens_f, gain_a, qkv_w, out_w, gain_m, router_w, gate_up_w, down_w):
        return forward(tables, tokens_f, gain_a, qkv_w, out_w, gain_m, router_w, gate_up_w, down_w)
    result, pullback = jax.vjp(wrapped, *floats)
    grads = pullback(cotangent.astype(jnp.float32))
    return (result.astype(jnp.bfloat16), grads[0].astype(jnp.bfloat16), grads[1], grads[2], grads[3], grads[4], grads[5], grads[6], grads[7])
```

```python
import math

import jax
import jax.numpy as jnp
from jax import lax
from jax.sharding import Mesh, PartitionSpec as P

QUERY_HEADS = 24
KEY_VALUE_HEADS = 8
HEAD_SIZE = 64
GROUP = QUERY_HEADS // KEY_VALUE_HEADS
FFE = 512
EXP_DEV = 5
EXPERTS = 40
WIDTH = 1536
TOK = 128
SEQ = 1024
CAP = 48
BLOCKS = 16
N_EXP = 8
N_FSDP = 16
N_YZ = 8
HALF_FFE = FFE // 2
HEAD_COLS = GROUP * HEAD_SIZE
QKV_COLS = HEAD_COLS + 2 * HEAD_SIZE
PACK = 384
SIDE = 128

EPS = 1e-06
THETA = 10000.0
LARGE_NEGATIVE = -1e30

EXP = ("x", "zl")
FSDP = ("y", "zh", "c")
YZ = ("y", "zh")
SWAP = ((0, 1), (1, 0))
BF = jnp.bfloat16
F32 = jnp.float32


def dot(a, b):
    return jnp.dot(a, b, preferred_element_type=F32)


def ein(spec, *args):
    return jnp.einsum(spec, *args, preferred_element_type=F32)


def core_swap(value):
    return lax.ppermute(value, "c", SWAP)


def to_all(value, axes, count):
    spread = jnp.broadcast_to(value[None], (count, *value.shape))
    return lax.all_to_all(spread, axes, 0, 0, tiled=True)


def exchange(value, axes):
    return lax.all_to_all(value, axes, 0, 0, tiled=True)


def rms_inverse(features):
    return lax.rsqrt(jnp.mean(features * features, axis=-1, keepdims=True) + EPS)


def rms_backward(features, inverse, gain_vec, grad_normed):
    scaled = gain_vec * grad_normed
    grad_rows = inverse * scaled - features * inverse**3 * jnp.mean(
        features * scaled, axis=-1, keepdims=True
    )
    grad_gain = jnp.sum(features * inverse * grad_normed, axis=0)
    return grad_rows, grad_gain


def rotate(features, cosine_table, sine_table):
    half = features.shape[-1] // 2
    low, high = features[..., :half], features[..., half:]
    return jnp.concatenate(
        [low * cosine_table - high * sine_table, high * cosine_table + low * sine_table], axis=-1
    )


def parity_matrix(parity):
    rows = jnp.arange(2 * FFE, dtype=jnp.int32)[:, None]
    cols = jnp.arange(FFE, dtype=jnp.int32)[None, :]
    part, rest = cols // HALF_FFE, cols % HALF_FFE
    source = part * FFE + (2 * (rest // 32) + parity) * 32 + rest % 32
    return (rows == source).astype(BF)


def split_pair(value):
    high = value.astype(BF)
    return high, (value - high.astype(F32)).astype(BF)


def body(tokens, seg_ids, routes, gain_attn, w_qkv, w_out, gain_moe, w_router, w_gate_up, w_down, cotangent):
    e = lax.axis_index(EXP)
    c = lax.axis_index("c")
    scale = 1.0 / math.sqrt(HEAD_SIZE)

    def own_columns(start, width):
        return lax.dynamic_slice_in_dim(w_qkv, start + e * width, width, axis=1)

    packet = jnp.concatenate(
        [
            own_columns(0, HEAD_COLS),
            own_columns(WIDTH, HEAD_SIZE),
            own_columns(WIDTH + KEY_VALUE_HEADS * HEAD_SIZE, HEAD_SIZE),
            w_router,
            gain_attn[:, None],
            gain_moe[:, None],
            jnp.zeros((w_qkv.shape[0], PACK - QKV_COLS - EXPERTS - 2), BF),
        ],
        axis=1,
    )
    packed = lax.all_gather(packet, FSDP, axis=0, tiled=True)
    qkv_cols = packed[:, :QKV_COLS]
    router = packed[:, QKV_COLS : QKV_COLS + EXPERTS]
    gain_one = packed[:, QKV_COLS + EXPERTS].astype(F32)
    gain_two = packed[:, QKV_COLS + EXPERTS + 1].astype(F32)
    full_out = lax.all_gather(w_out, FSDP, axis=0, tiled=True)

    mine_matrix, other_matrix = parity_matrix(c), parity_matrix(1 - c)
    flat_gu = w_gate_up.reshape(EXP_DEV * 96, 2 * FFE)
    gu_mine = dot(flat_gu, mine_matrix).astype(BF).reshape(EXP_DEV, 96, FFE)
    gu_other = dot(flat_gu, other_matrix).astype(BF).reshape(EXP_DEV, 96, FFE)
    gu_recv = core_swap(gu_other)
    gu_rows = jnp.where(
        c == 0,
        jnp.concatenate([gu_mine, gu_recv], axis=1),
        jnp.concatenate([gu_recv, gu_mine], axis=1),
    )
    gu_full = lax.all_gather(gu_rows, YZ, axis=1, tiled=True)
    dn_full = lax.all_gather(w_down, YZ, axis=1, tiled=True)

    tok_all = to_all(tokens[0], EXP, N_EXP).reshape(SEQ, WIDTH).astype(F32)
    cot_packet = jnp.concatenate(
        [cotangent[0], routes[0].astype(BF), jnp.zeros((TOK, SIDE - routes.shape[-1]), BF)], axis=1
    )
    cot_all = to_all(cot_packet, EXP, N_EXP).reshape(SEQ, WIDTH + SIDE)
    cot_pair = jnp.stack([cot_all, core_swap(cot_all)])

    inv_one = rms_inverse(tok_all)
    normed_one = (tok_all * inv_one * gain_one).astype(BF)
    projected = dot(normed_one, qkv_cols)
    positions = jnp.arange(SEQ, dtype=jnp.int32)
    inv_freq = THETA ** (-jnp.arange(0, HEAD_SIZE, 2, dtype=F32) / HEAD_SIZE)
    angles = positions.astype(F32)[:, None] * inv_freq[None, :]
    cosine, sine = jnp.cos(angles), jnp.sin(angles)
    queries = rotate(
        jnp.transpose(projected[:, :HEAD_COLS].reshape(SEQ, GROUP, HEAD_SIZE), (1, 0, 2)), cosine, sine
    ).astype(BF)
    keys = rotate(projected[:, HEAD_COLS : HEAD_COLS + HEAD_SIZE], cosine, sine).astype(BF)
    values = projected[:, HEAD_COLS + HEAD_SIZE :].astype(BF)
    seg = seg_ids[0]
    visible = (positions[None, :] <= positions[:, None]) & (seg[None, :] == seg[:, None])

    def softmax_rows(row_max=None, row_sum=None):
        scores = jnp.where(visible, ein("hqd,kd->hqk", queries, keys) * scale, LARGE_NEGATIVE)
        if row_max is None:
            row_max = jnp.max(scores, axis=-1, keepdims=True)
        weights = jnp.where(visible, jnp.exp(scores - row_max), 0.0)
        if row_sum is None:
            row_sum = jnp.sum(weights, axis=-1, keepdims=True)
        return weights / row_sum, row_max, row_sum

    soft, row_max, row_sum = softmax_rows()
    attended = ein("hqk,kd->hqd", soft.astype(BF), values)
    attended_low = jnp.transpose(attended, (1, 0, 2)).reshape(SEQ, HEAD_COLS).astype(BF)
    attended_all = to_all(attended_low, EXP, N_EXP)

    resid = tok_all + ein("etk,ekn->tn", attended_all, full_out.reshape(N_EXP, HEAD_COLS, WIDTH))
    inv_two = rms_inverse(resid)
    normed_two = (resid * inv_two * gain_two).astype(BF)

    normed_pair = jnp.stack([normed_two, core_swap(normed_two)])
    logits = dot(normed_pair.reshape(2 * SEQ, WIDTH), router)
    routes_pair = cot_pair[:, :, WIDTH : WIDTH + routes.shape[-1]].reshape(2 * SEQ, -1).astype(jnp.int32)
    chosen = jnp.any(routes_pair[:, :, None] == jnp.arange(EXPERTS, dtype=jnp.int32), axis=1)
    masked = jnp.where(chosen, logits, LARGE_NEGATIVE)
    exps = jnp.where(chosen, jnp.exp(masked - jnp.max(masked, axis=-1, keepdims=True)), 0.0)
    gates = exps / jnp.sum(exps, axis=-1, keepdims=True)
    gates_own = lax.dynamic_slice_in_dim(gates, e * EXP_DEV, EXP_DEV, axis=1).reshape(BLOCKS, TOK, EXP_DEV)
    hit = lax.dynamic_slice_in_dim(chosen, e * EXP_DEV, EXP_DEV, axis=1).reshape(BLOCKS, TOK, EXP_DEV)
    before = (jnp.arange(TOK)[:, None] > jnp.arange(TOK)[None, :]).astype(BF)
    ranks = ein("ts,bsj->bjt", before, hit.astype(BF)).astype(jnp.int32)
    hit_t = jnp.transpose(hit, (0, 2, 1))
    taken = (ranks[:, :, None, :] == jnp.arange(CAP, dtype=jnp.int32)[:, None]) & hit_t[:, :, None, :]
    one_hot = taken.astype(BF)
    slot_gates = jnp.sum(
        jnp.where(taken, jnp.transpose(gates_own, (0, 2, 1))[:, :, None, :], 0.0), axis=-1
    )
    slot_gates = jnp.transpose(slot_gates, (1, 0, 2)).reshape(EXP_DEV, BLOCKS * CAP)[:, :, None]

    def dispatch(rows):
        placed = ein("bjct,btd->jbcd", one_hot, rows.reshape(BLOCKS, TOK, WIDTH)).astype(BF)
        return placed.reshape(EXP_DEV, BLOCKS * CAP, WIDTH)

    def combine(rows):
        return ein(
            "bjct,jbcd->btd", one_hot, rows.reshape(EXP_DEV, BLOCKS, CAP, -1)
        ).reshape(2, SEQ, -1)

    received = dispatch(normed_pair)
    upstream_slots = dispatch(cot_pair[:, :, :WIDTH])
    pre_act = ein("jrd,jdf->jrf", received, gu_full)
    gate_part, up_part = pre_act[..., :HALF_FFE], pre_act[..., HALF_FFE:]
    sigmoid_gate = jax.nn.sigmoid(gate_part)
    silu_gate = gate_part * sigmoid_gate
    hidden = (silu_gate * up_part).astype(BF)
    hidden_gated = (hidden.astype(F32) * slot_gates).astype(BF)
    grad_plain = ein("jrd,jfd->jrf", upstream_slots, dn_full)
    gate_grad_slots = jnp.sum(hidden.astype(F32) * grad_plain, axis=-1)
    grad_down = ein("jrf,jrd->jfd", hidden_gated, upstream_slots).astype(BF)
    out_slots = ein("jrf,jfd->jrd", hidden_gated, dn_full).astype(BF)
    grad_hidden = grad_plain * slot_gates
    grad_pre = jnp.concatenate(
        [
            grad_hidden * up_part * sigmoid_gate * (1.0 + gate_part * (1.0 - sigmoid_gate)),
            grad_hidden * silu_gate,
        ],
        axis=-1,
    ).astype(BF)
    grad_sent = ein("jrf,jdf->jrd", grad_pre, gu_full).astype(BF)
    grad_gate_up = ein("jrd,jrf->jdf", received, grad_pre).astype(BF)

    routed_grad = combine(grad_sent)
    gate_grads = jnp.sum(
        jnp.where(
            taken,
            jnp.transpose(gate_grad_slots.reshape(EXP_DEV, BLOCKS, CAP), (1, 0, 2))[..., None],
            0.0,
        ),
        axis=2,
    )
    gate_grads = jnp.transpose(gate_grads, (0, 2, 1)).reshape(2, SEQ, EXP_DEV)

    def with_side(main, side):
        high, low = split_pair(side)
        zeros = jnp.zeros((*side.shape[:-1], SIDE - 2 * EXP_DEV), BF)
        return jnp.concatenate([main.astype(BF), high, low, zeros], axis=-1)

    def read_side(block):
        block = block.astype(F32)
        return block[..., WIDTH : WIDTH + EXP_DEV] + block[..., WIDTH + EXP_DEV : WIDTH + 2 * EXP_DEV]

    from_core = core_swap(with_side(routed_grad[1], gate_grads[1]))
    routed_sum = routed_grad[0] + from_core[:, :WIDTH].astype(F32)
    gate_sum = gate_grads[0] + read_side(from_core)
    routed_back = exchange(with_side(routed_sum, gate_sum).reshape(N_EXP, TOK, WIDTH + SIDE), EXP)
    routed_total = jnp.sum(routed_back[..., :WIDTH].astype(F32), axis=0)
    grad_gates = jnp.transpose(read_side(routed_back), (1, 0, 2)).reshape(TOK, EXPERTS)

    out_part = combine(out_slots)
    out_sum = out_part[0] + core_swap(out_part[1].astype(BF)).astype(F32)
    out_back = exchange(out_sum.astype(BF).reshape(N_EXP, TOK, WIDTH), EXP)

    def own_rows(value):
        return lax.dynamic_slice_in_dim(value, e * TOK, TOK, axis=0)

    resid_own, inv_two_own, normed_two_own = own_rows(resid), own_rows(inv_two), own_rows(normed_two)
    output = (resid_own + jnp.sum(out_back.astype(F32), axis=0)).astype(BF)
    gates_tok = own_rows(gates)
    upstream = cotangent[0].astype(F32)
    grad_logits = (
        gates_tok * (grad_gates - jnp.sum(gates_tok * grad_gates, axis=-1, keepdims=True))
    ).astype(BF)
    router_part = dot(normed_two_own.T, grad_logits)
    grad_normed_two = dot(grad_logits, router.T) + routed_total
    grad_rows, gain_two_part = rms_backward(resid_own, inv_two_own, gain_two, grad_normed_two)
    grad_resid = upstream + grad_rows
    grad_branch = grad_resid.astype(BF)
    grad_attended_own = ein("tn,ekn->etk", grad_branch, full_out.reshape(N_EXP, HEAD_COLS, WIDTH)).astype(BF)
    branch_blocks = jnp.transpose(grad_branch.reshape(TOK, N_EXP, HEAD_COLS), (1, 0, 2))
    back = exchange(jnp.concatenate([grad_attended_own, branch_blocks], axis=-1), EXP)
    grad_attended = jnp.transpose(back[..., :HEAD_COLS].reshape(SEQ, GROUP, HEAD_SIZE), (1, 0, 2))
    branch_cols = back[..., HEAD_COLS:].reshape(SEQ, HEAD_COLS)
    out_grad_part = ein("etk,tn->ekn", attended_all, branch_cols).reshape(WIDTH, HEAD_COLS)

    def reduce_over_all(parts):
        sent = parts.astype(BF).reshape(N_FSDP, WIDTH // N_FSDP, -1)
        summed = jnp.sum(exchange(sent, FSDP).astype(F32), axis=0).astype(BF)
        return to_all(summed, EXP, N_EXP).astype(F32)

    first_totals = reduce_over_all(
        jnp.concatenate(
            [
                out_grad_part,
                router_part,
                gain_two_part[:, None],
                jnp.zeros((WIDTH, 256 - HEAD_COLS - EXPERTS - 1), F32),
            ],
            axis=1,
        )
    )
    total_out = jnp.transpose(first_totals[..., :HEAD_COLS], (1, 0, 2)).reshape(-1, WIDTH)
    shared = jnp.sum(first_totals[..., HEAD_COLS : HEAD_COLS + EXPERTS + 1], axis=0)

    soft, _, _ = softmax_rows(row_max, row_sum)
    delta = jnp.sum(grad_attended.astype(F32) * attended, axis=-1, keepdims=True)
    grad_probs = ein("hqd,kd->hqk", grad_attended, values)
    grad_scores = (soft * (grad_probs - delta)).astype(BF)
    grad_values = ein("hqk,hqd->kd", soft.astype(BF), grad_attended)
    grad_queries = ein("hqk,kd->hqd", grad_scores, keys) * scale
    grad_keys = ein("hqk,hqd->kd", grad_scores, queries) * scale
    grad_projected = jnp.concatenate(
        [
            jnp.transpose(rotate(grad_queries, cosine, -sine), (1, 0, 2)).reshape(SEQ, HEAD_COLS),
            rotate(grad_keys, cosine, -sine),
            grad_values,
        ],
        axis=1,
    ).astype(BF)
    normed_grad_part = dot(grad_projected, qkv_cols.T).astype(BF)
    normed_back = exchange(normed_grad_part.reshape(N_EXP, TOK, WIDTH), EXP)
    grad_normed_one = jnp.sum(normed_back.astype(F32), axis=0)
    grad_in, gain_one_part = rms_backward(
        tokens[0].astype(F32), own_rows(inv_one), gain_one, grad_normed_one
    )
    grad_tokens = (grad_resid + grad_in).astype(BF)
    qkv_grad_part = dot(normed_one.T, grad_projected)
    last_totals = reduce_over_all(
        jnp.concatenate(
            [qkv_grad_part, gain_one_part[:, None], jnp.zeros((WIDTH, PACK - QKV_COLS - 1), F32)], axis=1
        )
    )

    def head_columns(start, width):
        return jnp.transpose(last_totals[..., start : start + width], (1, 0, 2)).reshape(-1, N_EXP * width)

    total_qkv = jnp.concatenate(
        [
            head_columns(0, HEAD_COLS),
            head_columns(HEAD_COLS, HEAD_SIZE),
            head_columns(HEAD_COLS + HEAD_SIZE, HEAD_SIZE),
        ],
        axis=1,
    )
    total_gain_one = jnp.sum(last_totals[..., QKV_COLS], axis=0)

    down_sent = jnp.transpose(grad_down.reshape(EXP_DEV, N_YZ, 32, WIDTH), (1, 0, 2, 3))
    total_down = jnp.sum(exchange(down_sent, YZ).astype(F32), axis=0)
    gu_sent = jnp.transpose(grad_gate_up.reshape(EXP_DEV, N_YZ, 192, FFE), (1, 0, 2, 3))
    gu_sum = jnp.sum(exchange(gu_sent, YZ).astype(F32), axis=0).astype(BF)
    first_rows, second_rows = gu_sum[:, :96], gu_sum[:, 96:]
    keep = jnp.where(c == 0, first_rows, second_rows).reshape(-1, FFE)
    arrived = core_swap(jnp.where(c == 0, second_rows, first_rows)).reshape(-1, FFE)
    total_gu = (dot(keep, mine_matrix.T) + dot(arrived, other_matrix.T)).reshape(EXP_DEV, 96, 2 * FFE)

    return (
        output[None],
        grad_tokens[None],
        total_gain_one,
        total_qkv,
        total_out,
        shared[:, EXPERTS],
        shared[:, :EXPERTS],
        total_gu,
        total_down,
    )


def solution(mesh):
    fine = Mesh(mesh.devices.reshape(4, 2, 4, 2, 2), ("x", "zl", "y", "zh", "c"))
    rows = P(FSDP, EXP, None)
    weight = P(FSDP, None)
    expert_weight = P(EXP, FSDP, None)
    in_specs = (
        rows,
        P(FSDP, None),
        rows,
        P(FSDP),
        weight,
        weight,
        P(FSDP),
        weight,
        expert_weight,
        expert_weight,
        rows,
    )
    out_specs = (rows, rows, P(FSDP), weight, weight, P(FSDP), weight, expert_weight, expert_weight)
    return jax.shard_map(body, mesh=fine, in_specs=in_specs, out_specs=out_specs, check_vma=False)
```

```python
import math

import jax
import jax.numpy as jnp
from jax import lax
from jax.experimental import pallas as pl
from jax.experimental.pallas import tpu as pltpu
from jax.sharding import Mesh, PartitionSpec as P

QUERY_HEADS = 24
KEY_VALUE_HEADS = 8
HEAD_SIZE = 64
GROUP = QUERY_HEADS // KEY_VALUE_HEADS
FFE = 512
EXP_DEV = 5
EXPERTS = 40
WIDTH = 1536
TOK = 128
SEQ = 1024
CAP = 48
BLOCKS = 16
N_EXP = 8
N_FSDP = 16
N_YZ = 8
HALF_FFE = FFE // 2
HEAD_COLS = GROUP * HEAD_SIZE
QKV_COLS = HEAD_COLS + 2 * HEAD_SIZE
PACK = 384
SIDE = 128
SLOTS = EXP_DEV * CAP
ROWS = BLOCKS * CAP
CHUNK = 256
PARTS = 2
STEPS = BLOCKS // PARTS
GU_ROWS = WIDTH // N_YZ
MIX_ROWS = GU_ROWS + 32 * WIDTH // FFE
TILE = 256
TILES = SEQ // TILE
QK_COLS = HEAD_COLS + HEAD_SIZE
SCALE = 1.0 / math.sqrt(HEAD_SIZE)

EPS = 1e-06
THETA = 10000.0
LARGE_NEGATIVE = -1e30

EXP = ("x", "zl")
FSDP = ("y", "zh", "c")
YZ = ("y", "zh")
SWAP = ((0, 1), (1, 0))
BF = jnp.bfloat16
F32 = jnp.float32


def dot(a, b):
    return jnp.dot(a, b, preferred_element_type=F32)


def ein(spec, *args):
    return jnp.einsum(spec, *args, preferred_element_type=F32)


def core_swap(value):
    return lax.ppermute(value, "c", SWAP)


def to_all(value, axes, count):
    spread = jnp.broadcast_to(value[None], (count, *value.shape))
    return lax.all_to_all(spread, axes, 0, 0, tiled=True)


def exchange(value, axes):
    return lax.all_to_all(value, axes, 0, 0, tiled=True)


def rms_inverse(features):
    return lax.rsqrt(jnp.mean(features * features, axis=-1, keepdims=True) + EPS)


def rms_backward(features, inverse, gain_vec, grad_normed):
    scaled = gain_vec * grad_normed
    grad_rows = inverse * scaled - features * inverse**3 * jnp.mean(
        features * scaled, axis=-1, keepdims=True
    )
    grad_gain = jnp.sum(features * inverse * grad_normed, axis=0)
    return grad_rows, grad_gain


def parity_matrix(parity):
    rows = jnp.arange(2 * FFE, dtype=jnp.int32)[:, None]
    cols = jnp.arange(FFE, dtype=jnp.int32)[None, :]
    part, rest = cols // HALF_FFE, cols % HALF_FFE
    source = part * FFE + (2 * (rest // 32) + parity) * 32 + rest % 32
    return (rows == source).astype(BF)


def contract(a, b, dims):
    return lax.dot_general(a, b, (dims, ((), ())), preferred_element_type=F32)


def expert_kernel(
    n_own, n_par, g_own, g_par, chosen, router, weights,
    out_own, out_par, back_own, back_par, grads,
    x_slots, g_slots, side_slots, gate_slots, sum_gate_up, sum_down,
):
    step = pl.program_id(0)
    token = lax.broadcasted_iota(jnp.int32, (TOK, TOK), 0)
    other = lax.broadcasted_iota(jnp.int32, (TOK, TOK), 1)

    @pl.when(step < STEPS)
    def dispatch():
        def place(n_ref, g_ref, part):
            here = slice(part * TOK, (part + 1) * TOK)
            rows = n_ref[here, :]
            picks = chosen[here, :]
            logits = jnp.dot(rows, router[...], preferred_element_type=F32)
            keep = picks > 0
            masked = jnp.where(keep, logits, LARGE_NEGATIVE)
            exps = jnp.where(keep, jnp.exp(masked - jnp.max(masked, axis=-1, keepdims=True)), 0.0)
            gates = exps / jnp.sum(exps, axis=-1, keepdims=True)
            ranks = contract(picks, (token < other).astype(BF), ((0,), (0,)))
            named = contract(picks, (token == other).astype(BF), ((0,), (0,)))
            ranks = jnp.where(named > 0, ranks, -1.0).astype(jnp.int32)
            slot = lax.broadcasted_iota(jnp.int32, (CAP, TOK), 0)
            one_hot = jnp.concatenate(
                [(slot == ranks[j : j + 1, :]).astype(F32) for j in range(EXP_DEV)], axis=0
            ).astype(BF)
            high = gates.astype(BF)
            rest = gates - high.astype(F32)
            middle = rest.astype(BF)
            low = (rest - middle.astype(F32)).astype(BF)
            spread = (
                jnp.dot(one_hot, high, preferred_element_type=F32)
                + jnp.dot(one_hot, middle, preferred_element_type=F32)
                + jnp.dot(one_hot, low, preferred_element_type=F32)
            )
            lane = lax.broadcasted_iota(jnp.int32, (CAP, TOK), 1)
            x = jnp.dot(one_hot, rows, preferred_element_type=F32).astype(BF)
            g = jnp.dot(one_hot, g_ref[here, :], preferred_element_type=F32).astype(BF)
            start = pl.multiple_of((step * PARTS + part) * CAP, 16)
            for j in range(EXP_DEV):
                piece = slice(j * CAP, (j + 1) * CAP)
                x_slots[j, pl.ds(start, CAP), :] = x[piece]
                g_slots[j, pl.ds(start, CAP), :] = g[piece]
                gate_slots[j, pl.ds(start, CAP), :] = jnp.sum(
                    jnp.where(lane == j, spread[piece], 0.0), axis=-1, keepdims=True
                )

        @pl.when(step < STEPS // 2)
        def _():
            for part in range(PARTS):
                place(n_own, g_own, part)

        @pl.when(step >= STEPS // 2)
        def _():
            for part in range(PARTS):
                place(n_par, g_par, part)

    @pl.when((step >= STEPS) & (step < STEPS + EXP_DEV))
    def experts():
        j = step - STEPS
        gate_up = weights[:, 0, :GU_ROWS, :].reshape(WIDTH, FFE)
        down = jnp.concatenate(
            [
                weights[:, 0, GU_ROWS + 32 * p : GU_ROWS + 32 * (p + 1), :].reshape(HALF_FFE, FFE)
                for p in range(WIDTH // FFE)
            ],
            axis=1,
        )
        sum_gate_up[...] = jnp.zeros_like(sum_gate_up)
        sum_down[...] = jnp.zeros_like(sum_down)

        @pl.loop(0, ROWS // CHUNK)
        def _(part):
            here = pl.ds(pl.multiple_of(part * CHUNK, CHUNK), CHUNK)
            x = x_slots[j, here, :]
            g = g_slots[j, here, :]
            gates = gate_slots[j, here, :]
            pre = jnp.dot(x, gate_up, preferred_element_type=F32)
            plain = contract(g, down, ((1,), (1,)))
            gate, up = pre[:, :HALF_FFE], pre[:, HALF_FFE:]
            sigmoid = jax.nn.sigmoid(gate)
            silu = gate * sigmoid
            hidden = (silu * up).astype(BF).astype(F32)
            gated = (hidden * gates).astype(BF)
            slope = jnp.sum(hidden * plain, axis=-1, keepdims=True)
            high = slope.astype(BF).astype(F32)
            lane = lax.broadcasted_iota(jnp.int32, (CHUNK, SIDE), 1)
            row = lax.broadcasted_iota(jnp.int32, (CHUNK, SIDE), 0) + part * CHUNK
            lane = jnp.where(row < ROWS // 2, lane, lane - 2 * EXP_DEV)
            side_slots[j, here, :] = jnp.where(
                lane == j, high, jnp.where(lane == j + EXP_DEV, slope - high, 0.0)
            ).astype(BF)
            grad_hidden = plain * gates
            grad_pre = jnp.concatenate(
                [grad_hidden * up * sigmoid * (1.0 + gate * (1.0 - sigmoid)), grad_hidden * silu], axis=-1
            ).astype(BF)
            sum_down[...] += contract(gated, g, ((0,), (0,)))
            sum_gate_up[...] += contract(x, grad_pre, ((0,), (0,)))
            g_slots[j, here, :] = jnp.dot(gated, down, preferred_element_type=F32).astype(BF)
            x_slots[j, here, :] = contract(grad_pre, gate_up, ((1,), (1,))).astype(BF)

        grads[:, 0, :GU_ROWS, :] = sum_gate_up[...].astype(BF).reshape(N_YZ, GU_ROWS, FFE)
        for p in range(WIDTH // FFE):
            grads[:, 0, GU_ROWS + 32 * p : GU_ROWS + 32 * (p + 1), :] = (
                sum_down[:, p * FFE : (p + 1) * FFE].astype(BF).reshape(N_YZ, 32, FFE)
            )

    @pl.when(step >= STEPS + EXP_DEV)
    def combine():
        block = step - STEPS - EXP_DEV

        def write(out_ref, back_ref, part):
            here = slice(part * TOK, (part + 1) * TOK)
            start = pl.multiple_of((block * PARTS + part) * CAP, 16)
            picks = chosen[here, :]
            ranks = jnp.dot((token > other).astype(BF), picks, preferred_element_type=F32).astype(jnp.int32)
            lane = lax.broadcasted_iota(jnp.int32, (TOK, SLOTS), 1)
            hot = jnp.zeros((TOK, SLOTS), F32)
            for j in range(EXP_DEV):
                hit = (picks[:, j : j + 1] > 0) & (lane == ranks[:, j : j + 1] + j * CAP)
                hot = jnp.where(hit, 1.0, hot)
            hot = hot.astype(BF)

            def rows_of(ref):
                return jnp.concatenate([ref[j, pl.ds(start, CAP), :] for j in range(EXP_DEV)], axis=0)

            out_ref[here, :] = jnp.dot(hot, rows_of(g_slots), preferred_element_type=F32).astype(BF)
            back_ref[here, :WIDTH] = jnp.dot(hot, rows_of(x_slots), preferred_element_type=F32).astype(BF)
            back_ref[here, WIDTH:] = jnp.dot(hot, rows_of(side_slots), preferred_element_type=F32).astype(BF)

        @pl.when(block < STEPS // 2)
        def _():
            for part in range(PARTS):
                write(out_own, back_own, part)

        @pl.when(block >= STEPS // 2)
        def _():
            for part in range(PARTS):
                write(out_par, back_par, part)


def experts_call(n_own, n_par, g_own, g_par, chosen, router, weights):
    half = STEPS // 2
    last = STEPS + EXP_DEV
    span = PARTS * TOK

    def first(i):
        return (jnp.clip(i, 0, half - 1), 0)

    def second(i):
        return (jnp.clip(i - half, 0, half - 1), 0)

    def any_block(i):
        return (jnp.where(i < last, jnp.clip(i, 0, STEPS - 1), i - last), 0)

    def grad(i):
        return (0, jnp.clip(i - STEPS, 0, EXP_DEV - 1), 0, 0)

    def out_first(i):
        return (jnp.clip(i - last, 0, half - 1), 0)

    def out_second(i):
        return (jnp.clip(i - last - half, 0, half - 1), 0)

    shape = jax.ShapeDtypeStruct
    return pl.pallas_call(
        expert_kernel,
        grid=(2 * STEPS + EXP_DEV,),
        in_specs=[
            pl.BlockSpec((span, WIDTH), first),
            pl.BlockSpec((span, WIDTH), second),
            pl.BlockSpec((span, WIDTH), first),
            pl.BlockSpec((span, WIDTH), second),
            pl.BlockSpec((span, SIDE), any_block),
            pl.BlockSpec((WIDTH, SIDE), lambda i: (0, 0)),
            pl.BlockSpec((N_YZ, 1, MIX_ROWS, FFE), grad),
        ],
        out_specs=[
            pl.BlockSpec((span, WIDTH), out_first),
            pl.BlockSpec((span, WIDTH), out_second),
            pl.BlockSpec((span, WIDTH + SIDE), out_first),
            pl.BlockSpec((span, WIDTH + SIDE), out_second),
            pl.BlockSpec((N_YZ, 1, MIX_ROWS, FFE), grad),
        ],
        out_shape=[
            shape((SEQ, WIDTH), BF),
            shape((SEQ, WIDTH), BF),
            shape((SEQ, WIDTH + SIDE), BF),
            shape((SEQ, WIDTH + SIDE), BF),
            shape((N_YZ, EXP_DEV, MIX_ROWS, FFE), BF),
        ],
        scratch_shapes=[
            pltpu.VMEM((EXP_DEV, ROWS, WIDTH), BF),
            pltpu.VMEM((EXP_DEV, ROWS, WIDTH), BF),
            pltpu.VMEM((EXP_DEV, ROWS, SIDE), BF),
            pltpu.VMEM((EXP_DEV, ROWS, 1), F32),
            pltpu.VMEM((WIDTH, FFE), F32),
            pltpu.VMEM((HALF_FFE, WIDTH), F32),
        ],
        compiler_params=pltpu.CompilerParams(
            dimension_semantics=("arbitrary",), vmem_limit_bytes=60 * 1024 * 1024
        ),
        cost_estimate=pl.CostEstimate(flops=40_000_000_000, bytes_accessed=60_000_000, transcendentals=1_000_000),
        name="experts",
    )(n_own, n_par, g_own, g_par, chosen, router, weights)


def swap_halves(value):
    width = value.shape[-1]
    lane = lax.broadcasted_iota(jnp.int32, value.shape, 1)
    return jnp.where(
        lane % HEAD_SIZE < HEAD_SIZE // 2,
        pltpu.roll(value, width - HEAD_SIZE // 2, 1),
        pltpu.roll(value, HEAD_SIZE // 2, 1),
    )


def visible_tile(tile, count, seg_rows, seg_cols):
    row = lax.broadcasted_iota(jnp.int32, (TILE, count), 0) + tile * TILE
    col = lax.broadcasted_iota(jnp.int32, (TILE, count), 1)
    return (col <= row) & (seg_rows[...] == seg_cols[:, :count])


def attend_kernel(
    tokens, packed, gain, cosine, sine, seg_rows, seg_cols,
    normed, heads, attended, attended_low, stats, keys, values,
):
    step = pl.program_id(0)
    features = tokens[...].astype(F32)
    inverse = lax.rsqrt(jnp.mean(features * features, axis=-1, keepdims=True) + EPS)
    rows = (features * inverse * gain[...]).astype(BF)
    normed[...] = rows
    projected = jnp.dot(rows, packed[...], preferred_element_type=F32)
    turned = projected[:, :QK_COLS]
    turned = (turned * cosine[...] + swap_halves(turned) * sine[...]).astype(BF)
    value_rows = projected[:, QK_COLS:QKV_COLS].astype(BF)
    heads[:, :QK_COLS] = turned
    heads[:, QK_COLS:] = jnp.concatenate([value_rows, jnp.zeros_like(value_rows)], axis=1)
    here = pl.ds(pl.multiple_of(step * TILE, TILE), TILE)
    keys[here, :] = turned[:, HEAD_COLS:]
    values[here, :] = value_rows

    for tile in range(TILES):

        @pl.when(step == tile)
        def _(tile=tile):
            count = (tile + 1) * TILE
            visible = visible_tile(tile, count, seg_rows, seg_cols)
            key_rows, value_all = keys[:count, :], values[:count, :]
            parts = []
            for h in range(GROUP):
                query = turned[:, h * HEAD_SIZE : (h + 1) * HEAD_SIZE]
                scores = contract(query, key_rows, ((1,), (1,))) * SCALE
                scores = jnp.where(visible, scores, LARGE_NEGATIVE)
                top = jnp.max(scores, axis=-1, keepdims=True)
                weights = jnp.where(visible, jnp.exp(scores - top), 0.0)
                total = jnp.sum(weights, axis=-1, keepdims=True)
                soft = (weights / total).astype(BF)
                parts.append(jnp.dot(soft, value_all, preferred_element_type=F32))
                stats[:, 2 * h : 2 * h + 1] = top
                stats[:, 2 * h + 1 : 2 * h + 2] = total
            result = jnp.concatenate(parts, axis=1)
            attended[...] = result
            attended_low[...] = result.astype(BF)


def attend_call(tokens, packed, gain, cosine, sine, seg_rows, seg_cols):
    def rows(i):
        return (i, 0)

    def whole(i):
        return (0, 0)

    shape = jax.ShapeDtypeStruct
    return pl.pallas_call(
        attend_kernel,
        grid=(TILES,),
        in_specs=[
            pl.BlockSpec((TILE, WIDTH), rows),
            pl.BlockSpec((WIDTH, PACK), whole),
            pl.BlockSpec((1, WIDTH), whole),
            pl.BlockSpec((TILE, QK_COLS), rows),
            pl.BlockSpec((TILE, QK_COLS), rows),
            pl.BlockSpec((TILE, 1), rows),
            pl.BlockSpec((1, SEQ), whole),
        ],
        out_specs=[
            pl.BlockSpec((TILE, WIDTH), rows),
            pl.BlockSpec((TILE, PACK), rows),
            pl.BlockSpec((TILE, HEAD_COLS), rows),
            pl.BlockSpec((TILE, HEAD_COLS), rows),
            pl.BlockSpec((TILE, 8), rows),
        ],
        out_shape=[
            shape((SEQ, WIDTH), BF),
            shape((SEQ, PACK), BF),
            shape((SEQ, HEAD_COLS), F32),
            shape((SEQ, HEAD_COLS), BF),
            shape((SEQ, 8), F32),
        ],
        scratch_shapes=[pltpu.VMEM((SEQ, HEAD_SIZE), BF), pltpu.VMEM((SEQ, HEAD_SIZE), BF)],
        compiler_params=pltpu.CompilerParams(
            dimension_semantics=("arbitrary",), vmem_limit_bytes=48 * 1024 * 1024
        ),
        cost_estimate=pl.CostEstimate(flops=3_000_000_000, bytes_accessed=12_000_000, transcendentals=3_000_000),
        name="attend",
    )(tokens, packed, gain, cosine, sine, seg_rows, seg_cols)


def attend_back_kernel(
    upstream, heads, attended, stats, all_heads, cosine, sine, all_cosine, all_sine, seg_rows, seg_cols,
    grads, grad_keys, grad_values,
):
    step = pl.program_id(0)

    @pl.when(step == 0)
    def _():
        grad_keys[...] = jnp.zeros_like(grad_keys)
        grad_values[...] = jnp.zeros_like(grad_values)

    for tile in range(TILES):

        @pl.when(step == tile)
        def _(tile=tile):
            count = (tile + 1) * TILE
            visible = visible_tile(tile, count, seg_rows, seg_cols)
            key_rows = all_heads[:count, HEAD_COLS:QK_COLS]
            value_rows = all_heads[:count, QK_COLS:QKV_COLS]
            parts = []
            sum_keys, sum_values = 0.0, 0.0
            for h in range(GROUP):
                columns = slice(h * HEAD_SIZE, (h + 1) * HEAD_SIZE)
                query, grad = heads[:, columns], upstream[:, columns]
                scores = contract(query, key_rows, ((1,), (1,))) * SCALE
                scores = jnp.where(visible, scores, LARGE_NEGATIVE)
                top, total = stats[:, 2 * h : 2 * h + 1], stats[:, 2 * h + 1 : 2 * h + 2]
                soft = jnp.where(visible, jnp.exp(scores - top), 0.0) / total
                delta = jnp.sum(grad.astype(F32) * attended[:, columns], axis=-1, keepdims=True)
                grad_probs = contract(grad, value_rows, ((1,), (1,)))
                grad_scores = (soft * (grad_probs - delta)).astype(BF)
                parts.append(jnp.dot(grad_scores, key_rows, preferred_element_type=F32) * SCALE)
                sum_keys = sum_keys + contract(grad_scores, query, ((0,), (0,)))
                sum_values = sum_values + contract(soft.astype(BF), grad, ((0,), (0,)))
            grad_keys[:count, :] += sum_keys * SCALE
            grad_values[:count, :] += sum_values
            turned = jnp.concatenate([*parts, jnp.zeros_like(parts[0])], axis=1)
            turned = turned * cosine[...] - swap_halves(turned) * sine[...]
            grads[tile * TILE : count, :HEAD_COLS] = turned[:, :HEAD_COLS].astype(BF)

    @pl.when(step == TILES - 1)
    def _():
        both = jnp.concatenate([grad_keys[...], grad_values[...]], axis=1)
        turned = both * all_cosine[...] - swap_halves(both) * all_sine[...]
        lane = lax.broadcasted_iota(jnp.int32, both.shape, 1)
        both = jnp.where(lane < HEAD_SIZE, turned, both)
        grads[:, HEAD_COLS:] = jnp.concatenate([both, jnp.zeros((SEQ, HEAD_SIZE), F32)], axis=1).astype(BF)


def attend_back_call(upstream, heads, attended, stats, cosine, sine, seg_rows, seg_cols):
    def rows(i):
        return (i, 0)

    def whole(i):
        return (0, 0)

    return pl.pallas_call(
        attend_back_kernel,
        grid=(TILES,),
        in_specs=[
            pl.BlockSpec((TILE, HEAD_COLS), rows),
            pl.BlockSpec((TILE, PACK), rows),
            pl.BlockSpec((TILE, HEAD_COLS), rows),
            pl.BlockSpec((TILE, 8), rows),
            pl.BlockSpec((SEQ, PACK), whole),
            pl.BlockSpec((TILE, QK_COLS), rows),
            pl.BlockSpec((TILE, QK_COLS), rows),
            pl.BlockSpec((SEQ, 2 * HEAD_SIZE), whole),
            pl.BlockSpec((SEQ, 2 * HEAD_SIZE), whole),
            pl.BlockSpec((TILE, 1), rows),
            pl.BlockSpec((1, SEQ), whole),
        ],
        out_specs=pl.BlockSpec((SEQ, PACK), whole),
        out_shape=jax.ShapeDtypeStruct((SEQ, PACK), BF),
        scratch_shapes=[pltpu.VMEM((SEQ, HEAD_SIZE), F32), pltpu.VMEM((SEQ, HEAD_SIZE), F32)],
        compiler_params=pltpu.CompilerParams(
            dimension_semantics=("arbitrary",), vmem_limit_bytes=48 * 1024 * 1024
        ),
        cost_estimate=pl.CostEstimate(flops=4_000_000_000, bytes_accessed=8_000_000, transcendentals=3_000_000),
        name="attend_back",
    )(upstream, heads, attended, stats, heads, cosine, sine, cosine, sine, seg_rows, seg_cols)


def ring_of_four(block, axis):
    half = block.shape[0] // 2
    ahead = [(i, (i + 1) % 4) for i in range(4)]
    back = [(i, (i + 3) % 4) for i in range(4)]
    before = lax.ppermute(block, axis, ahead)
    after = lax.ppermute(block, axis, back)
    far_low = lax.ppermute(before[:half], axis, ahead)
    far_high = lax.ppermute(after[half:], axis, back)
    return [block, after, jnp.concatenate([far_low, far_high]), before]


def in_order(blocks, start):
    count = len(blocks)
    twice = jnp.stack([*blocks, *blocks])
    return lax.dynamic_slice_in_dim(twice, lax.rem(count - start, count), count, axis=0)


def body(tokens, seg_ids, routes, gain_attn, w_qkv, w_out, gain_moe, w_router, w_gate_up, w_down, cotangent):
    e = lax.axis_index(EXP)
    c = lax.axis_index("c")
    y = lax.axis_index("y")

    mine_matrix, other_matrix = parity_matrix(c), parity_matrix(1 - c)
    flat_gu = w_gate_up.reshape(EXP_DEV * 96, 2 * FFE)
    gu_other = dot(flat_gu, other_matrix).astype(BF).reshape(EXP_DEV, 96, FFE)
    gu_recv = core_swap(gu_other)
    gu_mine = dot(flat_gu, mine_matrix).astype(BF).reshape(EXP_DEV, 96, FFE)
    mixed = jnp.concatenate(
        [
            jnp.where(c == 0, gu_mine, gu_recv),
            jnp.where(c == 0, gu_recv, gu_mine),
            *(w_down[:, :, p * FFE : (p + 1) * FFE] for p in range(WIDTH // FFE)),
        ],
        axis=1,
    )
    weights = lax.all_gather(mixed, YZ, axis=0, tiled=False)

    def own_columns(start, width):
        return lax.dynamic_slice_in_dim(w_qkv, start + e * width, width, axis=1)

    packet = jnp.concatenate(
        [
            own_columns(0, HEAD_COLS),
            own_columns(WIDTH, HEAD_SIZE),
            own_columns(WIDTH + KEY_VALUE_HEADS * HEAD_SIZE, HEAD_SIZE),
            w_router,
            gain_attn[:, None],
            gain_moe[:, None],
            jnp.zeros((w_qkv.shape[0], PACK - QKV_COLS - EXPERTS - 2), BF),
        ],
        axis=1,
    )
    packed = to_all(packet, FSDP, N_FSDP).reshape(WIDTH, PACK)
    router = packed[:, QKV_COLS : QKV_COLS + EXPERTS]
    gain_one = packed[:, QKV_COLS + EXPERTS].astype(F32)
    gain_two = packed[:, QKV_COLS + EXPERTS + 1].astype(F32)
    tok_all = to_all(tokens[0], EXP, N_EXP).reshape(SEQ, WIDTH)

    row_of_z = [w_out, lax.ppermute(w_out, "zh", SWAP)]
    rings = [in_order(ring_of_four(block, "y"), y) for block in row_of_z]
    near, far = rings
    zh = lax.axis_index("zh")
    out_mine = jnp.stack([jnp.where(zh == 0, near, far), jnp.where(zh == 0, far, near)], axis=1)
    out_other = core_swap(out_mine)
    full_out = jnp.stack(
        [jnp.where(c == 0, out_mine, out_other), jnp.where(c == 0, out_other, out_mine)], axis=2
    ).reshape(N_EXP, HEAD_COLS, WIDTH)

    cot_packet = jnp.concatenate(
        [cotangent[0], routes[0].astype(BF), jnp.zeros((TOK, SIDE - routes.shape[-1]), BF)], axis=1
    )
    cot_packet, tok_all = lax.optimization_barrier((cot_packet, tok_all))
    cot_all = to_all(cot_packet, EXP, N_EXP).reshape(SEQ, WIDTH + SIDE)
    cot_other = core_swap(cot_all)

    lanes = jnp.arange(QK_COLS, dtype=jnp.int32)
    inv_freq = THETA ** (-2.0 * (lanes % (HEAD_SIZE // 2)).astype(F32) / HEAD_SIZE)
    angles = jnp.arange(SEQ, dtype=jnp.int32).astype(F32)[:, None] * inv_freq[None, :]
    cosine = jnp.cos(angles)
    sine = jnp.sin(angles) * jnp.where(lanes % HEAD_SIZE < HEAD_SIZE // 2, -1.0, 1.0)
    seg_rows, seg_cols = seg_ids[0][:, None], seg_ids
    normed_one, heads, attended, attended_low, stats = attend_call(
        tok_all, packed, gain_one[None], cosine, sine, seg_rows, seg_cols
    )
    attended_all = to_all(attended_low, EXP, N_EXP)

    resid = tok_all.astype(F32) + ein("etk,ekn->tn", attended_all, full_out)
    inv_two = rms_inverse(resid)
    normed_two = (resid * inv_two * gain_two).astype(BF)

    def own_first(value):
        return lax.dynamic_slice_in_dim(
            jnp.concatenate([value, value], axis=1), e * EXP_DEV, EXPERTS, axis=1
        )

    router_turned = jnp.pad(own_first(router), ((0, 0), (0, SIDE - EXPERTS)))
    routes_pair = jnp.concatenate(
        [side[:, WIDTH : WIDTH + routes.shape[-1]] for side in (cot_all, cot_other)]
    ).astype(jnp.int32)
    routes_turned = (routes_pair + (EXPERTS - e * EXP_DEV)) % EXPERTS
    chosen = jnp.any(routes_turned[:, :, None] == jnp.arange(SIDE, dtype=jnp.int32), axis=1).astype(BF)
    out_own, out_par, back_own, back_par, grad_weights = experts_call(
        normed_two, core_swap(normed_two), cot_all, cot_other, chosen, router_turned, weights
    )
    shard_weights = lax.psum_scatter(grad_weights, YZ, scatter_dimension=0, tiled=False)

    def both_cores(own, par):
        return (own.astype(F32) + core_swap(par).astype(F32)).astype(BF).reshape(N_EXP, TOK, -1)

    routed_back = exchange(both_cores(back_own, back_par), EXP)
    routed_total = jnp.sum(routed_back[..., :WIDTH].astype(F32), axis=0)
    sides = routed_back[..., WIDTH : WIDTH + 4 * EXP_DEV].astype(F32).reshape(N_EXP, TOK, 4, EXP_DEV)
    grad_gates = jnp.transpose(jnp.sum(sides, axis=2), (1, 0, 2)).reshape(TOK, EXPERTS)

    def own_rows(value):
        return lax.dynamic_slice_in_dim(value, e * TOK, TOK, axis=0)

    resid_own, inv_two_own, normed_two_own = own_rows(resid), own_rows(inv_two), own_rows(normed_two)
    logits = dot(normed_two_own, router)
    picked = jnp.any(routes[0][:, :, None] == jnp.arange(EXPERTS, dtype=jnp.int32), axis=1)
    masked = jnp.where(picked, logits, LARGE_NEGATIVE)
    exps = jnp.where(picked, jnp.exp(masked - jnp.max(masked, axis=-1, keepdims=True)), 0.0)
    gates = exps / jnp.sum(exps, axis=-1, keepdims=True)
    upstream = cotangent[0].astype(F32)
    grad_logits = (
        gates * (grad_gates - jnp.sum(gates * grad_gates, axis=-1, keepdims=True))
    ).astype(BF)
    router_part = dot(normed_two_own.T, grad_logits)
    grad_normed_two = dot(grad_logits, router.T) + routed_total
    grad_rows, gain_two_part = rms_backward(resid_own, inv_two_own, gain_two, grad_normed_two)
    grad_resid = upstream + grad_rows
    grad_branch = grad_resid.astype(BF)
    grad_attended_own = ein("tn,ekn->etk", grad_branch, full_out).astype(BF)
    branch_blocks = jnp.transpose(grad_branch.reshape(TOK, N_EXP, HEAD_COLS), (1, 0, 2))
    back = exchange(jnp.concatenate([grad_attended_own, branch_blocks], axis=-1), EXP)
    back = back.reshape(SEQ, 2 * HEAD_COLS)
    grad_attended, branch_cols = back[:, :HEAD_COLS], back[:, HEAD_COLS:]

    grad_projected = attend_back_call(
        grad_attended, heads, attended, stats, cosine, sine, seg_rows, seg_cols
    )
    normed_grad_part = contract(grad_projected, packed, ((1,), (1,))).astype(BF)

    out_part, out_back_in = lax.optimization_barrier((both_cores(out_own, out_par), back))
    out_back = exchange(out_part, EXP)
    output = (resid_own + jnp.sum(out_back.astype(F32), axis=0)).astype(BF)

    normed_back = exchange(normed_grad_part.reshape(N_EXP, TOK, WIDTH), EXP)

    def reduce_over_all(parts):
        sent = parts.astype(BF).reshape(N_FSDP, WIDTH // N_FSDP, -1)
        summed = jnp.sum(exchange(sent, FSDP).astype(F32), axis=0).astype(BF)
        return to_all(summed, EXP, N_EXP).astype(F32)

    out_grad_part = ein("etk,tn->ekn", attended_all, branch_cols).reshape(WIDTH, HEAD_COLS)
    first_totals = reduce_over_all(
        jnp.concatenate(
            [
                out_grad_part,
                router_part,
                gain_two_part[:, None],
                jnp.zeros((WIDTH, 256 - HEAD_COLS - EXPERTS - 1), F32),
            ],
            axis=1,
        )
    )
    total_out = jnp.transpose(first_totals[..., :HEAD_COLS], (1, 0, 2)).reshape(-1, WIDTH)
    shared = jnp.sum(first_totals[..., HEAD_COLS : HEAD_COLS + EXPERTS + 1], axis=0)

    grad_normed_one = jnp.sum(normed_back.astype(F32), axis=0)
    own_tokens = tokens[0].astype(F32)
    grad_in, gain_one_part = rms_backward(own_tokens, rms_inverse(own_tokens), gain_one, grad_normed_one)
    grad_tokens = (grad_resid + grad_in).astype(BF)
    qkv_grad_part = contract(normed_one, grad_projected, ((0,), (0,)))[:, :QKV_COLS]
    last_totals = reduce_over_all(
        jnp.concatenate(
            [qkv_grad_part, gain_one_part[:, None], jnp.zeros((WIDTH, PACK - QKV_COLS - 1), F32)], axis=1
        )
    )

    def head_columns(start, width):
        return jnp.transpose(last_totals[..., start : start + width], (1, 0, 2)).reshape(-1, N_EXP * width)

    total_qkv = jnp.concatenate(
        [
            head_columns(0, HEAD_COLS),
            head_columns(HEAD_COLS, HEAD_SIZE),
            head_columns(HEAD_COLS + HEAD_SIZE, HEAD_SIZE),
        ],
        axis=1,
    )
    total_gain_one = jnp.sum(last_totals[..., QKV_COLS], axis=0)

    first_rows, second_rows = shard_weights[:, :96], shard_weights[:, 96:GU_ROWS]
    keep = jnp.where(c == 0, first_rows, second_rows).reshape(-1, FFE)
    arrived = core_swap(jnp.where(c == 0, second_rows, first_rows)).reshape(-1, FFE)
    total_gu = (dot(keep, mine_matrix.T) + dot(arrived, other_matrix.T)).reshape(EXP_DEV, 96, 2 * FFE)
    total_down = jnp.concatenate(
        [shard_weights[:, GU_ROWS + 32 * p : GU_ROWS + 32 * (p + 1)] for p in range(WIDTH // FFE)], axis=2
    ).astype(F32)

    return (
        output[None],
        grad_tokens[None],
        total_gain_one,
        total_qkv,
        total_out,
        shared[:, EXPERTS],
        shared[:, :EXPERTS],
        total_gu,
        total_down,
    )


def solution(mesh):
    fine = Mesh(mesh.devices.reshape(4, 2, 4, 2, 2), ("x", "zl", "y", "zh", "c"))
    rows = P(FSDP, EXP, None)
    weight = P(FSDP, None)
    expert_weight = P(EXP, FSDP, None)
    in_specs = (
        rows,
        P(FSDP, None),
        rows,
        P(FSDP),
        weight,
        weight,
        P(FSDP),
        weight,
        expert_weight,
        expert_weight,
        rows,
    )
    out_specs = (rows, rows, P(FSDP), weight, weight, P(FSDP), weight, expert_weight, expert_weight)
    return jax.shard_map(body, mesh=fine, in_specs=in_specs, out_specs=out_specs, check_vma=False)
```

```python
import math

import jax
import jax.numpy as jnp
from jax import lax
from jax.experimental import pallas as pl
from jax.experimental.pallas import tpu as pltpu
from jax.sharding import Mesh, PartitionSpec as P

QUERY_HEADS = 24
KEY_VALUE_HEADS = 8
HEAD_SIZE = 64
GROUP = QUERY_HEADS // KEY_VALUE_HEADS
FFE = 512
TOP = 8
EXP_DEV = 5
EXPERTS = 40
WIDTH = 1536
TOK = 128
SEQ = 1024
CAP = 48
BLOCKS = 16
N_EXP = 8
N_FSDP = 16
N_YZ = 8
HALF_FFE = FFE // 2
HEAD_COLS = GROUP * HEAD_SIZE
QKV_COLS = HEAD_COLS + 2 * HEAD_SIZE
PACK = 384
DENSE_COLS = 640
SIDE = 128
SLOTS = EXP_DEV * CAP
ROWS = BLOCKS * CAP
PARTS = 4
STEPS = BLOCKS // PARTS
GU_ROWS = WIDTH // N_YZ
MIX_ROWS = GU_ROWS + 32 * WIDTH // FFE
TILE = 256
TILES = SEQ // TILE
QK_COLS = HEAD_COLS + HEAD_SIZE
SCALE = 1.0 / math.sqrt(HEAD_SIZE)

EPS = 1e-06
THETA = 10000.0
LARGE_NEGATIVE = -1e30

EXP = ("x", "zl")
FSDP = ("y", "zh", "c")
YZ = ("y", "zh")
SWAP = ((0, 1), (1, 0))
BF = jnp.bfloat16
F32 = jnp.float32


def dot(a, b):
    return jnp.dot(a, b, preferred_element_type=F32)


def ein(spec, *args):
    return jnp.einsum(spec, *args, preferred_element_type=F32)


def core_swap(value):
    return lax.ppermute(value, "c", SWAP)


def to_all(value, axes, count):
    spread = jnp.broadcast_to(value[None], (count, *value.shape))
    return lax.all_to_all(spread, axes, 0, 0, tiled=True)


def exchange(value, axes):
    return lax.all_to_all(value, axes, 0, 0, tiled=True)


def rms_inverse(features):
    return lax.rsqrt(jnp.mean(features * features, axis=-1, keepdims=True) + EPS)


def rms_backward(features, inverse, gain_vec, grad_normed):
    scaled = gain_vec * grad_normed
    grad_rows = inverse * scaled - features * inverse**3 * jnp.mean(
        features * scaled, axis=-1, keepdims=True
    )
    grad_gain = jnp.sum(features * inverse * grad_normed, axis=0)
    return grad_rows, grad_gain


def parity_matrix(parity):
    rows = jnp.arange(2 * FFE, dtype=jnp.int32)[:, None]
    cols = jnp.arange(FFE, dtype=jnp.int32)[None, :]
    part, rest = cols // HALF_FFE, cols % HALF_FFE
    source = part * FFE + (2 * (rest // 32) + parity) * 32 + rest % 32
    return (rows == source).astype(BF)


def contract(a, b, dims):
    return lax.dot_general(a, b, (dims, ((), ())), preferred_element_type=F32)


def picked_lanes(routes):
    lane = lax.broadcasted_iota(jnp.int32, routes.shape, 1).astype(F32)
    numbers = routes.astype(F32)
    found = lane < 0
    for r in range(TOP):
        found = found | (lane == numbers[:, r : r + 1])
    return found.astype(F32).astype(BF)


def token_square():
    shape = (TOK, TOK)
    return lax.broadcasted_iota(jnp.int32, shape, 0), lax.broadcasted_iota(jnp.int32, shape, 1)


def slots_by_token(picks):
    token, other = token_square()
    ranks = contract(picks, (token < other).astype(BF), ((0,), (0,)))
    named = contract(picks, (token == other).astype(BF), ((0,), (0,)))
    ranks = jnp.where(named > 0, ranks, -1.0).astype(jnp.int32)
    slot = lax.broadcasted_iota(jnp.int32, (CAP, TOK), 0)
    hits = [(slot == ranks[j : j + 1, :]).astype(F32) for j in range(EXP_DEV)]
    return jnp.concatenate(hits, axis=0).astype(BF)


def tokens_by_slot(picks):
    token, other = token_square()
    ranks = jnp.dot((token > other).astype(BF), picks, preferred_element_type=F32).astype(jnp.int32)
    lane = lax.broadcasted_iota(jnp.int32, (TOK, SLOTS), 1)
    hot = jnp.zeros((TOK, SLOTS), F32)
    for j in range(EXP_DEV):
        hit = (picks[:, j : j + 1] > 0) & (lane == ranks[:, j : j + 1] + j * CAP)
        hot = jnp.where(hit, 1.0, hot)
    return hot.astype(BF)


def thirds(value):
    high = value.astype(BF)
    rest = value - high.astype(F32)
    middle = rest.astype(BF)
    return high, middle, (rest - middle.astype(F32)).astype(BF)


def block_rows(ref, start):
    return jnp.concatenate([ref[j, pl.ds(start, CAP), :] for j in range(EXP_DEV)], axis=0)


def expert_weights(ref):
    w_in = ref[:, 0, :GU_ROWS, :].reshape(WIDTH, FFE)
    pieces = [
        ref[:, 0, GU_ROWS + 32 * p : GU_ROWS + 32 * (p + 1), :].reshape(HALF_FFE, FFE)
        for p in range(WIDTH // FFE)
    ]
    return w_in, jnp.concatenate(pieces, axis=1)


def block_start(step, part):
    return pl.multiple_of((step * PARTS + part) * CAP, 16)


def forward_kernel(
    n_own, n_par, routes, router, weights,
    out_own, out_par, x_kept, pre_kept,
    x_slots, gate_slots,
):
    step = pl.program_id(0)

    @pl.when(step < STEPS)
    def dispatch():
        def place(n_ref, part):
            here = slice(part * TOK, (part + 1) * TOK)
            rows = n_ref[here, :]
            picks = picked_lanes(routes[here, :])
            logits = jnp.dot(rows, router[...], preferred_element_type=F32)
            keep = picks > 0
            masked = jnp.where(keep, logits, LARGE_NEGATIVE)
            exps = jnp.where(keep, jnp.exp(masked - jnp.max(masked, axis=-1, keepdims=True)), 0.0)
            gates = exps / jnp.sum(exps, axis=-1, keepdims=True)
            one_hot = slots_by_token(picks)
            spread = sum(jnp.dot(one_hot, third, preferred_element_type=F32) for third in thirds(gates))
            lane = lax.broadcasted_iota(jnp.int32, (CAP, TOK), 1)
            x = jnp.dot(one_hot, rows, preferred_element_type=F32).astype(BF)
            start = block_start(step, part)
            for j in range(EXP_DEV):
                piece = slice(j * CAP, (j + 1) * CAP)
                x_slots[j, pl.ds(start, CAP), :] = x[piece]
                gate_slots[j, pl.ds(start, CAP), :] = jnp.sum(
                    jnp.where(lane == j, spread[piece], 0.0), axis=-1, keepdims=True
                )

        @pl.when(step < STEPS // 2)
        def _():
            for part in range(PARTS):
                place(n_own, part)

        @pl.when(step >= STEPS // 2)
        def _():
            for part in range(PARTS):
                place(n_par, part)

    @pl.when((step >= STEPS) & (step < STEPS + EXP_DEV))
    def experts():
        j = step - STEPS
        w_in, w_back = expert_weights(weights)

        x = x_slots[j]
        gates = gate_slots[j]
        pre = jnp.dot(x, w_in, preferred_element_type=F32)
        x_kept[0] = x
        pre_kept[0, :, :FFE] = pre.astype(BF)
        high, middle, low = thirds(gates)
        lane = lax.broadcasted_iota(jnp.int32, (ROWS, SIDE), 1)
        pre_kept[0, :, FFE:] = jnp.where(
            lane == 0, high.astype(F32), jnp.where(lane == 1, middle.astype(F32), low.astype(F32))
        ).astype(BF)
        gate, up = pre[:, :HALF_FFE], pre[:, HALF_FFE:]
        hidden = (gate * jax.nn.sigmoid(gate) * up).astype(BF).astype(F32)
        gated = (hidden * gates).astype(BF)
        x_slots[j] = jnp.dot(gated, w_back, preferred_element_type=F32).astype(BF)

    @pl.when(step >= STEPS + EXP_DEV)
    def combine():
        block = step - STEPS - EXP_DEV

        def write(out_ref, part):
            here = slice(part * TOK, (part + 1) * TOK)
            hot = tokens_by_slot(picked_lanes(routes[here, :]))
            rows = block_rows(x_slots, block_start(block, part))
            out_ref[here, :] = jnp.dot(hot, rows, preferred_element_type=F32).astype(BF)

        @pl.when(block < STEPS // 2)
        def _():
            for part in range(PARTS):
                write(out_own, part)

        @pl.when(block >= STEPS // 2)
        def _():
            for part in range(PARTS):
                write(out_par, part)


def backward_kernel(
    place_ref, g_own, g_par, routes, x_kept, pre_kept, weights,
    back_own, back_par, grads,
    g_slots, side_slots,
):
    step = pl.program_id(0)

    @pl.when(step < STEPS)
    def dispatch():
        def place(g_ref, part):
            here = slice(part * TOK, (part + 1) * TOK)
            one_hot = slots_by_token(picked_lanes(routes[here, :]))
            g = jnp.dot(one_hot, g_ref[here, :], preferred_element_type=F32).astype(BF)
            start = block_start(step, part)
            for j in range(EXP_DEV):
                g_slots[j, pl.ds(start, CAP), :] = g[j * CAP : (j + 1) * CAP]

        @pl.when(step < STEPS // 2)
        def _():
            for part in range(PARTS):
                place(g_own, part)

        @pl.when(step >= STEPS // 2)
        def _():
            for part in range(PARTS):
                place(g_par, part)

    @pl.when((step >= STEPS) & (step < STEPS + EXP_DEV))
    def experts():
        j = step - STEPS
        w_in, w_back = expert_weights(weights)
        g = g_slots[j]
        pre = pre_kept[0, :, :FFE].astype(F32)
        kept = pre_kept[0, :, FFE:].astype(F32)
        gates = kept[:, 0:1] + kept[:, 1:2] + kept[:, 2:3]
        plain = contract(g, w_back, ((1,), (1,)))
        gate, up = pre[:, :HALF_FFE], pre[:, HALF_FFE:]
        sigmoid = jax.nn.sigmoid(gate)
        silu = gate * sigmoid
        hidden = (silu * up).astype(BF).astype(F32)
        gated = (hidden * gates).astype(BF)
        slope = jnp.sum(hidden * plain, axis=-1, keepdims=True)
        high = slope.astype(BF).astype(F32)
        lane = lax.broadcasted_iota(jnp.int32, (ROWS, SIDE), 1)
        row = lax.broadcasted_iota(jnp.int32, (ROWS, SIDE), 0)
        number = place_ref[0] * EXP_DEV + j
        first_lane = jnp.where(row < ROWS // 2, number, number + EXPERTS)
        side_slots[j] = jnp.where(
            lane == first_lane, high, jnp.where(lane == number + 2 * EXPERTS, slope - high, 0.0)
        ).astype(BF)
        grad_hidden = plain * gates
        grad_pre = jnp.concatenate(
            [grad_hidden * up * sigmoid * (1.0 + gate * (1.0 - sigmoid)), grad_hidden * silu], axis=-1
        ).astype(BF)
        grad_down = contract(gated, g, ((0,), (0,))).astype(BF)
        grad_gate_up = contract(x_kept[0], grad_pre, ((0,), (0,))).astype(BF)
        g_slots[j] = contract(grad_pre, w_in, ((1,), (1,))).astype(BF)
        grads[:, 0, :GU_ROWS, :] = grad_gate_up.reshape(N_YZ, GU_ROWS, FFE)
        for p in range(WIDTH // FFE):
            grads[:, 0, GU_ROWS + 32 * p : GU_ROWS + 32 * (p + 1), :] = grad_down[
                :, p * FFE : (p + 1) * FFE
            ].reshape(N_YZ, 32, FFE)

    @pl.when(step >= STEPS + EXP_DEV)
    def combine():
        block = step - STEPS - EXP_DEV

        def write(back_ref, part):
            here = slice(part * TOK, (part + 1) * TOK)
            hot = tokens_by_slot(picked_lanes(routes[here, :]))
            start = block_start(block, part)
            back_ref[here, :WIDTH] = jnp.dot(
                hot, block_rows(g_slots, start), preferred_element_type=F32
            ).astype(BF)
            back_ref[here, WIDTH:] = jnp.dot(
                hot, block_rows(side_slots, start), preferred_element_type=F32
            ).astype(BF)

        @pl.when(block < STEPS // 2)
        def _():
            for part in range(PARTS):
                write(back_own, part)

        @pl.when(block >= STEPS // 2)
        def _():
            for part in range(PARTS):
                write(back_par, part)


HALF_STEPS = STEPS // 2
LAST = STEPS + EXP_DEV
SPAN = PARTS * TOK


def first(i):
    return (jnp.clip(i, 0, HALF_STEPS - 1), 0)


def second(i):
    return (jnp.clip(i - HALF_STEPS, 0, HALF_STEPS - 1), 0)


def any_block(i):
    return (jnp.where(i < LAST, jnp.clip(i, 0, STEPS - 1), i - LAST), 0)


def expert(i):
    return (jnp.clip(i - STEPS, 0, EXP_DEV - 1), 0, 0)


def expert_split(i):
    return (0, jnp.clip(i - STEPS, 0, EXP_DEV - 1), 0, 0)


def out_first(i):
    return (jnp.clip(i - LAST, 0, HALF_STEPS - 1), 0)


def out_second(i):
    return (jnp.clip(i - LAST - HALF_STEPS, 0, HALF_STEPS - 1), 0)


KEPT = [
    pl.BlockSpec((1, ROWS, WIDTH), expert),
    pl.BlockSpec((1, ROWS, FFE + SIDE), expert),
]
WEIGHTS = pl.BlockSpec((N_YZ, 1, MIX_ROWS, FFE), expert_split)


def experts_forward(n_own, n_par, routes, router, weights):
    shape = jax.ShapeDtypeStruct
    return pl.pallas_call(
        forward_kernel,
        grid=(2 * STEPS + EXP_DEV,),
        in_specs=[
            pl.BlockSpec((SPAN, WIDTH), first),
            pl.BlockSpec((SPAN, WIDTH), second),
            pl.BlockSpec((SPAN, SIDE), any_block),
            pl.BlockSpec((WIDTH, SIDE), lambda i: (0, 0)),
            WEIGHTS,
        ],
        out_specs=[pl.BlockSpec((SPAN, WIDTH), out_first), pl.BlockSpec((SPAN, WIDTH), out_second), *KEPT],
        out_shape=[
            shape((SEQ, WIDTH), BF),
            shape((SEQ, WIDTH), BF),
            shape((EXP_DEV, ROWS, WIDTH), BF),
            shape((EXP_DEV, ROWS, FFE + SIDE), BF),
        ],
        scratch_shapes=[pltpu.VMEM((EXP_DEV, ROWS, WIDTH), BF), pltpu.VMEM((EXP_DEV, ROWS, 1), F32)],
        compiler_params=pltpu.CompilerParams(
            dimension_semantics=("arbitrary",), vmem_limit_bytes=56 * 1024 * 1024
        ),
        cost_estimate=pl.CostEstimate(flops=40_000_000_000, bytes_accessed=40_000_000, transcendentals=1_000_000),
        name="experts_forward",
    )(n_own, n_par, routes, router, weights)


def experts_backward(place, g_own, g_par, routes, kept, weights):
    shape = jax.ShapeDtypeStruct
    return pl.pallas_call(
        backward_kernel,
        grid=(2 * STEPS + EXP_DEV,),
        in_specs=[
            pl.BlockSpec(memory_space=pltpu.SMEM),
            pl.BlockSpec((SPAN, WIDTH), first),
            pl.BlockSpec((SPAN, WIDTH), second),
            pl.BlockSpec((SPAN, SIDE), any_block),
            *KEPT,
            WEIGHTS,
        ],
        out_specs=[
            pl.BlockSpec((SPAN, WIDTH + SIDE), out_first),
            pl.BlockSpec((SPAN, WIDTH + SIDE), out_second),
            WEIGHTS,
        ],
        out_shape=[
            shape((SEQ, WIDTH + SIDE), BF),
            shape((SEQ, WIDTH + SIDE), BF),
            shape((N_YZ, EXP_DEV, MIX_ROWS, FFE), BF),
        ],
        scratch_shapes=[
            pltpu.VMEM((EXP_DEV, ROWS, WIDTH), BF),
            pltpu.VMEM((EXP_DEV, ROWS, SIDE), BF),
        ],
        compiler_params=pltpu.CompilerParams(
            dimension_semantics=("arbitrary",), vmem_limit_bytes=60 * 1024 * 1024
        ),
        cost_estimate=pl.CostEstimate(flops=50_000_000_000, bytes_accessed=60_000_000, transcendentals=1_000_000),
        name="experts_backward",
    )(place.reshape(1), g_own, g_par, routes, *kept, weights)


def swap_halves(value):
    width = value.shape[-1]
    lane = lax.broadcasted_iota(jnp.int32, value.shape, 1)
    return jnp.where(
        lane % HEAD_SIZE < HEAD_SIZE // 2,
        pltpu.roll(value, width - HEAD_SIZE // 2, 1),
        pltpu.roll(value, HEAD_SIZE // 2, 1),
    )


def visible_tile(tile, count, seg_rows, seg_cols):
    row = lax.broadcasted_iota(jnp.int32, (TILE, count), 0) + tile * TILE
    col = lax.broadcasted_iota(jnp.int32, (TILE, count), 1)
    return (col <= row) & (seg_rows[...] == seg_cols[:, :count])


def attend_kernel(
    place_ref, block_0, block_1, block_2, block_3, packed, gain, cosine, sine, seg_rows, seg_cols,
    tokens, normed, heads, attended, attended_low, stats, keys, values,
):
    step = pl.program_id(0)
    distance = lax.rem(step - place_ref[0] + TILES, TILES)
    for k, block in enumerate((block_0, block_1, block_2, block_3)):

        @pl.when(distance == k)
        def _(block=block):
            tokens[...] = block[...]

    features = tokens[:, :WIDTH].astype(F32)
    inverse = lax.rsqrt(jnp.mean(features * features, axis=-1, keepdims=True) + EPS)
    rows = (features * inverse * gain[...]).astype(BF)
    normed[...] = rows
    projected = jnp.dot(rows, packed[...], preferred_element_type=F32)
    turned = projected[:, :QK_COLS]
    turned = (turned * cosine[...] + swap_halves(turned) * sine[...]).astype(BF)
    value_rows = projected[:, QK_COLS:QKV_COLS].astype(BF)
    heads[:, :QK_COLS] = turned
    heads[:, QK_COLS:] = jnp.concatenate([value_rows, jnp.zeros_like(value_rows)], axis=1)
    here = pl.ds(pl.multiple_of(step * TILE, TILE), TILE)
    keys[here, :] = turned[:, HEAD_COLS:]
    values[here, :] = value_rows

    for tile in range(TILES):

        @pl.when(step == tile)
        def _(tile=tile):
            count = (tile + 1) * TILE
            visible = visible_tile(tile, count, seg_rows, seg_cols)
            key_rows, value_all = keys[:count, :], values[:count, :]
            parts = []
            for h in range(GROUP):
                query = turned[:, h * HEAD_SIZE : (h + 1) * HEAD_SIZE]
                scores = contract(query, key_rows, ((1,), (1,))) * SCALE
                scores = jnp.where(visible, scores, LARGE_NEGATIVE)
                top = jnp.max(scores, axis=-1, keepdims=True)
                weights = jnp.where(visible, jnp.exp(scores - top), 0.0)
                total = jnp.sum(weights, axis=-1, keepdims=True)
                soft = (weights / total).astype(BF)
                parts.append(jnp.dot(soft, value_all, preferred_element_type=F32))
                stats[:, 2 * h : 2 * h + 1] = top
                stats[:, 2 * h + 1 : 2 * h + 2] = total
            result = jnp.concatenate(parts, axis=1)
            attended[...] = result
            attended_low[...] = result.astype(BF)


def attend_call(place, blocks, packed, gain, cosine, sine, seg_rows, seg_cols):
    def rows(i):
        return (i, 0)

    def whole(i):
        return (0, 0)

    shape = jax.ShapeDtypeStruct
    return pl.pallas_call(
        attend_kernel,
        grid=(TILES,),
        in_specs=[
            pl.BlockSpec(memory_space=pltpu.SMEM),
            *[pl.BlockSpec((TILE, WIDTH + SIDE), whole)] * TILES,
            pl.BlockSpec((WIDTH, PACK), whole),
            pl.BlockSpec((1, WIDTH), whole),
            pl.BlockSpec((TILE, QK_COLS), rows),
            pl.BlockSpec((TILE, QK_COLS), rows),
            pl.BlockSpec((TILE, 1), rows),
            pl.BlockSpec((1, SEQ), whole),
        ],
        out_specs=[
            pl.BlockSpec((TILE, WIDTH + SIDE), rows),
            pl.BlockSpec((TILE, WIDTH), rows),
            pl.BlockSpec((TILE, PACK), rows),
            pl.BlockSpec((TILE, HEAD_COLS), rows),
            pl.BlockSpec((TILE, HEAD_COLS), rows),
            pl.BlockSpec((TILE, 8), rows),
        ],
        out_shape=[
            shape((SEQ, WIDTH + SIDE), BF),
            shape((SEQ, WIDTH), BF),
            shape((SEQ, PACK), BF),
            shape((SEQ, HEAD_COLS), F32),
            shape((SEQ, HEAD_COLS), BF),
            shape((SEQ, 8), F32),
        ],
        scratch_shapes=[pltpu.VMEM((SEQ, HEAD_SIZE), BF), pltpu.VMEM((SEQ, HEAD_SIZE), BF)],
        compiler_params=pltpu.CompilerParams(
            dimension_semantics=("arbitrary",), vmem_limit_bytes=48 * 1024 * 1024
        ),
        cost_estimate=pl.CostEstimate(flops=13_000_000_000, bytes_accessed=12_000_000, transcendentals=3_000_000),
        name="attend",
    )(place.reshape(1), *blocks, packed, gain, cosine, sine, seg_rows, seg_cols)


def attend_back_kernel(
    upstream, heads, attended, stats, all_heads, cosine, sine, all_cosine, all_sine, seg_rows, seg_cols,
    grads, grad_keys, grad_values,
):
    step = pl.program_id(0)

    @pl.when(step == 0)
    def _():
        grad_keys[...] = jnp.zeros_like(grad_keys)
        grad_values[...] = jnp.zeros_like(grad_values)

    for tile in range(TILES):

        @pl.when(step == tile)
        def _(tile=tile):
            count = (tile + 1) * TILE
            visible = visible_tile(tile, count, seg_rows, seg_cols)
            key_rows = all_heads[:count, HEAD_COLS:QK_COLS]
            value_rows = all_heads[:count, QK_COLS:QKV_COLS]
            parts = []
            sum_keys, sum_values = 0.0, 0.0
            for h in range(GROUP):
                columns = slice(h * HEAD_SIZE, (h + 1) * HEAD_SIZE)
                query, grad = heads[:, columns], upstream[:, columns]
                scores = contract(query, key_rows, ((1,), (1,))) * SCALE
                scores = jnp.where(visible, scores, LARGE_NEGATIVE)
                top, total = stats[:, 2 * h : 2 * h + 1], stats[:, 2 * h + 1 : 2 * h + 2]
                soft = jnp.where(visible, jnp.exp(scores - top), 0.0) / total
                delta = jnp.sum(grad.astype(F32) * attended[:, columns], axis=-1, keepdims=True)
                grad_probs = contract(grad, value_rows, ((1,), (1,)))
                grad_scores = (soft * (grad_probs - delta)).astype(BF)
                parts.append(jnp.dot(grad_scores, key_rows, preferred_element_type=F32) * SCALE)
                sum_keys = sum_keys + contract(grad_scores, query, ((0,), (0,)))
                sum_values = sum_values + contract(soft.astype(BF), grad, ((0,), (0,)))
            grad_keys[:count, :] += sum_keys * SCALE
            grad_values[:count, :] += sum_values
            turned = jnp.concatenate([*parts, jnp.zeros_like(parts[0])], axis=1)
            turned = turned * cosine[...] - swap_halves(turned) * sine[...]
            grads[tile * TILE : count, :HEAD_COLS] = turned[:, :HEAD_COLS].astype(BF)

    @pl.when(step == TILES - 1)
    def _():
        both = jnp.concatenate([grad_keys[...], grad_values[...]], axis=1)
        turned = both * all_cosine[...] - swap_halves(both) * all_sine[...]
        lane = lax.broadcasted_iota(jnp.int32, both.shape, 1)
        both = jnp.where(lane < HEAD_SIZE, turned, both)
        grads[:, HEAD_COLS:] = jnp.concatenate([both, jnp.zeros((SEQ, HEAD_SIZE), F32)], axis=1).astype(BF)


def attend_back_call(upstream, heads, attended, stats, cosine, sine, seg_rows, seg_cols):
    def rows(i):
        return (i, 0)

    def whole(i):
        return (0, 0)

    return pl.pallas_call(
        attend_back_kernel,
        grid=(TILES,),
        in_specs=[
            pl.BlockSpec((TILE, 2 * HEAD_COLS), rows),
            pl.BlockSpec((TILE, PACK), rows),
            pl.BlockSpec((TILE, HEAD_COLS), rows),
            pl.BlockSpec((TILE, 8), rows),
            pl.BlockSpec((SEQ, PACK), whole),
            pl.BlockSpec((TILE, QK_COLS), rows),
            pl.BlockSpec((TILE, QK_COLS), rows),
            pl.BlockSpec((SEQ, 2 * HEAD_SIZE), whole),
            pl.BlockSpec((SEQ, 2 * HEAD_SIZE), whole),
            pl.BlockSpec((TILE, 1), rows),
            pl.BlockSpec((1, SEQ), whole),
        ],
        out_specs=pl.BlockSpec((SEQ, PACK), whole),
        out_shape=jax.ShapeDtypeStruct((SEQ, PACK), BF),
        scratch_shapes=[pltpu.VMEM((SEQ, HEAD_SIZE), F32), pltpu.VMEM((SEQ, HEAD_SIZE), F32)],
        compiler_params=pltpu.CompilerParams(
            dimension_semantics=("arbitrary",), vmem_limit_bytes=48 * 1024 * 1024
        ),
        cost_estimate=pl.CostEstimate(flops=11_000_000_000, bytes_accessed=8_000_000, transcendentals=3_000_000),
        name="attend_back",
    )(upstream, heads, attended, stats, heads, cosine, sine, cosine, sine, seg_rows, seg_cols)


def rotation(count, by):
    return [(i, (i + by) % count) for i in range(count)]


def straight_four(block, axis):
    return [block, *(lax.ppermute(block, axis, rotation(4, k)) for k in (3, 2, 1))]


def pair_up(own, other, index, axis):
    return jnp.where(index == 0, jnp.stack([own, other], axis=axis), jnp.stack([other, own], axis=axis))


def after(value, *others):
    return lax.optimization_barrier((value, *others))[0]


def gather_pairs(value, partner, index, axis, *others):
    pair = after(pair_up(value, partner, index, 0), *others)
    return lax.all_to_all(jnp.broadcast_to(pair[None], (4, *pair.shape)), axis, 0, 0, tiled=True)


def gather_experts(value, *others):
    partner = lax.ppermute(value, "zl", SWAP)
    return gather_pairs(value, partner, lax.axis_index("zl"), "x", *others).reshape(N_EXP, *value.shape)


def sum_start(*parts):
    x = lax.axis_index("x")
    rows = 2 * TOK

    def rows_for(k):
        start = lax.rem(x + k, 4) * rows
        return sum(lax.dynamic_slice_in_dim(part, start, rows).astype(F32) for part in parts)

    return rows_for(0), [rows_for(k).astype(BF) for k in (2, 1, 3)]


def sum_send(sent):
    return [lax.ppermute(value, "x", rotation(4, k)) for k, value in zip((2, 1, 3), sent)]


def sum_finish(own, arrived):
    zl = lax.axis_index("zl")
    total = own + sum(value.astype(F32) for value in arrived)
    keep = lax.dynamic_slice_in_dim(total, zl * TOK, TOK)
    send = lax.dynamic_slice_in_dim(total, (1 - zl) * TOK, TOK).astype(BF)
    return keep + lax.ppermute(send, "zl", SWAP).astype(F32)


def body(tokens, seg_ids, routes, gain_attn, w_qkv, w_out, gain_moe, w_router, w_gate_up, w_down, cotangent):
    e = lax.axis_index(EXP)
    c = lax.axis_index("c")
    zh = lax.axis_index("zh")

    mine_matrix, other_matrix = parity_matrix(c), parity_matrix(1 - c)
    flat_gu = w_gate_up.reshape(EXP_DEV * 96, 2 * FFE)
    gu_other = dot(flat_gu, other_matrix).astype(BF).reshape(EXP_DEV, 96, FFE)
    gu_recv = core_swap(gu_other)
    gu_mine = dot(flat_gu, mine_matrix).astype(BF).reshape(EXP_DEV, 96, FFE)
    mixed = jnp.concatenate(
        [
            pair_up(gu_mine, gu_recv, c, 1).reshape(EXP_DEV, GU_ROWS, FFE),
            *(w_down[:, :, p * FFE : (p + 1) * FFE] for p in range(WIDTH // FFE)),
        ],
        axis=1,
    )

    def own_columns(start, width):
        return lax.dynamic_slice_in_dim(w_qkv, start + e * width, width, axis=1)

    packet = jnp.concatenate(
        [
            own_columns(0, HEAD_COLS),
            own_columns(WIDTH, HEAD_SIZE),
            own_columns(WIDTH + KEY_VALUE_HEADS * HEAD_SIZE, HEAD_SIZE),
            w_router,
            gain_attn[:, None],
            gain_moe[:, None],
            jnp.zeros((w_qkv.shape[0], PACK - QKV_COLS - EXPERTS - 2), BF),
        ],
        axis=1,
    )
    packet = pair_up(packet, core_swap(packet), c, 0)
    mixed, packet = lax.optimization_barrier((mixed, packet))
    weights = lax.all_gather(mixed, YZ, axis=0, tiled=False)
    packet = pair_up(packet, lax.ppermute(packet, "zh", SWAP), zh, 0)

    tok_packet = jnp.concatenate(
        [tokens[0], routes[0].astype(BF), jnp.zeros((TOK, SIDE - routes.shape[-1]), BF)], axis=1
    )
    tok_pair = pair_up(tok_packet, lax.ppermute(tok_packet, "zl", SWAP), lax.axis_index("zl"), 0)
    tok_pair = after(tok_pair.reshape(2 * TOK, -1), packet)
    tok_blocks = straight_four(tok_pair, "x")
    y = lax.axis_index("y")
    packed = jnp.zeros((4, *packet.shape), BF)
    for k, piece in enumerate(straight_four(packet, "y")):
        packed = lax.dynamic_update_slice(packed, piece[None], (lax.rem(y + k, 4), 0, 0, 0, 0))
    packed = packed.reshape(WIDTH, PACK)
    router = packed[:, QKV_COLS : QKV_COLS + EXPERTS]
    gain_one = packed[:, QKV_COLS + EXPERTS].astype(F32)
    gain_two = packed[:, QKV_COLS + EXPERTS + 1].astype(F32)

    out_partner = lax.ppermute(w_out, ("zl", "zh"), ((0, 3), (1, 2), (2, 1), (3, 0)))
    out_mine = gather_pairs(w_out, out_partner, zh, "y")
    tok_blocks, packed, out_mine = lax.optimization_barrier((tok_blocks, packed, out_mine))

    lanes = jnp.arange(QK_COLS, dtype=jnp.int32)
    inv_freq = THETA ** (-2.0 * (lanes % (HEAD_SIZE // 2)).astype(F32) / HEAD_SIZE)
    angles = jnp.arange(SEQ, dtype=jnp.int32).astype(F32)[:, None] * inv_freq[None, :]
    cosine = jnp.cos(angles)
    sine = jnp.sin(angles) * jnp.where(lanes % HEAD_SIZE < HEAD_SIZE // 2, -1.0, 1.0)
    seg_rows, seg_cols = seg_ids[0][:, None], seg_ids
    tok_all, normed_one, heads, attended, attended_low, stats = attend_call(
        lax.axis_index("x"), tok_blocks, packed, gain_one[None], cosine, sine, seg_rows, seg_cols
    )
    routes_all = tok_all[:, WIDTH:]
    routes_pair = jnp.concatenate([routes_all, core_swap(routes_all)]).astype(jnp.int32)
    routes_turned = ((routes_pair + (EXPERTS - e * EXP_DEV)) % EXPERTS).astype(BF)
    attended_all = to_all(after(attended_low, routes_turned), EXP, N_EXP)
    full_out = jnp.zeros((4, 2, 2, *w_out.shape), BF)
    full_out = lax.dynamic_update_slice(full_out, out_mine[:, :, None], (0, 0, c, 0, 0))
    full_out = lax.dynamic_update_slice(full_out, core_swap(out_mine)[:, :, None], (0, 0, 1 - c, 0, 0))
    full_out = full_out.reshape(N_EXP, HEAD_COLS, WIDTH)

    features = tok_all[:, :WIDTH].astype(F32)
    resid = features + ein("etk,ekn->tn", attended_all, full_out)
    inv_two = rms_inverse(resid)
    normed_two = (resid * inv_two * gain_two).astype(BF)

    cot_partner = lax.ppermute(after(cotangent[0], packed), "zl", SWAP)
    cot_pair = after(pair_up(cotangent[0], cot_partner, lax.axis_index("zl"), 0), weights)
    cot_all = lax.all_gather(cot_pair, "x", axis=0, tiled=False).reshape(SEQ, WIDTH)

    def own_first(value):
        return lax.dynamic_slice_in_dim(
            jnp.concatenate([value, value], axis=1), e * EXP_DEV, EXPERTS, axis=1
        )

    router_turned = jnp.pad(own_first(router), ((0, 0), (0, SIDE - EXPERTS)))
    out_own, out_par, *kept = experts_forward(
        normed_two, core_swap(normed_two), routes_turned, router_turned, weights
    )

    out_rows, out_sent = sum_start(out_own, core_swap(out_par))
    routes_turned, out_sent = lax.optimization_barrier((routes_turned, out_sent))
    out_arrived = sum_send(out_sent)
    back_own, back_par, grad_weights = experts_backward(
        e, cot_all, core_swap(cot_all), routes_turned, kept, weights
    )
    grad_weights, out_arrived = lax.optimization_barrier((grad_weights, out_arrived))
    shard_weights = lax.psum_scatter(grad_weights, YZ, scatter_dimension=0, tiled=False)

    back_rows, back_sent = sum_start(back_own, core_swap(back_par))
    routed_back = sum_finish(back_rows, sum_send(back_sent))
    routed_total, sides = routed_back[:, :WIDTH], routed_back[:, WIDTH:]
    grad_gates = sides[:, :EXPERTS] + sides[:, EXPERTS : 2 * EXPERTS] + sides[:, 2 * EXPERTS : 3 * EXPERTS]

    def own_rows(value):
        return lax.dynamic_slice_in_dim(value, e * TOK, TOK, axis=0)

    resid_own, inv_two_own, normed_two_own = own_rows(resid), own_rows(inv_two), own_rows(normed_two)
    logits = dot(normed_two_own, router)
    picked = jnp.any(routes[0][:, :, None] == jnp.arange(EXPERTS, dtype=jnp.int32), axis=1)
    masked = jnp.where(picked, logits, LARGE_NEGATIVE)
    exps = jnp.where(picked, jnp.exp(masked - jnp.max(masked, axis=-1, keepdims=True)), 0.0)
    gates = exps / jnp.sum(exps, axis=-1, keepdims=True)
    upstream = cotangent[0].astype(F32)
    grad_logits = (
        gates * (grad_gates - jnp.sum(gates * grad_gates, axis=-1, keepdims=True))
    ).astype(BF)
    router_part = dot(normed_two_own.T, grad_logits)
    grad_normed_two = dot(grad_logits, router.T) + routed_total
    grad_rows, gain_two_part = rms_backward(resid_own, inv_two_own, gain_two, grad_normed_two)
    grad_resid = upstream + grad_rows
    grad_branch = grad_resid.astype(BF)
    grad_attended_own = ein("tn,ekn->etk", grad_branch, full_out).astype(BF)
    branch_blocks = jnp.transpose(grad_branch.reshape(TOK, N_EXP, HEAD_COLS), (1, 0, 2))
    back = exchange(jnp.concatenate([grad_attended_own, branch_blocks], axis=-1), EXP)
    back = back.reshape(SEQ, 2 * HEAD_COLS)
    output = (resid_own + sum_finish(out_rows, after(out_arrived, back))).astype(BF)

    grad_projected = attend_back_call(
        back, heads, attended, stats, cosine, sine, seg_rows, seg_cols
    )

    columns = [
        ein("etk,tn->ekn", attended_all, back[:, HEAD_COLS:]).reshape(WIDTH, HEAD_COLS),
        contract(normed_one, grad_projected, ((0,), (0,)))[:, :QKV_COLS],
        router_part,
        gain_two_part[:, None],
        jnp.zeros((WIDTH, DENSE_COLS - HEAD_COLS - QKV_COLS - EXPERTS - 1), F32),
    ]
    parts = jnp.concatenate([column.astype(BF) for column in columns], axis=1)
    parts = parts.reshape(N_YZ, 2, WIDTH // N_FSDP, DENSE_COLS)
    grad_projected, parts = lax.optimization_barrier((grad_projected, parts))
    normed_grad_part = contract(grad_projected, packed, ((1,), (1,)))
    gain_one_part = jnp.sum(features * rms_inverse(features) * normed_grad_part, axis=0)
    gain_blocks = gain_one_part.astype(BF).reshape(N_YZ, 2, WIDTH // N_FSDP, 1)
    parts = jnp.where(jnp.arange(DENSE_COLS, dtype=jnp.int32) == DENSE_COLS - 1, gain_blocks, parts)
    keep = jnp.where(c == 0, parts[:, 0], parts[:, 1])
    arrived = core_swap(jnp.where(c == 0, parts[:, 1], parts[:, 0]))
    parts = (keep.astype(F32) + arrived.astype(F32)).astype(BF)
    normed_rows, normed_sent = sum_start(normed_grad_part.astype(BF))
    normed_arrived = sum_send(normed_sent)
    exchanged = exchange(parts, YZ)

    first_rows, second_rows = shard_weights[:, :96], shard_weights[:, 96:GU_ROWS]
    keep = jnp.where(c == 0, first_rows, second_rows).reshape(-1, FFE)
    arrived = core_swap(jnp.where(c == 0, second_rows, first_rows)).reshape(-1, FFE)
    total_gu = (dot(keep, mine_matrix.T) + dot(arrived, other_matrix.T)).reshape(EXP_DEV, 96, 2 * FFE)
    total_down = jnp.concatenate(
        [shard_weights[:, GU_ROWS + 32 * p : GU_ROWS + 32 * (p + 1)] for p in range(WIDTH // FFE)], axis=2
    ).astype(F32)

    exchanged, normed_arrived, total_gu, total_down = lax.optimization_barrier(
        (exchanged, normed_arrived, total_gu, total_down)
    )
    summed = jnp.sum(exchanged.astype(F32), axis=0).astype(BF)
    totals = to_all(summed, EXP, N_EXP).astype(F32)
    grad_normed_one = sum_finish(normed_rows, after(normed_arrived, summed))

    def head_columns(start, width):
        return jnp.transpose(totals[..., start : start + width], (1, 0, 2)).reshape(-1, N_EXP * width)

    total_out = head_columns(0, HEAD_COLS)
    total_qkv = jnp.concatenate(
        [
            head_columns(HEAD_COLS, HEAD_COLS),
            head_columns(2 * HEAD_COLS, HEAD_SIZE),
            head_columns(2 * HEAD_COLS + HEAD_SIZE, HEAD_SIZE),
        ],
        axis=1,
    )
    shared = jnp.sum(totals[..., HEAD_COLS + QKV_COLS :], axis=0)

    own_tokens = tokens[0].astype(F32)
    grad_in, _ = rms_backward(own_tokens, rms_inverse(own_tokens), gain_one, grad_normed_one)
    grad_tokens = (grad_resid + grad_in).astype(BF)

    return (
        output[None],
        grad_tokens[None],
        shared[:, -1],
        total_qkv,
        total_out,
        shared[:, EXPERTS],
        shared[:, :EXPERTS],
        total_gu,
        total_down,
    )


def solution(mesh):
    fine = Mesh(mesh.devices.reshape(4, 2, 4, 2, 2), ("x", "zl", "y", "zh", "c"))
    rows = P(FSDP, EXP, None)
    weight = P(FSDP, None)
    expert_weight = P(EXP, FSDP, None)
    in_specs = (
        rows,
        P(FSDP, None),
        rows,
        P(FSDP),
        weight,
        weight,
        P(FSDP),
        weight,
        expert_weight,
        expert_weight,
        rows,
    )
    out_specs = (rows, rows, P(FSDP), weight, weight, P(FSDP), weight, expert_weight, expert_weight)
    return jax.shard_map(body, mesh=fine, in_specs=in_specs, out_specs=out_specs, check_vma=False)
```

```python
import math

import jax
import jax.numpy as jnp
from jax import lax
from jax.experimental import pallas as pl
from jax.experimental.pallas import tpu as pltpu
from jax.sharding import Mesh, PartitionSpec as P

QUERY_HEADS = 24
KEY_VALUE_HEADS = 8
HEAD_SIZE = 64
GROUP = QUERY_HEADS // KEY_VALUE_HEADS
FFE = 512
TOP = 8
EXP_DEV = 5
EXPERTS = 40
WIDTH = 1536
TOK = 128
SEQ = 1024
CAP = 48
BLOCKS = 16
N_EXP = 8
N_FSDP = 16
N_YZ = 8
HALF_FFE = FFE // 2
HEAD_COLS = GROUP * HEAD_SIZE
QKV_COLS = HEAD_COLS + 2 * HEAD_SIZE
PACK = 384
DENSE_COLS = 640
SIDE = 128
SLOTS = EXP_DEV * CAP
ROWS = BLOCKS * CAP
PARTS = 4
STEPS = BLOCKS // PARTS
GU_ROWS = WIDTH // N_YZ
MIX_ROWS = GU_ROWS + 32 * WIDTH // FFE
TILE = 256
TILES = SEQ // TILE
QK_COLS = HEAD_COLS + HEAD_SIZE
SCALE = 1.0 / math.sqrt(HEAD_SIZE)

EPS = 1e-06
THETA = 10000.0
LARGE_NEGATIVE = -1e30

EXP = ("x", "zl")
FSDP = ("y", "zh", "c")
YZ = ("y", "zh")
SWAP = ((0, 1), (1, 0))
BF = jnp.bfloat16
F32 = jnp.float32


def dot(a, b):
    return jnp.dot(a, b, preferred_element_type=F32)


def ein(spec, *args):
    return jnp.einsum(spec, *args, preferred_element_type=F32)


def core_swap(value):
    return lax.ppermute(value, "c", SWAP)


def to_all(value, axes, count):
    spread = jnp.broadcast_to(value[None], (count, *value.shape))
    return lax.all_to_all(spread, axes, 0, 0, tiled=True)


def exchange(value, axes):
    return lax.all_to_all(value, axes, 0, 0, tiled=True)


def rms_inverse(features):
    return lax.rsqrt(jnp.mean(features * features, axis=-1, keepdims=True) + EPS)


def rms_backward(features, inverse, gain_vec, grad_normed):
    scaled = gain_vec * grad_normed
    grad_rows = inverse * scaled - features * inverse**3 * jnp.mean(
        features * scaled, axis=-1, keepdims=True
    )
    grad_gain = jnp.sum(features * inverse * grad_normed, axis=0)
    return grad_rows, grad_gain


def parity_matrix(parity):
    rows = jnp.arange(2 * FFE, dtype=jnp.int32)[:, None]
    cols = jnp.arange(FFE, dtype=jnp.int32)[None, :]
    part, rest = cols // HALF_FFE, cols % HALF_FFE
    source = part * FFE + (2 * (rest // 32) + parity) * 32 + rest % 32
    return (rows == source).astype(BF)


def contract(a, b, dims):
    return lax.dot_general(a, b, (dims, ((), ())), preferred_element_type=F32)


def picked_lanes(routes):
    lane = lax.broadcasted_iota(jnp.int32, routes.shape, 1).astype(F32)
    numbers = routes.astype(F32)
    found = lane < 0
    for r in range(TOP):
        found = found | (lane == numbers[:, r : r + 1])
    return found.astype(F32).astype(BF)


def token_square():
    shape = (TOK, TOK)
    return lax.broadcasted_iota(jnp.int32, shape, 0), lax.broadcasted_iota(jnp.int32, shape, 1)


def slots_by_token(picks):
    token, other = token_square()
    ranks = contract(picks, (token < other).astype(BF), ((0,), (0,)))
    named = contract(picks, (token == other).astype(BF), ((0,), (0,)))
    ranks = jnp.where(named > 0, ranks, -1.0).astype(jnp.int32)
    slot = lax.broadcasted_iota(jnp.int32, (CAP, TOK), 0)
    hits = [(slot == ranks[j : j + 1, :]).astype(F32) for j in range(EXP_DEV)]
    return jnp.concatenate(hits, axis=0).astype(BF)


def tokens_by_slot(picks):
    token, other = token_square()
    ranks = jnp.dot((token > other).astype(BF), picks, preferred_element_type=F32).astype(jnp.int32)
    lane = lax.broadcasted_iota(jnp.int32, (TOK, SLOTS), 1)
    hot = jnp.zeros((TOK, SLOTS), F32)
    for j in range(EXP_DEV):
        hit = (picks[:, j : j + 1] > 0) & (lane == ranks[:, j : j + 1] + j * CAP)
        hot = jnp.where(hit, 1.0, hot)
    return hot.astype(BF)


def thirds(value):
    high = value.astype(BF)
    rest = value - high.astype(F32)
    middle = rest.astype(BF)
    return high, middle, (rest - middle.astype(F32)).astype(BF)


def block_rows(ref, start):
    return jnp.concatenate([ref[j, pl.ds(start, CAP), :] for j in range(EXP_DEV)], axis=0)


def expert_weights(ref):
    w_in = ref[:, 0, :GU_ROWS, :].reshape(WIDTH, FFE)
    pieces = [
        ref[:, 0, GU_ROWS + 32 * p : GU_ROWS + 32 * (p + 1), :].reshape(HALF_FFE, FFE)
        for p in range(WIDTH // FFE)
    ]
    return w_in, jnp.concatenate(pieces, axis=1)


def block_start(step, part):
    return pl.multiple_of((step * PARTS + part) * CAP, 16)


def forward_kernel(
    n_own, n_par, routes, router, weights,
    out_own, out_par, x_kept, pre_kept,
    x_slots, gate_slots,
):
    step = pl.program_id(0)

    @pl.when(step < STEPS)
    def dispatch():
        def place(n_ref, part):
            here = slice(part * TOK, (part + 1) * TOK)
            rows = n_ref[here, :]
            picks = picked_lanes(routes[here, :])
            logits = jnp.dot(rows, router[...], preferred_element_type=F32)
            keep = picks > 0
            masked = jnp.where(keep, logits, LARGE_NEGATIVE)
            exps = jnp.where(keep, jnp.exp(masked - jnp.max(masked, axis=-1, keepdims=True)), 0.0)
            gates = exps / jnp.sum(exps, axis=-1, keepdims=True)
            one_hot = slots_by_token(picks)
            spread = sum(jnp.dot(one_hot, third, preferred_element_type=F32) for third in thirds(gates))
            lane = lax.broadcasted_iota(jnp.int32, (CAP, TOK), 1)
            x = jnp.dot(one_hot, rows, preferred_element_type=F32).astype(BF)
            start = block_start(step, part)
            for j in range(EXP_DEV):
                piece = slice(j * CAP, (j + 1) * CAP)
                x_slots[j, pl.ds(start, CAP), :] = x[piece]
                gate_slots[j, pl.ds(start, CAP), :] = jnp.sum(
                    jnp.where(lane == j, spread[piece], 0.0), axis=-1, keepdims=True
                )

        @pl.when(step < STEPS // 2)
        def _():
            for part in range(PARTS):
                place(n_own, part)

        @pl.when(step >= STEPS // 2)
        def _():
            for part in range(PARTS):
                place(n_par, part)

    @pl.when((step >= STEPS) & (step < STEPS + EXP_DEV))
    def experts():
        j = step - STEPS
        w_in, w_back = expert_weights(weights)

        x = x_slots[j]
        gates = gate_slots[j]
        pre = jnp.dot(x, w_in, preferred_element_type=F32)
        x_kept[0] = x
        pre_kept[0, :, :FFE] = pre.astype(BF)
        high, middle, low = thirds(gates)
        lane = lax.broadcasted_iota(jnp.int32, (ROWS, SIDE), 1)
        pre_kept[0, :, FFE:] = jnp.where(
            lane == 0, high.astype(F32), jnp.where(lane == 1, middle.astype(F32), low.astype(F32))
        ).astype(BF)
        gate, up = pre[:, :HALF_FFE], pre[:, HALF_FFE:]
        hidden = (gate * jax.nn.sigmoid(gate) * up).astype(BF).astype(F32)
        gated = (hidden * gates).astype(BF)
        x_slots[j] = jnp.dot(gated, w_back, preferred_element_type=F32).astype(BF)

    @pl.when(step >= STEPS + EXP_DEV)
    def combine():
        block = step - STEPS - EXP_DEV

        def write(out_ref, part):
            here = slice(part * TOK, (part + 1) * TOK)
            hot = tokens_by_slot(picked_lanes(routes[here, :]))
            rows = block_rows(x_slots, block_start(block, part))
            out_ref[here, :] = jnp.dot(hot, rows, preferred_element_type=F32).astype(BF)

        @pl.when(block < STEPS // 2)
        def _():
            for part in range(PARTS):
                write(out_own, part)

        @pl.when(block >= STEPS // 2)
        def _():
            for part in range(PARTS):
                write(out_par, part)


def backward_kernel(
    place_ref, g_own, g_par, routes, x_kept, pre_kept, weights,
    back_own, back_par, grads,
    g_slots, side_slots,
):
    step = pl.program_id(0)

    @pl.when(step < STEPS)
    def dispatch():
        def place(g_ref, part):
            here = slice(part * TOK, (part + 1) * TOK)
            one_hot = slots_by_token(picked_lanes(routes[here, :]))
            g = jnp.dot(one_hot, g_ref[here, :], preferred_element_type=F32).astype(BF)
            start = block_start(step, part)
            for j in range(EXP_DEV):
                g_slots[j, pl.ds(start, CAP), :] = g[j * CAP : (j + 1) * CAP]

        @pl.when(step < STEPS // 2)
        def _():
            for part in range(PARTS):
                place(g_own, part)

        @pl.when(step >= STEPS // 2)
        def _():
            for part in range(PARTS):
                place(g_par, part)

    @pl.when((step >= STEPS) & (step < STEPS + EXP_DEV))
    def experts():
        j = step - STEPS
        w_in, w_back = expert_weights(weights)
        g = g_slots[j]
        pre = pre_kept[0, :, :FFE].astype(F32)
        kept = pre_kept[0, :, FFE:].astype(F32)
        gates = kept[:, 0:1] + kept[:, 1:2] + kept[:, 2:3]
        plain = contract(g, w_back, ((1,), (1,)))
        gate, up = pre[:, :HALF_FFE], pre[:, HALF_FFE:]
        sigmoid = jax.nn.sigmoid(gate)
        silu = gate * sigmoid
        hidden = (silu * up).astype(BF).astype(F32)
        gated = (hidden * gates).astype(BF)
        slope = jnp.sum(hidden * plain, axis=-1, keepdims=True)
        high = slope.astype(BF).astype(F32)
        lane = lax.broadcasted_iota(jnp.int32, (ROWS, SIDE), 1)
        row = lax.broadcasted_iota(jnp.int32, (ROWS, SIDE), 0)
        number = place_ref[0] * EXP_DEV + j
        first_lane = jnp.where(row < ROWS // 2, number, number + EXPERTS)
        side_slots[j] = jnp.where(
            lane == first_lane, high, jnp.where(lane == number + 2 * EXPERTS, slope - high, 0.0)
        ).astype(BF)
        grad_hidden = plain * gates
        grad_pre = jnp.concatenate(
            [grad_hidden * up * sigmoid * (1.0 + gate * (1.0 - sigmoid)), grad_hidden * silu], axis=-1
        ).astype(BF)
        grad_down = contract(gated, g, ((0,), (0,))).astype(BF)
        grad_gate_up = contract(x_kept[0], grad_pre, ((0,), (0,))).astype(BF)
        g_slots[j] = contract(grad_pre, w_in, ((1,), (1,))).astype(BF)
        grads[:, 0, :GU_ROWS, :] = grad_gate_up.reshape(N_YZ, GU_ROWS, FFE)
        for p in range(WIDTH // FFE):
            grads[:, 0, GU_ROWS + 32 * p : GU_ROWS + 32 * (p + 1), :] = grad_down[
                :, p * FFE : (p + 1) * FFE
            ].reshape(N_YZ, 32, FFE)

    @pl.when(step >= STEPS + EXP_DEV)
    def combine():
        block = step - STEPS - EXP_DEV

        def write(back_ref, part):
            here = slice(part * TOK, (part + 1) * TOK)
            hot = tokens_by_slot(picked_lanes(routes[here, :]))
            start = block_start(block, part)
            back_ref[here, :WIDTH] = jnp.dot(
                hot, block_rows(g_slots, start), preferred_element_type=F32
            ).astype(BF)
            back_ref[here, WIDTH:] = jnp.dot(
                hot, block_rows(side_slots, start), preferred_element_type=F32
            ).astype(BF)

        @pl.when(block < STEPS // 2)
        def _():
            for part in range(PARTS):
                write(back_own, part)

        @pl.when(block >= STEPS // 2)
        def _():
            for part in range(PARTS):
                write(back_par, part)


HALF_STEPS = STEPS // 2
LAST = STEPS + EXP_DEV
SPAN = PARTS * TOK


def first(i):
    return (jnp.clip(i, 0, HALF_STEPS - 1), 0)


def second(i):
    return (jnp.clip(i - HALF_STEPS, 0, HALF_STEPS - 1), 0)


def any_block(i):
    return (jnp.where(i < LAST, jnp.clip(i, 0, STEPS - 1), i - LAST), 0)


def expert(i):
    return (jnp.clip(i - STEPS, 0, EXP_DEV - 1), 0, 0)


def expert_split(i):
    return (0, jnp.clip(i - STEPS, 0, EXP_DEV - 1), 0, 0)


def out_first(i):
    return (jnp.clip(i - LAST, 0, HALF_STEPS - 1), 0)


def out_second(i):
    return (jnp.clip(i - LAST - HALF_STEPS, 0, HALF_STEPS - 1), 0)


KEPT = [
    pl.BlockSpec((1, ROWS, WIDTH), expert),
    pl.BlockSpec((1, ROWS, FFE + SIDE), expert),
]
WEIGHTS = pl.BlockSpec((N_YZ, 1, MIX_ROWS, FFE), expert_split)


def experts_forward(n_own, n_par, routes, router, weights):
    shape = jax.ShapeDtypeStruct
    return pl.pallas_call(
        forward_kernel,
        grid=(2 * STEPS + EXP_DEV,),
        in_specs=[
            pl.BlockSpec((SPAN, WIDTH), first),
            pl.BlockSpec((SPAN, WIDTH), second),
            pl.BlockSpec((SPAN, SIDE), any_block),
            pl.BlockSpec((WIDTH, SIDE), lambda i: (0, 0)),
            WEIGHTS,
        ],
        out_specs=[pl.BlockSpec((SPAN, WIDTH), out_first), pl.BlockSpec((SPAN, WIDTH), out_second), *KEPT],
        out_shape=[
            shape((SEQ, WIDTH), BF),
            shape((SEQ, WIDTH), BF),
            shape((EXP_DEV, ROWS, WIDTH), BF),
            shape((EXP_DEV, ROWS, FFE + SIDE), BF),
        ],
        scratch_shapes=[pltpu.VMEM((EXP_DEV, ROWS, WIDTH), BF), pltpu.VMEM((EXP_DEV, ROWS, 1), F32)],
        compiler_params=pltpu.CompilerParams(
            dimension_semantics=("arbitrary",), vmem_limit_bytes=56 * 1024 * 1024
        ),
        cost_estimate=pl.CostEstimate(flops=40_000_000_000, bytes_accessed=40_000_000, transcendentals=1_000_000),
        name="experts_forward",
    )(n_own, n_par, routes, router, weights)


def experts_backward(place, g_own, g_par, routes, kept, weights):
    shape = jax.ShapeDtypeStruct
    return pl.pallas_call(
        backward_kernel,
        grid=(2 * STEPS + EXP_DEV,),
        in_specs=[
            pl.BlockSpec(memory_space=pltpu.SMEM),
            pl.BlockSpec((SPAN, WIDTH), first),
            pl.BlockSpec((SPAN, WIDTH), second),
            pl.BlockSpec((SPAN, SIDE), any_block),
            *KEPT,
            WEIGHTS,
        ],
        out_specs=[
            pl.BlockSpec((SPAN, WIDTH + SIDE), out_first),
            pl.BlockSpec((SPAN, WIDTH + SIDE), out_second),
            WEIGHTS,
        ],
        out_shape=[
            shape((SEQ, WIDTH + SIDE), BF),
            shape((SEQ, WIDTH + SIDE), BF),
            shape((N_YZ, EXP_DEV, MIX_ROWS, FFE), BF),
        ],
        scratch_shapes=[
            pltpu.VMEM((EXP_DEV, ROWS, WIDTH), BF),
            pltpu.VMEM((EXP_DEV, ROWS, SIDE), BF),
        ],
        compiler_params=pltpu.CompilerParams(
            dimension_semantics=("arbitrary",), vmem_limit_bytes=60 * 1024 * 1024
        ),
        cost_estimate=pl.CostEstimate(flops=50_000_000_000, bytes_accessed=60_000_000, transcendentals=1_000_000),
        name="experts_backward",
    )(place.reshape(1), g_own, g_par, routes, *kept, weights)


def swap_halves(value):
    width = value.shape[-1]
    lane = lax.broadcasted_iota(jnp.int32, value.shape, 1)
    return jnp.where(
        lane % HEAD_SIZE < HEAD_SIZE // 2,
        pltpu.roll(value, width - HEAD_SIZE // 2, 1),
        pltpu.roll(value, HEAD_SIZE // 2, 1),
    )


def visible_tile(tile, count, seg_rows, seg_cols):
    row = lax.broadcasted_iota(jnp.int32, (TILE, count), 0) + tile * TILE
    col = lax.broadcasted_iota(jnp.int32, (TILE, count), 1)
    return (col <= row) & (seg_rows[...] == seg_cols[:, :count])


def attend_kernel(
    place_ref, block_0, block_1, block_2, block_3, packed, gain, cosine, sine, seg_rows, seg_cols,
    tokens, normed, heads, attended, attended_low, stats, keys, values,
):
    step = pl.program_id(0)
    distance = lax.rem(step - place_ref[0] + TILES, TILES)
    for k, block in enumerate((block_0, block_1, block_2, block_3)):

        @pl.when(distance == k)
        def _(block=block):
            tokens[...] = block[...]

    features = tokens[:, :WIDTH].astype(F32)
    inverse = lax.rsqrt(jnp.mean(features * features, axis=-1, keepdims=True) + EPS)
    rows = (features * inverse * gain[...]).astype(BF)
    normed[...] = rows
    projected = jnp.dot(rows, packed[...], preferred_element_type=F32)
    turned = projected[:, :QK_COLS]
    turned = (turned * cosine[...] + swap_halves(turned) * sine[...]).astype(BF)
    value_rows = projected[:, QK_COLS:QKV_COLS].astype(BF)
    heads[:, :QK_COLS] = turned
    heads[:, QK_COLS:] = jnp.concatenate([value_rows, jnp.zeros_like(value_rows)], axis=1)
    here = pl.ds(pl.multiple_of(step * TILE, TILE), TILE)
    keys[here, :] = turned[:, HEAD_COLS:]
    values[here, :] = value_rows

    for tile in range(TILES):

        @pl.when(step == tile)
        def _(tile=tile):
            count = (tile + 1) * TILE
            visible = visible_tile(tile, count, seg_rows, seg_cols)
            key_rows, value_all = keys[:count, :], values[:count, :]
            parts = []
            for h in range(GROUP):
                query = turned[:, h * HEAD_SIZE : (h + 1) * HEAD_SIZE]
                scores = contract(query, key_rows, ((1,), (1,))) * SCALE
                scores = jnp.where(visible, scores, LARGE_NEGATIVE)
                top = jnp.max(scores, axis=-1, keepdims=True)
                weights = jnp.where(visible, jnp.exp(scores - top), 0.0)
                total = jnp.sum(weights, axis=-1, keepdims=True)
                soft = (weights / total).astype(BF)
                parts.append(jnp.dot(soft, value_all, preferred_element_type=F32))
                stats[:, 2 * h : 2 * h + 1] = top
                stats[:, 2 * h + 1 : 2 * h + 2] = total
            result = jnp.concatenate(parts, axis=1)
            attended[...] = result
            attended_low[...] = result.astype(BF)


def attend_call(place, blocks, packed, gain, cosine, sine, seg_rows, seg_cols):
    def rows(i):
        return (i, 0)

    def whole(i):
        return (0, 0)

    shape = jax.ShapeDtypeStruct
    return pl.pallas_call(
        attend_kernel,
        grid=(TILES,),
        in_specs=[
            pl.BlockSpec(memory_space=pltpu.SMEM),
            *[pl.BlockSpec((TILE, WIDTH + SIDE), whole)] * TILES,
            pl.BlockSpec((WIDTH, PACK), whole),
            pl.BlockSpec((1, WIDTH), whole),
            pl.BlockSpec((TILE, QK_COLS), rows),
            pl.BlockSpec((TILE, QK_COLS), rows),
            pl.BlockSpec((TILE, 1), rows),
            pl.BlockSpec((1, SEQ), whole),
        ],
        out_specs=[
            pl.BlockSpec((TILE, WIDTH + SIDE), rows),
            pl.BlockSpec((TILE, WIDTH), rows),
            pl.BlockSpec((TILE, PACK), rows),
            pl.BlockSpec((TILE, HEAD_COLS), rows),
            pl.BlockSpec((TILE, HEAD_COLS), rows),
            pl.BlockSpec((TILE, 8), rows),
        ],
        out_shape=[
            shape((SEQ, WIDTH + SIDE), BF),
            shape((SEQ, WIDTH), BF),
            shape((SEQ, PACK), BF),
            shape((SEQ, HEAD_COLS), F32),
            shape((SEQ, HEAD_COLS), BF),
            shape((SEQ, 8), F32),
        ],
        scratch_shapes=[pltpu.VMEM((SEQ, HEAD_SIZE), BF), pltpu.VMEM((SEQ, HEAD_SIZE), BF)],
        compiler_params=pltpu.CompilerParams(
            dimension_semantics=("arbitrary",), vmem_limit_bytes=48 * 1024 * 1024
        ),
        cost_estimate=pl.CostEstimate(flops=13_000_000_000, bytes_accessed=12_000_000, transcendentals=3_000_000),
        name="attend",
    )(place.reshape(1), *blocks, packed, gain, cosine, sine, seg_rows, seg_cols)


def attend_back_kernel(
    upstream, heads, attended, stats, all_heads, cosine, sine, all_cosine, all_sine, seg_rows, seg_cols,
    grads, grad_keys, grad_values,
):
    step = pl.program_id(0)

    @pl.when(step == 0)
    def _():
        grad_keys[...] = jnp.zeros_like(grad_keys)
        grad_values[...] = jnp.zeros_like(grad_values)

    for tile in range(TILES):

        @pl.when(step == tile)
        def _(tile=tile):
            count = (tile + 1) * TILE
            visible = visible_tile(tile, count, seg_rows, seg_cols)
            key_rows = all_heads[:count, HEAD_COLS:QK_COLS]
            value_rows = all_heads[:count, QK_COLS:QKV_COLS]
            parts = []
            sum_keys, sum_values = 0.0, 0.0
            for h in range(GROUP):
                columns = slice(h * HEAD_SIZE, (h + 1) * HEAD_SIZE)
                query, grad = heads[:, columns], upstream[:, columns]
                scores = contract(query, key_rows, ((1,), (1,))) * SCALE
                scores = jnp.where(visible, scores, LARGE_NEGATIVE)
                top, total = stats[:, 2 * h : 2 * h + 1], stats[:, 2 * h + 1 : 2 * h + 2]
                soft = jnp.where(visible, jnp.exp(scores - top), 0.0) / total
                delta = jnp.sum(grad.astype(F32) * attended[:, columns], axis=-1, keepdims=True)
                grad_probs = contract(grad, value_rows, ((1,), (1,)))
                grad_scores = (soft * (grad_probs - delta)).astype(BF)
                parts.append(jnp.dot(grad_scores, key_rows, preferred_element_type=F32) * SCALE)
                sum_keys = sum_keys + contract(grad_scores, query, ((0,), (0,)))
                sum_values = sum_values + contract(soft.astype(BF), grad, ((0,), (0,)))
            grad_keys[:count, :] += sum_keys * SCALE
            grad_values[:count, :] += sum_values
            turned = jnp.concatenate([*parts, jnp.zeros_like(parts[0])], axis=1)
            turned = turned * cosine[...] - swap_halves(turned) * sine[...]
            grads[tile * TILE : count, :HEAD_COLS] = turned[:, :HEAD_COLS].astype(BF)

    @pl.when(step == TILES - 1)
    def _():
        both = jnp.concatenate([grad_keys[...], grad_values[...]], axis=1)
        turned = both * all_cosine[...] - swap_halves(both) * all_sine[...]
        lane = lax.broadcasted_iota(jnp.int32, both.shape, 1)
        both = jnp.where(lane < HEAD_SIZE, turned, both)
        grads[:, HEAD_COLS:] = jnp.concatenate([both, jnp.zeros((SEQ, HEAD_SIZE), F32)], axis=1).astype(BF)


def attend_back_call(upstream, heads, attended, stats, cosine, sine, seg_rows, seg_cols):
    def rows(i):
        return (i, 0)

    def whole(i):
        return (0, 0)

    return pl.pallas_call(
        attend_back_kernel,
        grid=(TILES,),
        in_specs=[
            pl.BlockSpec((TILE, 2 * HEAD_COLS), rows),
            pl.BlockSpec((TILE, PACK), rows),
            pl.BlockSpec((TILE, HEAD_COLS), rows),
            pl.BlockSpec((TILE, 8), rows),
            pl.BlockSpec((SEQ, PACK), whole),
            pl.BlockSpec((TILE, QK_COLS), rows),
            pl.BlockSpec((TILE, QK_COLS), rows),
            pl.BlockSpec((SEQ, 2 * HEAD_SIZE), whole),
            pl.BlockSpec((SEQ, 2 * HEAD_SIZE), whole),
            pl.BlockSpec((TILE, 1), rows),
            pl.BlockSpec((1, SEQ), whole),
        ],
        out_specs=pl.BlockSpec((SEQ, PACK), whole),
        out_shape=jax.ShapeDtypeStruct((SEQ, PACK), BF),
        scratch_shapes=[pltpu.VMEM((SEQ, HEAD_SIZE), F32), pltpu.VMEM((SEQ, HEAD_SIZE), F32)],
        compiler_params=pltpu.CompilerParams(
            dimension_semantics=("arbitrary",), vmem_limit_bytes=48 * 1024 * 1024
        ),
        cost_estimate=pl.CostEstimate(flops=11_000_000_000, bytes_accessed=8_000_000, transcendentals=3_000_000),
        name="attend_back",
    )(upstream, heads, attended, stats, heads, cosine, sine, cosine, sine, seg_rows, seg_cols)


def arrange_kernel(totals, total_out, total_qkv, shared):
    blocks = [totals[e].astype(F32) for e in range(N_EXP)]

    def side_by_side(start, width):
        return jnp.concatenate([block[:, start : start + width] for block in blocks], axis=1)

    total_out[...] = side_by_side(0, HEAD_COLS)
    total_qkv[:, :WIDTH] = side_by_side(HEAD_COLS, HEAD_COLS)
    total_qkv[:, WIDTH : WIDTH + KEY_VALUE_HEADS * HEAD_SIZE] = side_by_side(2 * HEAD_COLS, HEAD_SIZE)
    total_qkv[:, WIDTH + KEY_VALUE_HEADS * HEAD_SIZE :] = side_by_side(2 * HEAD_COLS + HEAD_SIZE, HEAD_SIZE)
    shared[...] = sum(block[:, HEAD_COLS + QKV_COLS :] for block in blocks)


def arrange_call(totals):
    rows = totals.shape[1]
    widths = (WIDTH, WIDTH + 2 * KEY_VALUE_HEADS * HEAD_SIZE, SIDE)
    return pl.pallas_call(
        arrange_kernel,
        out_shape=[jax.ShapeDtypeStruct((rows, width), F32) for width in widths],
        compiler_params=pltpu.CompilerParams(vmem_limit_bytes=32 * 1024 * 1024),
        cost_estimate=pl.CostEstimate(flops=1_000_000, bytes_accessed=3_000_000, transcendentals=0),
        name="arrange",
    )(totals)


def small_call(kernel, out_shape, name, *operands):
    return pl.pallas_call(
        kernel,
        in_specs=[
            pl.BlockSpec(memory_space=pltpu.SMEM if operand.ndim == 1 else pltpu.VMEM) for operand in operands
        ],
        out_shape=out_shape,
        compiler_params=pltpu.CompilerParams(vmem_limit_bytes=48 * 1024 * 1024),
        cost_estimate=pl.CostEstimate(flops=0, bytes_accessed=0, transcendentals=0),
        name=name,
    )(*operands)


def line_up_kernel(start, piece_0, piece_1, piece_2, piece_3, lined):
    for k, piece in enumerate((piece_0, piece_1, piece_2, piece_3)):
        lined[pl.ds(lax.rem(start[0] + k, 4), 1)] = piece[...][None]


def line_up(pieces, start):
    shape = jax.ShapeDtypeStruct((4, *pieces[0].shape), pieces[0].dtype)
    return small_call(line_up_kernel, shape, "line_up", start.reshape(1), *pieces)


def both_cores_kernel(core, mine, other, both):
    both[:, :, pl.ds(core[0], 1)] = mine[...][:, :, None]
    both[:, :, pl.ds(1 - core[0], 1)] = other[...][:, :, None]


def both_cores(mine, other, core):
    shape = jax.ShapeDtypeStruct((4, 2, 2, *mine.shape[2:]), mine.dtype)
    return small_call(both_cores_kernel, shape, "both_cores", core.reshape(1), mine, other)


def dense_kernel(core, attended_all, back, normed, grad_projected, packed, side, keep, send, parts):
    branch = back[:, HEAD_COLS:]
    for e in range(N_EXP):
        parts[e * HEAD_COLS : (e + 1) * HEAD_COLS, :HEAD_COLS] = contract(attended_all[e], branch, ((0,), (0,)))
    for half in range(2):
        rows = slice(half * WIDTH // 2, (half + 1) * WIDTH // 2)
        grads = contract(normed[:, rows], grad_projected[...], ((0,), (0,)))
        weight = packed[rows, :].astype(F32)
        gain = weight[:, QKV_COLS + EXPERTS : QKV_COLS + EXPERTS + 1]
        slope = jnp.sum(grads * weight, axis=-1, keepdims=True) / gain
        lane = lax.broadcasted_iota(jnp.int32, (WIDTH // 2, SIDE), 1)
        last = jnp.where(lane == SIDE - 1, slope, side[rows, :])
        parts[rows, HEAD_COLS:] = jnp.concatenate([grads[:, :QKV_COLS], last], axis=1)
    for k in range(N_YZ):
        for ref, index in ((keep, core[0]), (send, 1 - core[0])):
            start = pl.multiple_of((2 * k + index) * (WIDTH // N_FSDP), 8)
            ref[k] = parts[pl.ds(start, WIDTH // N_FSDP), :].astype(BF)


def dense_call(core, attended_all, back, normed, grad_projected, packed, side):
    shape = jax.ShapeDtypeStruct((N_YZ, WIDTH // N_FSDP, DENSE_COLS), BF)
    return pl.pallas_call(
        dense_kernel,
        in_specs=[pl.BlockSpec(memory_space=pltpu.SMEM), *[pl.BlockSpec(memory_space=pltpu.VMEM)] * 6],
        out_shape=[shape, shape],
        scratch_shapes=[pltpu.VMEM((WIDTH, DENSE_COLS), F32)],
        compiler_params=pltpu.CompilerParams(vmem_limit_bytes=48 * 1024 * 1024),
        cost_estimate=pl.CostEstimate(flops=0, bytes_accessed=0, transcendentals=0),
        name="dense",
    )(core.reshape(1), attended_all, back, normed, grad_projected, packed, side)


def rotation(count, by):
    return [(i, (i + by) % count) for i in range(count)]


def straight_four(block, axis):
    return [block, *(lax.ppermute(block, axis, rotation(4, k)) for k in (3, 2, 1))]


def pair_up(own, other, index, axis):
    return jnp.where(index == 0, jnp.stack([own, other], axis=axis), jnp.stack([other, own], axis=axis))


def after(value, *others):
    return lax.optimization_barrier((value, *others))[0]


def sum_start(*parts):
    x = lax.axis_index("x")
    rows = 2 * TOK

    def rows_for(k):
        start = lax.rem(x + k, 4) * rows
        return sum(lax.dynamic_slice_in_dim(part, start, rows).astype(F32) for part in parts)

    return rows_for(0), [rows_for(k).astype(BF) for k in (2, 1, 3)]


def sum_send(sent):
    return [lax.ppermute(value, "x", rotation(4, k)) for k, value in zip((2, 1, 3), sent)]


def sum_finish(own, arrived):
    zl = lax.axis_index("zl")
    total = own + sum(value.astype(F32) for value in arrived)
    keep = lax.dynamic_slice_in_dim(total, zl * TOK, TOK)
    send = lax.dynamic_slice_in_dim(total, (1 - zl) * TOK, TOK).astype(BF)
    return keep + lax.ppermute(send, "zl", SWAP).astype(F32)


def body(tokens, seg_ids, routes, gain_attn, w_qkv, w_out, gain_moe, w_router, w_gate_up, w_down, cotangent):
    e = lax.axis_index(EXP)
    c = lax.axis_index("c")
    zh = lax.axis_index("zh")

    mine_matrix, other_matrix = parity_matrix(c), parity_matrix(1 - c)
    flat_gu = w_gate_up.reshape(EXP_DEV * 96, 2 * FFE)
    gu_other = dot(flat_gu, other_matrix).astype(BF).reshape(EXP_DEV, 96, FFE)
    gu_recv = core_swap(gu_other)
    gu_mine = dot(flat_gu, mine_matrix).astype(BF).reshape(EXP_DEV, 96, FFE)
    mixed = jnp.concatenate(
        [
            pair_up(gu_mine, gu_recv, c, 1).reshape(EXP_DEV, GU_ROWS, FFE),
            *(w_down[:, :, p * FFE : (p + 1) * FFE] for p in range(WIDTH // FFE)),
        ],
        axis=1,
    )

    def own_columns(start, width):
        return lax.dynamic_slice_in_dim(w_qkv, start + e * width, width, axis=1)

    packet = jnp.concatenate(
        [
            own_columns(0, HEAD_COLS),
            own_columns(WIDTH, HEAD_SIZE),
            own_columns(WIDTH + KEY_VALUE_HEADS * HEAD_SIZE, HEAD_SIZE),
            w_router,
            gain_attn[:, None],
            gain_moe[:, None],
            jnp.zeros((w_qkv.shape[0], PACK - QKV_COLS - EXPERTS - 2), BF),
        ],
        axis=1,
    )
    packet = pair_up(packet, core_swap(packet), c, 0)
    packet = pair_up(packet, lax.ppermute(packet, "zh", SWAP), zh, 0)

    tok_packet = jnp.concatenate(
        [tokens[0], routes[0].astype(BF), jnp.zeros((TOK, SIDE - routes.shape[-1]), BF)], axis=1
    )
    tok_pair = pair_up(tok_packet, lax.ppermute(tok_packet, "zl", SWAP), lax.axis_index("zl"), 0)
    out_partner = lax.ppermute(w_out, ("zl", "zh"), ((0, 3), (1, 2), (2, 1), (3, 0)))

    mixed, tok_pair, packet, out_partner = lax.optimization_barrier((mixed, tok_pair, packet, out_partner))
    weights = lax.all_gather(mixed, YZ, axis=0, tiled=False)
    tok_pair = tok_pair.reshape(2 * TOK, -1)
    tok_blocks = straight_four(tok_pair, "x")
    packet_pieces = straight_four(packet, "y")

    tok_blocks, packet_pieces = lax.optimization_barrier((tok_blocks, packet_pieces))
    out_pair = after(pair_up(w_out, out_partner, zh, 0), packet_pieces)
    out_pieces = straight_four(out_pair, "y")
    packed = jnp.zeros((4, *packet.shape), BF)
    for k, piece in enumerate(packet_pieces):
        spot = lax.rem(lax.axis_index("y") + k, 4)
        packed = lax.dynamic_update_slice(packed, piece[None], (spot, 0, 0, 0, 0))
    packed = packed.reshape(WIDTH, PACK)
    router = packed[:, QKV_COLS : QKV_COLS + EXPERTS]
    gain_one = packed[:, QKV_COLS + EXPERTS].astype(F32)
    gain_two = packed[:, QKV_COLS + EXPERTS + 1].astype(F32)

    lanes = jnp.arange(QK_COLS, dtype=jnp.int32)
    inv_freq = THETA ** (-2.0 * (lanes % (HEAD_SIZE // 2)).astype(F32) / HEAD_SIZE)
    angles = jnp.arange(SEQ, dtype=jnp.int32).astype(F32)[:, None] * inv_freq[None, :]
    cosine = jnp.cos(angles)
    sine = jnp.sin(angles) * jnp.where(lanes % HEAD_SIZE < HEAD_SIZE // 2, -1.0, 1.0)
    seg_rows, seg_cols = seg_ids[0][:, None], seg_ids
    tok_all, normed_one, heads, attended, attended_low, stats = attend_call(
        lax.axis_index("x"), tok_blocks, packed, gain_one[None], cosine, sine, seg_rows, seg_cols
    )
    routes_all = tok_all[:, WIDTH:]
    routes_pair = jnp.concatenate([routes_all, core_swap(routes_all)]).astype(jnp.int32)
    routes_turned = ((routes_pair + (EXPERTS - e * EXP_DEV)) % EXPERTS).astype(BF)
    attended_pair = pair_up(attended_low, lax.ppermute(attended_low, "zl", SWAP), lax.axis_index("zl"), 0)
    attended_all = to_all(after(attended_pair, routes_turned), "x", 4).reshape(N_EXP, SEQ, HEAD_COLS)
    out_mine = line_up(after(out_pieces, attended_low), lax.axis_index("y"))
    full_out = both_cores(out_mine, core_swap(out_mine), c)
    full_out = full_out.reshape(N_EXP, HEAD_COLS, WIDTH)

    features = tok_all[:, :WIDTH].astype(F32)
    resid = features + ein("etk,ekn->tn", attended_all, full_out)
    inv_two = rms_inverse(resid)
    normed_two = (resid * inv_two * gain_two).astype(BF)

    cot_partner = lax.ppermute(after(cotangent[0], packed), "zl", SWAP)
    cot_pair = after(pair_up(cotangent[0], cot_partner, lax.axis_index("zl"), 0), weights)
    cot_all = lax.all_gather(cot_pair, "x", axis=0, tiled=False).reshape(SEQ, WIDTH)

    def own_first(value):
        return lax.dynamic_slice_in_dim(
            jnp.concatenate([value, value], axis=1), e * EXP_DEV, EXPERTS, axis=1
        )

    router_turned = jnp.pad(own_first(router), ((0, 0), (0, SIDE - EXPERTS)))
    out_own, out_par, *kept = experts_forward(
        normed_two, core_swap(normed_two), routes_turned, router_turned, weights
    )

    out_rows, out_sent = sum_start(out_own, core_swap(out_par))
    routes_turned, out_sent = lax.optimization_barrier((routes_turned, out_sent))
    out_arrived = sum_send(out_sent)
    back_own, back_par, grad_weights = experts_backward(
        e, cot_all, core_swap(cot_all), routes_turned, kept, weights
    )
    grad_weights, out_arrived = lax.optimization_barrier((grad_weights, out_arrived))
    shard_weights = lax.psum_scatter(grad_weights, YZ, scatter_dimension=0, tiled=False)

    back_rows, back_sent = sum_start(back_own, core_swap(back_par))
    routed_back = sum_finish(back_rows, sum_send(back_sent))
    routed_total, sides = routed_back[:, :WIDTH], routed_back[:, WIDTH:]
    grad_gates = sides[:, :EXPERTS] + sides[:, EXPERTS : 2 * EXPERTS] + sides[:, 2 * EXPERTS : 3 * EXPERTS]

    def own_rows(value):
        return lax.dynamic_slice_in_dim(value, e * TOK, TOK, axis=0)

    resid_own, inv_two_own, normed_two_own = own_rows(resid), own_rows(inv_two), own_rows(normed_two)
    logits = dot(normed_two_own, router)
    picked = jnp.any(routes[0][:, :, None] == jnp.arange(EXPERTS, dtype=jnp.int32), axis=1)
    masked = jnp.where(picked, logits, LARGE_NEGATIVE)
    exps = jnp.where(picked, jnp.exp(masked - jnp.max(masked, axis=-1, keepdims=True)), 0.0)
    gates = exps / jnp.sum(exps, axis=-1, keepdims=True)
    upstream = cotangent[0].astype(F32)
    grad_logits = (
        gates * (grad_gates - jnp.sum(gates * grad_gates, axis=-1, keepdims=True))
    ).astype(BF)
    router_part = dot(normed_two_own.T, grad_logits)
    grad_normed_two = dot(grad_logits, router.T) + routed_total
    grad_rows, gain_two_part = rms_backward(resid_own, inv_two_own, gain_two, grad_normed_two)
    grad_resid = upstream + grad_rows
    grad_branch = grad_resid.astype(BF)
    grad_attended_own = ein("tn,ekn->etk", grad_branch, full_out).astype(BF)
    branch_blocks = jnp.transpose(grad_branch.reshape(TOK, N_EXP, HEAD_COLS), (1, 0, 2))
    back = exchange(jnp.concatenate([grad_attended_own, branch_blocks], axis=-1), EXP)
    back = back.reshape(SEQ, 2 * HEAD_COLS)
    output = (resid_own + sum_finish(out_rows, after(out_arrived, back))).astype(BF)

    grad_projected = attend_back_call(
        back, heads, attended, stats, cosine, sine, seg_rows, seg_cols
    )

    side = jnp.concatenate(
        [router_part, gain_two_part[:, None], jnp.zeros((WIDTH, SIDE - EXPERTS - 1), F32)], axis=1
    )
    normed_grad_part = contract(grad_projected, packed, ((1,), (1,)))
    keep, send = dense_call(c, attended_all, back, normed_one, grad_projected, packed, side)
    parts = (keep.astype(F32) + core_swap(send).astype(F32)).astype(BF)
    normed_rows, normed_sent = sum_start(normed_grad_part.astype(BF))
    normed_arrived = sum_send(normed_sent)
    exchanged = exchange(parts, YZ)

    first_rows, second_rows = shard_weights[:, :96], shard_weights[:, 96:GU_ROWS]
    keep = jnp.where(c == 0, first_rows, second_rows).reshape(-1, FFE)
    arrived = core_swap(jnp.where(c == 0, second_rows, first_rows)).reshape(-1, FFE)
    total_gu = (dot(keep, mine_matrix.T) + dot(arrived, other_matrix.T)).reshape(EXP_DEV, 96, 2 * FFE)
    total_down = jnp.concatenate(
        [shard_weights[:, GU_ROWS + 32 * p : GU_ROWS + 32 * (p + 1)] for p in range(WIDTH // FFE)], axis=2
    ).astype(F32)

    exchanged, normed_arrived, total_gu, total_down = lax.optimization_barrier(
        (exchanged, normed_arrived, total_gu, total_down)
    )
    summed = jnp.sum(exchanged.astype(F32), axis=0).astype(BF)
    totals = to_all(summed, EXP, N_EXP)
    grad_normed_one = sum_finish(normed_rows, after(normed_arrived, summed))
    total_out, total_qkv, shared = arrange_call(totals)

    own_tokens = tokens[0].astype(F32)
    grad_in, _ = rms_backward(own_tokens, rms_inverse(own_tokens), gain_one, grad_normed_one)
    grad_tokens = (grad_resid + grad_in).astype(BF)

    return (
        output[None],
        grad_tokens[None],
        shared[:, SIDE - 1],
        total_qkv,
        total_out,
        shared[:, EXPERTS],
        shared[:, :EXPERTS],
        total_gu,
        total_down,
    )


def solution(mesh):
    fine = Mesh(mesh.devices.reshape(4, 2, 4, 2, 2), ("x", "zl", "y", "zh", "c"))
    rows = P(FSDP, EXP, None)
    weight = P(FSDP, None)
    expert_weight = P(EXP, FSDP, None)
    in_specs = (
        rows,
        P(FSDP, None),
        rows,
        P(FSDP),
        weight,
        weight,
        P(FSDP),
        weight,
        expert_weight,
        expert_weight,
        rows,
    )
    out_specs = (rows, rows, P(FSDP), weight, weight, P(FSDP), weight, expert_weight, expert_weight)
    return jax.shard_map(body, mesh=fine, in_specs=in_specs, out_specs=out_specs, check_vma=False)
```

```python
import math

import jax
import jax.numpy as jnp
from jax import lax
from jax.experimental import pallas as pl
from jax.experimental.pallas import tpu as pltpu
from jax.sharding import Mesh, PartitionSpec as P

QUERY_HEADS = 24
KEY_VALUE_HEADS = 8
HEAD_SIZE = 64
GROUP = QUERY_HEADS // KEY_VALUE_HEADS
FFE = 512
TOP = 8
EXP_DEV = 5
EXPERTS = 40
WIDTH = 1536
TOK = 128
SEQ = 1024
CAP = 48
BLOCKS = 16
N_EXP = 8
N_FSDP = 16
N_YZ = 8
HALF_FFE = FFE // 2
HEAD_COLS = GROUP * HEAD_SIZE
QKV_COLS = HEAD_COLS + 2 * HEAD_SIZE
PACK = 384
DENSE_COLS = 640
SIDE = 128
SLOTS = EXP_DEV * CAP
ROWS = BLOCKS * CAP
PARTS = 4
STEPS = BLOCKS // PARTS
GU_ROWS = WIDTH // N_YZ
MIX_ROWS = GU_ROWS + 32 * WIDTH // FFE
TILE = 256
TILES = SEQ // TILE
QK_COLS = HEAD_COLS + HEAD_SIZE
SCALE = 1.0 / math.sqrt(HEAD_SIZE)

EPS = 1e-06
THETA = 10000.0
LARGE_NEGATIVE = -1e30

EXP = ("x", "zl")
FSDP = ("y", "zh", "c")
YZ = ("y", "zh")
SWAP = ((0, 1), (1, 0))
BF = jnp.bfloat16
F32 = jnp.float32


def dot(a, b):
    return jnp.dot(a, b, preferred_element_type=F32)


def ein(spec, *args):
    return jnp.einsum(spec, *args, preferred_element_type=F32)


def core_swap(value):
    return lax.ppermute(value, "c", SWAP)


def to_all(value, axes, count):
    spread = jnp.broadcast_to(value[None], (count, *value.shape))
    return lax.all_to_all(spread, axes, 0, 0, tiled=True)


def exchange(value, axes):
    return lax.all_to_all(value, axes, 0, 0, tiled=True)


def rms_inverse(features):
    return lax.rsqrt(jnp.mean(features * features, axis=-1, keepdims=True) + EPS)


def rms_backward(features, inverse, gain_vec, grad_normed):
    scaled = gain_vec * grad_normed
    grad_rows = inverse * scaled - features * inverse**3 * jnp.mean(
        features * scaled, axis=-1, keepdims=True
    )
    grad_gain = jnp.sum(features * inverse * grad_normed, axis=0)
    return grad_rows, grad_gain


def parity_matrix(parity):
    rows = jnp.arange(2 * FFE, dtype=jnp.int32)[:, None]
    cols = jnp.arange(FFE, dtype=jnp.int32)[None, :]
    part, rest = cols // HALF_FFE, cols % HALF_FFE
    source = part * FFE + (2 * (rest // 32) + parity) * 32 + rest % 32
    return (rows == source).astype(BF)


def contract(a, b, dims):
    return lax.dot_general(a, b, (dims, ((), ())), preferred_element_type=F32)


def picked_lanes(routes):
    lane = lax.broadcasted_iota(jnp.int32, routes.shape, 1).astype(F32)
    numbers = routes.astype(F32)
    found = lane < 0
    for r in range(TOP):
        found = found | (lane == numbers[:, r : r + 1])
    return found.astype(F32).astype(BF)


def token_square():
    shape = (TOK, TOK)
    return lax.broadcasted_iota(jnp.int32, shape, 0), lax.broadcasted_iota(jnp.int32, shape, 1)


def slots_by_token(picks):
    token, other = token_square()
    ranks = contract(picks, (token < other).astype(BF), ((0,), (0,)))
    named = contract(picks, (token == other).astype(BF), ((0,), (0,)))
    ranks = jnp.where(named > 0, ranks, -1.0).astype(jnp.int32)
    slot = lax.broadcasted_iota(jnp.int32, (CAP, TOK), 0)
    hits = [(slot == ranks[j : j + 1, :]).astype(F32) for j in range(EXP_DEV)]
    return jnp.concatenate(hits, axis=0).astype(BF)


def tokens_by_slot(picks):
    token, other = token_square()
    ranks = jnp.dot((token > other).astype(BF), picks, preferred_element_type=F32).astype(jnp.int32)
    lane = lax.broadcasted_iota(jnp.int32, (TOK, SLOTS), 1)
    hot = jnp.zeros((TOK, SLOTS), F32)
    for j in range(EXP_DEV):
        hit = (picks[:, j : j + 1] > 0) & (lane == ranks[:, j : j + 1] + j * CAP)
        hot = jnp.where(hit, 1.0, hot)
    return hot.astype(BF)


def thirds(value):
    high = value.astype(BF)
    rest = value - high.astype(F32)
    middle = rest.astype(BF)
    return high, middle, (rest - middle.astype(F32)).astype(BF)


def block_rows(ref, start):
    return jnp.concatenate([ref[j, pl.ds(start, CAP), :] for j in range(EXP_DEV)], axis=0)


def expert_weights(ref):
    w_in = ref[:, 0, :GU_ROWS, :].reshape(WIDTH, FFE)
    pieces = [
        ref[:, 0, GU_ROWS + 32 * p : GU_ROWS + 32 * (p + 1), :].reshape(HALF_FFE, FFE)
        for p in range(WIDTH // FFE)
    ]
    return w_in, jnp.concatenate(pieces, axis=1)


def block_start(step, part):
    return pl.multiple_of((step * PARTS + part) * CAP, 16)


def forward_kernel(
    n_own, n_par, routes, router, weights,
    out_own, out_par, x_kept, pre_kept,
    x_slots, gate_slots,
):
    step = pl.program_id(0)

    @pl.when(step < STEPS)
    def dispatch():
        def place(n_ref, part):
            here = slice(part * TOK, (part + 1) * TOK)
            rows = n_ref[here, :]
            picks = picked_lanes(routes[here, :])
            logits = jnp.dot(rows, router[...], preferred_element_type=F32)
            keep = picks > 0
            masked = jnp.where(keep, logits, LARGE_NEGATIVE)
            exps = jnp.where(keep, jnp.exp(masked - jnp.max(masked, axis=-1, keepdims=True)), 0.0)
            gates = exps / jnp.sum(exps, axis=-1, keepdims=True)
            one_hot = slots_by_token(picks)
            spread = sum(jnp.dot(one_hot, third, preferred_element_type=F32) for third in thirds(gates))
            lane = lax.broadcasted_iota(jnp.int32, (CAP, TOK), 1)
            x = jnp.dot(one_hot, rows, preferred_element_type=F32).astype(BF)
            start = block_start(step, part)
            for j in range(EXP_DEV):
                piece = slice(j * CAP, (j + 1) * CAP)
                x_slots[j, pl.ds(start, CAP), :] = x[piece]
                gate_slots[j, pl.ds(start, CAP), :] = jnp.sum(
                    jnp.where(lane == j, spread[piece], 0.0), axis=-1, keepdims=True
                )

        @pl.when(step < STEPS // 2)
        def _():
            for part in range(PARTS):
                place(n_own, part)

        @pl.when(step >= STEPS // 2)
        def _():
            for part in range(PARTS):
                place(n_par, part)

    @pl.when((step >= STEPS) & (step < STEPS + EXP_DEV))
    def experts():
        j = step - STEPS
        w_in, w_back = expert_weights(weights)

        x = x_slots[j]
        gates = gate_slots[j]
        pre = jnp.dot(x, w_in, preferred_element_type=F32)
        x_kept[0] = x
        pre_kept[0, :, :FFE] = pre.astype(BF)
        high, middle, low = thirds(gates)
        lane = lax.broadcasted_iota(jnp.int32, (ROWS, SIDE), 1)
        pre_kept[0, :, FFE:] = jnp.where(
            lane == 0, high.astype(F32), jnp.where(lane == 1, middle.astype(F32), low.astype(F32))
        ).astype(BF)
        gate, up = pre[:, :HALF_FFE], pre[:, HALF_FFE:]
        hidden = (gate * jax.nn.sigmoid(gate) * up).astype(BF).astype(F32)
        gated = (hidden * gates).astype(BF)
        x_slots[j] = jnp.dot(gated, w_back, preferred_element_type=F32).astype(BF)

    @pl.when(step >= STEPS + EXP_DEV)
    def combine():
        block = step - STEPS - EXP_DEV

        def write(out_ref, part):
            here = slice(part * TOK, (part + 1) * TOK)
            hot = tokens_by_slot(picked_lanes(routes[here, :]))
            rows = block_rows(x_slots, block_start(block, part))
            out_ref[here, :] = jnp.dot(hot, rows, preferred_element_type=F32).astype(BF)

        @pl.when(block < STEPS // 2)
        def _():
            for part in range(PARTS):
                write(out_own, part)

        @pl.when(block >= STEPS // 2)
        def _():
            for part in range(PARTS):
                write(out_par, part)


def backward_kernel(
    place_ref, g_own, g_par, routes, x_kept, pre_kept, weights,
    back_own, back_par, grads,
    g_slots, side_slots,
):
    step = pl.program_id(0)

    @pl.when(step < STEPS)
    def dispatch():
        def place(g_ref, part):
            here = slice(part * TOK, (part + 1) * TOK)
            one_hot = slots_by_token(picked_lanes(routes[here, :]))
            g = jnp.dot(one_hot, g_ref[here, :], preferred_element_type=F32).astype(BF)
            start = block_start(step, part)
            for j in range(EXP_DEV):
                g_slots[j, pl.ds(start, CAP), :] = g[j * CAP : (j + 1) * CAP]

        @pl.when(step < STEPS // 2)
        def _():
            for part in range(PARTS):
                place(g_own, part)

        @pl.when(step >= STEPS // 2)
        def _():
            for part in range(PARTS):
                place(g_par, part)

    @pl.when((step >= STEPS) & (step < STEPS + EXP_DEV))
    def experts():
        j = step - STEPS
        w_in, w_back = expert_weights(weights)
        g = g_slots[j]
        pre = pre_kept[0, :, :FFE].astype(F32)
        kept = pre_kept[0, :, FFE:].astype(F32)
        gates = kept[:, 0:1] + kept[:, 1:2] + kept[:, 2:3]
        plain = contract(g, w_back, ((1,), (1,)))
        gate, up = pre[:, :HALF_FFE], pre[:, HALF_FFE:]
        sigmoid = jax.nn.sigmoid(gate)
        silu = gate * sigmoid
        hidden = (silu * up).astype(BF).astype(F32)
        gated = (hidden * gates).astype(BF)
        slope = jnp.sum(hidden * plain, axis=-1, keepdims=True)
        high = slope.astype(BF).astype(F32)
        lane = lax.broadcasted_iota(jnp.int32, (ROWS, SIDE), 1)
        row = lax.broadcasted_iota(jnp.int32, (ROWS, SIDE), 0)
        number = place_ref[0] * EXP_DEV + j
        first_lane = jnp.where(row < ROWS // 2, number, number + EXPERTS)
        side_slots[j] = jnp.where(
            lane == first_lane, high, jnp.where(lane == number + 2 * EXPERTS, slope - high, 0.0)
        ).astype(BF)
        grad_hidden = plain * gates
        grad_pre = jnp.concatenate(
            [grad_hidden * up * sigmoid * (1.0 + gate * (1.0 - sigmoid)), grad_hidden * silu], axis=-1
        ).astype(BF)
        grad_down = contract(gated, g, ((0,), (0,))).astype(BF)
        grad_gate_up = contract(x_kept[0], grad_pre, ((0,), (0,))).astype(BF)
        g_slots[j] = contract(grad_pre, w_in, ((1,), (1,))).astype(BF)
        grads[:, 0, :GU_ROWS, :] = grad_gate_up.reshape(N_YZ, GU_ROWS, FFE)
        for p in range(WIDTH // FFE):
            grads[:, 0, GU_ROWS + 32 * p : GU_ROWS + 32 * (p + 1), :] = grad_down[
                :, p * FFE : (p + 1) * FFE
            ].reshape(N_YZ, 32, FFE)

    @pl.when(step >= STEPS + EXP_DEV)
    def combine():
        block = step - STEPS - EXP_DEV

        def write(back_ref, part):
            here = slice(part * TOK, (part + 1) * TOK)
            hot = tokens_by_slot(picked_lanes(routes[here, :]))
            start = block_start(block, part)
            back_ref[here, :WIDTH] = jnp.dot(
                hot, block_rows(g_slots, start), preferred_element_type=F32
            ).astype(BF)
            back_ref[here, WIDTH:] = jnp.dot(
                hot, block_rows(side_slots, start), preferred_element_type=F32
            ).astype(BF)

        @pl.when(block < STEPS // 2)
        def _():
            for part in range(PARTS):
                write(back_own, part)

        @pl.when(block >= STEPS // 2)
        def _():
            for part in range(PARTS):
                write(back_par, part)


HALF_STEPS = STEPS // 2
LAST = STEPS + EXP_DEV
SPAN = PARTS * TOK


def first(i):
    return (jnp.clip(i, 0, HALF_STEPS - 1), 0)


def second(i):
    return (jnp.clip(i - HALF_STEPS, 0, HALF_STEPS - 1), 0)


def any_block(i):
    return (jnp.where(i < LAST, jnp.clip(i, 0, STEPS - 1), i - LAST), 0)


def expert(i):
    return (jnp.clip(i - STEPS, 0, EXP_DEV - 1), 0, 0)


def expert_split(i):
    return (0, jnp.clip(i - STEPS, 0, EXP_DEV - 1), 0, 0)


def out_first(i):
    return (jnp.clip(i - LAST, 0, HALF_STEPS - 1), 0)


def out_second(i):
    return (jnp.clip(i - LAST - HALF_STEPS, 0, HALF_STEPS - 1), 0)


KEPT = [
    pl.BlockSpec((1, ROWS, WIDTH), expert),
    pl.BlockSpec((1, ROWS, FFE + SIDE), expert),
]
WEIGHTS = pl.BlockSpec((N_YZ, 1, MIX_ROWS, FFE), expert_split)


def experts_forward(n_own, n_par, routes, router, weights):
    shape = jax.ShapeDtypeStruct
    return pl.pallas_call(
        forward_kernel,
        grid=(2 * STEPS + EXP_DEV,),
        in_specs=[
            pl.BlockSpec((SPAN, WIDTH), first),
            pl.BlockSpec((SPAN, WIDTH), second),
            pl.BlockSpec((SPAN, SIDE), any_block),
            pl.BlockSpec((WIDTH, SIDE), lambda i: (0, 0)),
            WEIGHTS,
        ],
        out_specs=[pl.BlockSpec((SPAN, WIDTH), out_first), pl.BlockSpec((SPAN, WIDTH), out_second), *KEPT],
        out_shape=[
            shape((SEQ, WIDTH), BF),
            shape((SEQ, WIDTH), BF),
            shape((EXP_DEV, ROWS, WIDTH), BF),
            shape((EXP_DEV, ROWS, FFE + SIDE), BF),
        ],
        scratch_shapes=[pltpu.VMEM((EXP_DEV, ROWS, WIDTH), BF), pltpu.VMEM((EXP_DEV, ROWS, 1), F32)],
        compiler_params=pltpu.CompilerParams(
            dimension_semantics=("arbitrary",), vmem_limit_bytes=56 * 1024 * 1024
        ),
        cost_estimate=pl.CostEstimate(flops=40_000_000_000, bytes_accessed=40_000_000, transcendentals=1_000_000),
        name="experts_forward",
    )(n_own, n_par, routes, router, weights)


def experts_backward(place, g_own, g_par, routes, kept, weights):
    shape = jax.ShapeDtypeStruct
    return pl.pallas_call(
        backward_kernel,
        grid=(2 * STEPS + EXP_DEV,),
        in_specs=[
            pl.BlockSpec(memory_space=pltpu.SMEM),
            pl.BlockSpec((SPAN, WIDTH), first),
            pl.BlockSpec((SPAN, WIDTH), second),
            pl.BlockSpec((SPAN, SIDE), any_block),
            *KEPT,
            WEIGHTS,
        ],
        out_specs=[
            pl.BlockSpec((SPAN, WIDTH + SIDE), out_first),
            pl.BlockSpec((SPAN, WIDTH + SIDE), out_second),
            WEIGHTS,
        ],
        out_shape=[
            shape((SEQ, WIDTH + SIDE), BF),
            shape((SEQ, WIDTH + SIDE), BF),
            shape((N_YZ, EXP_DEV, MIX_ROWS, FFE), BF),
        ],
        scratch_shapes=[
            pltpu.VMEM((EXP_DEV, ROWS, WIDTH), BF),
            pltpu.VMEM((EXP_DEV, ROWS, SIDE), BF),
        ],
        compiler_params=pltpu.CompilerParams(
            dimension_semantics=("arbitrary",), vmem_limit_bytes=60 * 1024 * 1024
        ),
        cost_estimate=pl.CostEstimate(flops=50_000_000_000, bytes_accessed=60_000_000, transcendentals=1_000_000),
        name="experts_backward",
    )(place.reshape(1), g_own, g_par, routes, *kept, weights)


def swap_halves(value):
    width = value.shape[-1]
    lane = lax.broadcasted_iota(jnp.int32, value.shape, 1)
    return jnp.where(
        lane % HEAD_SIZE < HEAD_SIZE // 2,
        pltpu.roll(value, width - HEAD_SIZE // 2, 1),
        pltpu.roll(value, HEAD_SIZE // 2, 1),
    )


def visible_tile(tile, count, seg_rows, seg_cols):
    row = lax.broadcasted_iota(jnp.int32, (TILE, count), 0) + tile * TILE
    col = lax.broadcasted_iota(jnp.int32, (TILE, count), 1)
    return (col <= row) & (seg_rows[...] == seg_cols[:, :count])


def attend_kernel(
    place_ref, block_0, block_1, block_2, block_3, packed, gain, cosine, sine, seg_rows, seg_cols,
    tokens, normed, heads, attended, attended_low, stats, keys, values,
):
    step = pl.program_id(0)
    distance = lax.rem(step - place_ref[0] + TILES, TILES)
    for k, block in enumerate((block_0, block_1, block_2, block_3)):

        @pl.when(distance == k)
        def _(block=block):
            tokens[...] = block[...]

    features = tokens[:, :WIDTH].astype(F32)
    inverse = lax.rsqrt(jnp.mean(features * features, axis=-1, keepdims=True) + EPS)
    rows = (features * inverse * gain[...]).astype(BF)
    normed[...] = rows
    projected = jnp.dot(rows, packed[...], preferred_element_type=F32)
    turned = projected[:, :QK_COLS]
    turned = (turned * cosine[...] + swap_halves(turned) * sine[...]).astype(BF)
    value_rows = projected[:, QK_COLS:QKV_COLS].astype(BF)
    heads[:, :QK_COLS] = turned
    heads[:, QK_COLS:] = jnp.concatenate([value_rows, jnp.zeros_like(value_rows)], axis=1)
    here = pl.ds(pl.multiple_of(step * TILE, TILE), TILE)
    keys[here, :] = turned[:, HEAD_COLS:]
    values[here, :] = value_rows

    for tile in range(TILES):

        @pl.when(step == tile)
        def _(tile=tile):
            count = (tile + 1) * TILE
            visible = visible_tile(tile, count, seg_rows, seg_cols)
            key_rows, value_all = keys[:count, :], values[:count, :]
            parts = []
            for h in range(GROUP):
                query = turned[:, h * HEAD_SIZE : (h + 1) * HEAD_SIZE]
                scores = contract(query, key_rows, ((1,), (1,))) * SCALE
                scores = jnp.where(visible, scores, LARGE_NEGATIVE)
                top = jnp.max(scores, axis=-1, keepdims=True)
                weights = jnp.where(visible, jnp.exp(scores - top), 0.0)
                total = jnp.sum(weights, axis=-1, keepdims=True)
                soft = (weights / total).astype(BF)
                parts.append(jnp.dot(soft, value_all, preferred_element_type=F32))
                stats[:, 2 * h : 2 * h + 1] = top
                stats[:, 2 * h + 1 : 2 * h + 2] = total
            result = jnp.concatenate(parts, axis=1)
            attended[...] = result
            attended_low[...] = result.astype(BF)


def attend_call(place, blocks, packed, gain, cosine, sine, seg_rows, seg_cols):
    def rows(i):
        return (i, 0)

    def whole(i):
        return (0, 0)

    shape = jax.ShapeDtypeStruct
    return pl.pallas_call(
        attend_kernel,
        grid=(TILES,),
        in_specs=[
            pl.BlockSpec(memory_space=pltpu.SMEM),
            *[pl.BlockSpec((TILE, WIDTH + SIDE), whole)] * TILES,
            pl.BlockSpec((WIDTH, PACK), whole),
            pl.BlockSpec((1, WIDTH), whole),
            pl.BlockSpec((TILE, QK_COLS), rows),
            pl.BlockSpec((TILE, QK_COLS), rows),
            pl.BlockSpec((TILE, 1), rows),
            pl.BlockSpec((1, SEQ), whole),
        ],
        out_specs=[
            pl.BlockSpec((TILE, WIDTH + SIDE), rows),
            pl.BlockSpec((TILE, WIDTH), rows),
            pl.BlockSpec((TILE, PACK), rows),
            pl.BlockSpec((TILE, HEAD_COLS), rows),
            pl.BlockSpec((TILE, HEAD_COLS), rows),
            pl.BlockSpec((TILE, 8), rows),
        ],
        out_shape=[
            shape((SEQ, WIDTH + SIDE), BF),
            shape((SEQ, WIDTH), BF),
            shape((SEQ, PACK), BF),
            shape((SEQ, HEAD_COLS), F32),
            shape((SEQ, HEAD_COLS), BF),
            shape((SEQ, 8), F32),
        ],
        scratch_shapes=[pltpu.VMEM((SEQ, HEAD_SIZE), BF), pltpu.VMEM((SEQ, HEAD_SIZE), BF)],
        compiler_params=pltpu.CompilerParams(
            dimension_semantics=("arbitrary",), vmem_limit_bytes=48 * 1024 * 1024
        ),
        cost_estimate=pl.CostEstimate(flops=13_000_000_000, bytes_accessed=12_000_000, transcendentals=3_000_000),
        name="attend",
    )(place.reshape(1), *blocks, packed, gain, cosine, sine, seg_rows, seg_cols)


def attend_back_kernel(
    upstream, heads, attended, stats, all_heads, cosine, sine, all_cosine, all_sine, seg_rows, seg_cols,
    grads, grad_keys, grad_values,
):
    step = pl.program_id(0)

    @pl.when(step == 0)
    def _():
        grad_keys[...] = jnp.zeros_like(grad_keys)
        grad_values[...] = jnp.zeros_like(grad_values)

    for tile in range(TILES):

        @pl.when(step == tile)
        def _(tile=tile):
            count = (tile + 1) * TILE
            visible = visible_tile(tile, count, seg_rows, seg_cols)
            key_rows = all_heads[:count, HEAD_COLS:QK_COLS]
            value_rows = all_heads[:count, QK_COLS:QKV_COLS]
            parts = []
            sum_keys, sum_values = 0.0, 0.0
            for h in range(GROUP):
                columns = slice(h * HEAD_SIZE, (h + 1) * HEAD_SIZE)
                query, grad = heads[:, columns], upstream[:, columns]
                scores = contract(query, key_rows, ((1,), (1,))) * SCALE
                scores = jnp.where(visible, scores, LARGE_NEGATIVE)
                top, total = stats[:, 2 * h : 2 * h + 1], stats[:, 2 * h + 1 : 2 * h + 2]
                soft = jnp.where(visible, jnp.exp(scores - top), 0.0) / total
                delta = jnp.sum(grad.astype(F32) * attended[:, columns], axis=-1, keepdims=True)
                grad_probs = contract(grad, value_rows, ((1,), (1,)))
                grad_scores = (soft * (grad_probs - delta)).astype(BF)
                parts.append(jnp.dot(grad_scores, key_rows, preferred_element_type=F32) * SCALE)
                sum_keys = sum_keys + contract(grad_scores, query, ((0,), (0,)))
                sum_values = sum_values + contract(soft.astype(BF), grad, ((0,), (0,)))
            grad_keys[:count, :] += sum_keys * SCALE
            grad_values[:count, :] += sum_values
            turned = jnp.concatenate([*parts, jnp.zeros_like(parts[0])], axis=1)
            turned = turned * cosine[...] - swap_halves(turned) * sine[...]
            grads[tile * TILE : count, :HEAD_COLS] = turned[:, :HEAD_COLS].astype(BF)

    @pl.when(step == TILES - 1)
    def _():
        both = jnp.concatenate([grad_keys[...], grad_values[...]], axis=1)
        turned = both * all_cosine[...] - swap_halves(both) * all_sine[...]
        lane = lax.broadcasted_iota(jnp.int32, both.shape, 1)
        both = jnp.where(lane < HEAD_SIZE, turned, both)
        grads[:, HEAD_COLS:] = jnp.concatenate([both, jnp.zeros((SEQ, HEAD_SIZE), F32)], axis=1).astype(BF)


def attend_back_call(upstream, heads, attended, stats, cosine, sine, seg_rows, seg_cols):
    def rows(i):
        return (i, 0)

    def whole(i):
        return (0, 0)

    return pl.pallas_call(
        attend_back_kernel,
        grid=(TILES,),
        in_specs=[
            pl.BlockSpec((TILE, 2 * HEAD_COLS), rows),
            pl.BlockSpec((TILE, PACK), rows),
            pl.BlockSpec((TILE, HEAD_COLS), rows),
            pl.BlockSpec((TILE, 8), rows),
            pl.BlockSpec((SEQ, PACK), whole),
            pl.BlockSpec((TILE, QK_COLS), rows),
            pl.BlockSpec((TILE, QK_COLS), rows),
            pl.BlockSpec((SEQ, 2 * HEAD_SIZE), whole),
            pl.BlockSpec((SEQ, 2 * HEAD_SIZE), whole),
            pl.BlockSpec((TILE, 1), rows),
            pl.BlockSpec((1, SEQ), whole),
        ],
        out_specs=pl.BlockSpec((SEQ, PACK), whole),
        out_shape=jax.ShapeDtypeStruct((SEQ, PACK), BF),
        scratch_shapes=[pltpu.VMEM((SEQ, HEAD_SIZE), F32), pltpu.VMEM((SEQ, HEAD_SIZE), F32)],
        compiler_params=pltpu.CompilerParams(
            dimension_semantics=("arbitrary",), vmem_limit_bytes=48 * 1024 * 1024
        ),
        cost_estimate=pl.CostEstimate(flops=11_000_000_000, bytes_accessed=8_000_000, transcendentals=3_000_000),
        name="attend_back",
    )(upstream, heads, attended, stats, heads, cosine, sine, cosine, sine, seg_rows, seg_cols)


def arrange_kernel(totals, total_out, total_qkv, shared):
    blocks = [totals[e].astype(F32) for e in range(N_EXP)]

    def side_by_side(start, width):
        return jnp.concatenate([block[:, start : start + width] for block in blocks], axis=1)

    total_out[...] = side_by_side(0, HEAD_COLS)
    total_qkv[:, :WIDTH] = side_by_side(HEAD_COLS, HEAD_COLS)
    total_qkv[:, WIDTH : WIDTH + KEY_VALUE_HEADS * HEAD_SIZE] = side_by_side(2 * HEAD_COLS, HEAD_SIZE)
    total_qkv[:, WIDTH + KEY_VALUE_HEADS * HEAD_SIZE :] = side_by_side(2 * HEAD_COLS + HEAD_SIZE, HEAD_SIZE)
    shared[...] = sum(block[:, HEAD_COLS + QKV_COLS :] for block in blocks)


def arrange_call(totals):
    rows = totals.shape[1]
    widths = (WIDTH, WIDTH + 2 * KEY_VALUE_HEADS * HEAD_SIZE, SIDE)
    return pl.pallas_call(
        arrange_kernel,
        out_shape=[jax.ShapeDtypeStruct((rows, width), F32) for width in widths],
        compiler_params=pltpu.CompilerParams(vmem_limit_bytes=32 * 1024 * 1024),
        cost_estimate=pl.CostEstimate(flops=1_000_000, bytes_accessed=3_000_000, transcendentals=0),
        name="arrange",
    )(totals)


def small_call(kernel, out_shape, name, *operands):
    return pl.pallas_call(
        kernel,
        in_specs=[
            pl.BlockSpec(memory_space=pltpu.SMEM if operand.ndim == 1 else pltpu.VMEM) for operand in operands
        ],
        out_shape=out_shape,
        compiler_params=pltpu.CompilerParams(vmem_limit_bytes=48 * 1024 * 1024),
        cost_estimate=pl.CostEstimate(flops=0, bytes_accessed=0, transcendentals=0),
        name=name,
    )(*operands)


def line_up_kernel(start, piece_0, piece_1, piece_2, piece_3, lined):
    for k, piece in enumerate((piece_0, piece_1, piece_2, piece_3)):
        lined[pl.ds(lax.rem(start[0] + k, 4), 1)] = piece[...][None]


def line_up(pieces, start):
    shape = jax.ShapeDtypeStruct((4, *pieces[0].shape), pieces[0].dtype)
    return small_call(line_up_kernel, shape, "line_up", start.reshape(1), *pieces)


def both_cores_kernel(core, mine, other, both):
    both[:, :, pl.ds(core[0], 1)] = mine[...][:, :, None]
    both[:, :, pl.ds(1 - core[0], 1)] = other[...][:, :, None]


def both_cores(mine, other, core):
    shape = jax.ShapeDtypeStruct((4, 2, 2, *mine.shape[2:]), mine.dtype)
    return small_call(both_cores_kernel, shape, "both_cores", core.reshape(1), mine, other)


def dense_kernel(core, attended_all, back, normed, grad_projected, packed, side, keep, send, parts):
    branch = back[:, HEAD_COLS:]
    for e in range(N_EXP):
        parts[e * HEAD_COLS : (e + 1) * HEAD_COLS, :HEAD_COLS] = contract(attended_all[e], branch, ((0,), (0,)))
    for half in range(2):
        rows = slice(half * WIDTH // 2, (half + 1) * WIDTH // 2)
        grads = contract(normed[:, rows], grad_projected[...], ((0,), (0,)))
        weight = packed[rows, :].astype(F32)
        gain = weight[:, QKV_COLS + EXPERTS : QKV_COLS + EXPERTS + 1]
        slope = jnp.sum(grads * weight, axis=-1, keepdims=True) / gain
        lane = lax.broadcasted_iota(jnp.int32, (WIDTH // 2, SIDE), 1)
        last = jnp.where(lane == SIDE - 1, slope, side[rows, :])
        parts[rows, HEAD_COLS:] = jnp.concatenate([grads[:, :QKV_COLS], last], axis=1)
    for k in range(N_YZ):
        for ref, index in ((keep, core[0]), (send, 1 - core[0])):
            start = pl.multiple_of((2 * k + index) * (WIDTH // N_FSDP), 8)
            ref[k] = parts[pl.ds(start, WIDTH // N_FSDP), :].astype(BF)


def dense_call(core, attended_all, back, normed, grad_projected, packed, side):
    shape = jax.ShapeDtypeStruct((N_YZ, WIDTH // N_FSDP, DENSE_COLS), BF)
    return pl.pallas_call(
        dense_kernel,
        in_specs=[pl.BlockSpec(memory_space=pltpu.SMEM), *[pl.BlockSpec(memory_space=pltpu.VMEM)] * 6],
        out_shape=[shape, shape],
        scratch_shapes=[pltpu.VMEM((WIDTH, DENSE_COLS), F32)],
        compiler_params=pltpu.CompilerParams(vmem_limit_bytes=48 * 1024 * 1024),
        cost_estimate=pl.CostEstimate(flops=0, bytes_accessed=0, transcendentals=0),
        name="dense",
    )(core.reshape(1), attended_all, back, normed, grad_projected, packed, side)


def rotation(count, by):
    return [(i, (i + by) % count) for i in range(count)]


def straight_four(block, axis):
    return [block, *(lax.ppermute(block, axis, rotation(4, k)) for k in (3, 2, 1))]


def pair_up(own, other, index, axis):
    return jnp.where(index == 0, jnp.stack([own, other], axis=axis), jnp.stack([other, own], axis=axis))


def after(value, *others):
    return lax.optimization_barrier((value, *others))[0]


def sum_start(*parts):
    x = lax.axis_index("x")
    rows = 2 * TOK

    def rows_for(k):
        start = lax.rem(x + k, 4) * rows
        return sum(lax.dynamic_slice_in_dim(part, start, rows).astype(F32) for part in parts)

    return rows_for(0), [rows_for(k).astype(BF) for k in (2, 1, 3)]


def sum_send(sent):
    return [lax.ppermute(value, "x", rotation(4, k)) for k, value in zip((2, 1, 3), sent)]


def sum_finish(own, arrived):
    zl = lax.axis_index("zl")
    total = own + sum(value.astype(F32) for value in arrived)
    keep = lax.dynamic_slice_in_dim(total, zl * TOK, TOK)
    send = lax.dynamic_slice_in_dim(total, (1 - zl) * TOK, TOK).astype(BF)
    return keep + lax.ppermute(send, "zl", SWAP).astype(F32)


def body(tokens, seg_ids, routes, gain_attn, w_qkv, w_out, gain_moe, w_router, w_gate_up, w_down, cotangent):
    e = lax.axis_index(EXP)
    c = lax.axis_index("c")
    zh = lax.axis_index("zh")

    mine_matrix, other_matrix = parity_matrix(c), parity_matrix(1 - c)
    flat_gu = w_gate_up.reshape(EXP_DEV * 96, 2 * FFE)
    gu_other = dot(flat_gu, other_matrix).astype(BF).reshape(EXP_DEV, 96, FFE)
    gu_recv = core_swap(gu_other)
    gu_mine = dot(flat_gu, mine_matrix).astype(BF).reshape(EXP_DEV, 96, FFE)
    mixed = jnp.concatenate(
        [
            pair_up(gu_mine, gu_recv, c, 1).reshape(EXP_DEV, GU_ROWS, FFE),
            *(w_down[:, :, p * FFE : (p + 1) * FFE] for p in range(WIDTH // FFE)),
        ],
        axis=1,
    )

    def own_columns(start, width):
        return lax.dynamic_slice_in_dim(w_qkv, start + e * width, width, axis=1)

    packet = jnp.concatenate(
        [
            own_columns(0, HEAD_COLS),
            own_columns(WIDTH, HEAD_SIZE),
            own_columns(WIDTH + KEY_VALUE_HEADS * HEAD_SIZE, HEAD_SIZE),
            w_router,
            gain_attn[:, None],
            gain_moe[:, None],
            jnp.zeros((w_qkv.shape[0], PACK - QKV_COLS - EXPERTS - 2), BF),
        ],
        axis=1,
    )
    packet = pair_up(packet, core_swap(packet), c, 0)
    packet = pair_up(packet, lax.ppermute(packet, "zh", SWAP), zh, 0)

    tok_packet = jnp.concatenate(
        [tokens[0], routes[0].astype(BF), jnp.zeros((TOK, SIDE - routes.shape[-1]), BF)], axis=1
    )
    tok_pair = pair_up(tok_packet, lax.ppermute(tok_packet, "zl", SWAP), lax.axis_index("zl"), 0)
    out_partner = lax.ppermute(w_out, ("zl", "zh"), ((0, 3), (1, 2), (2, 1), (3, 0)))

    mixed, tok_pair, packet, out_partner = lax.optimization_barrier((mixed, tok_pair, packet, out_partner))
    weights = lax.all_gather(mixed, YZ, axis=0, tiled=False)
    tok_pair = tok_pair.reshape(2 * TOK, -1)
    tok_blocks = straight_four(tok_pair, "x")
    packet_pieces = straight_four(packet, "y")

    tok_blocks, packet_pieces = lax.optimization_barrier((tok_blocks, packet_pieces))
    out_pair = after(pair_up(w_out, out_partner, zh, 0), packet_pieces)
    out_pieces = straight_four(out_pair, "y")
    packed = jnp.zeros((4, *packet.shape), BF)
    for k, piece in enumerate(packet_pieces):
        spot = lax.rem(lax.axis_index("y") + k, 4)
        packed = lax.dynamic_update_slice(packed, piece[None], (spot, 0, 0, 0, 0))
    packed = packed.reshape(WIDTH, PACK)
    router = packed[:, QKV_COLS : QKV_COLS + EXPERTS]
    gain_one = packed[:, QKV_COLS + EXPERTS].astype(F32)
    gain_two = packed[:, QKV_COLS + EXPERTS + 1].astype(F32)

    lanes = jnp.arange(QK_COLS, dtype=jnp.int32)
    inv_freq = THETA ** (-2.0 * (lanes % (HEAD_SIZE // 2)).astype(F32) / HEAD_SIZE)
    angles = jnp.arange(SEQ, dtype=jnp.int32).astype(F32)[:, None] * inv_freq[None, :]
    cosine = jnp.cos(angles)
    sine = jnp.sin(angles) * jnp.where(lanes % HEAD_SIZE < HEAD_SIZE // 2, -1.0, 1.0)
    seg_rows, seg_cols = seg_ids[0][:, None], seg_ids
    tok_all, normed_one, heads, attended, attended_low, stats = attend_call(
        lax.axis_index("x"), tok_blocks, packed, gain_one[None], cosine, sine, seg_rows, seg_cols
    )
    routes_all = tok_all[:, WIDTH:]
    routes_pair = jnp.concatenate([routes_all, core_swap(routes_all)]).astype(jnp.int32)
    routes_turned = ((routes_pair + (EXPERTS - e * EXP_DEV)) % EXPERTS).astype(BF)
    attended_pair = pair_up(attended_low, lax.ppermute(attended_low, "zl", SWAP), lax.axis_index("zl"), 0)
    attended_all = to_all(after(attended_pair, routes_turned), "x", 4).reshape(N_EXP, SEQ, HEAD_COLS)
    out_mine = line_up(after(out_pieces, attended_low), lax.axis_index("y"))
    full_out = both_cores(out_mine, core_swap(out_mine), c)
    full_out = full_out.reshape(N_EXP, HEAD_COLS, WIDTH)

    features = tok_all[:, :WIDTH].astype(F32)
    resid = features + ein("etk,ekn->tn", attended_all, full_out)
    inv_two = rms_inverse(resid)
    normed_two = (resid * inv_two * gain_two).astype(BF)

    cot_partner = lax.ppermute(after(cotangent[0], packed), "zl", SWAP)
    cot_pair = after(pair_up(cotangent[0], cot_partner, lax.axis_index("zl"), 0), weights)
    cot_all = lax.all_gather(cot_pair, "x", axis=0, tiled=False).reshape(SEQ, WIDTH)

    def own_first(value):
        return lax.dynamic_slice_in_dim(
            jnp.concatenate([value, value], axis=1), e * EXP_DEV, EXPERTS, axis=1
        )

    router_turned = jnp.pad(own_first(router), ((0, 0), (0, SIDE - EXPERTS)))
    out_own, out_par, *kept = experts_forward(
        normed_two, core_swap(normed_two), routes_turned, router_turned, weights
    )

    out_rows, out_sent = sum_start(out_own, core_swap(out_par))
    routes_turned, out_sent = lax.optimization_barrier((routes_turned, out_sent))
    out_arrived = sum_send(out_sent)
    back_own, back_par, grad_weights = experts_backward(
        e, cot_all, core_swap(cot_all), routes_turned, kept, weights
    )
    grad_weights, out_arrived = lax.optimization_barrier((grad_weights, out_arrived))
    shard_weights = lax.psum_scatter(grad_weights, YZ, scatter_dimension=0, tiled=False)

    back_rows, back_sent = sum_start(back_own, core_swap(back_par))
    routed_back = sum_finish(back_rows, sum_send(back_sent))
    routed_total, sides = routed_back[:, :WIDTH], routed_back[:, WIDTH:]
    grad_gates = sides[:, :EXPERTS] + sides[:, EXPERTS : 2 * EXPERTS] + sides[:, 2 * EXPERTS : 3 * EXPERTS]

    def own_rows(value):
        return lax.dynamic_slice_in_dim(value, e * TOK, TOK, axis=0)

    resid_own, inv_two_own, normed_two_own = own_rows(resid), own_rows(inv_two), own_rows(normed_two)
    logits = dot(normed_two_own, router)
    picked = jnp.any(routes[0][:, :, None] == jnp.arange(EXPERTS, dtype=jnp.int32), axis=1)
    masked = jnp.where(picked, logits, LARGE_NEGATIVE)
    exps = jnp.where(picked, jnp.exp(masked - jnp.max(masked, axis=-1, keepdims=True)), 0.0)
    gates = exps / jnp.sum(exps, axis=-1, keepdims=True)
    upstream = cotangent[0].astype(F32)
    grad_logits = (
        gates * (grad_gates - jnp.sum(gates * grad_gates, axis=-1, keepdims=True))
    ).astype(BF)
    router_part = dot(normed_two_own.T, grad_logits)
    grad_normed_two = dot(grad_logits, router.T) + routed_total
    grad_rows, gain_two_part = rms_backward(resid_own, inv_two_own, gain_two, grad_normed_two)
    grad_resid = upstream + grad_rows
    grad_branch = grad_resid.astype(BF)
    grad_attended_own = ein("tn,ekn->etk", grad_branch, full_out).astype(BF)
    branch_blocks = jnp.transpose(grad_branch.reshape(TOK, N_EXP, HEAD_COLS), (1, 0, 2))
    back = exchange(jnp.concatenate([grad_attended_own, branch_blocks], axis=-1), EXP)
    back = back.reshape(SEQ, 2 * HEAD_COLS)
    output = (resid_own + sum_finish(out_rows, after(out_arrived, back))).astype(BF)

    grad_projected = attend_back_call(
        back, heads, attended, stats, cosine, sine, seg_rows, seg_cols
    )

    side = jnp.concatenate(
        [router_part, gain_two_part[:, None], jnp.zeros((WIDTH, SIDE - EXPERTS - 1), F32)], axis=1
    )
    normed_grad_part = contract(grad_projected, packed, ((1,), (1,)))
    normed_rows, normed_sent = sum_start(normed_grad_part.astype(BF))
    normed_arrived = sum_send(normed_sent)
    keep, send = dense_call(c, attended_all, back, normed_one, grad_projected, packed, side)
    keep, send, normed_arrived = lax.optimization_barrier((keep, send, normed_arrived))
    parts = (keep.astype(F32) + core_swap(send).astype(F32)).astype(BF)
    exchanged = exchange(parts, YZ)

    first_rows, second_rows = shard_weights[:, :96], shard_weights[:, 96:GU_ROWS]
    keep = jnp.where(c == 0, first_rows, second_rows).reshape(-1, FFE)
    arrived = core_swap(jnp.where(c == 0, second_rows, first_rows)).reshape(-1, FFE)
    total_gu = (dot(keep, mine_matrix.T) + dot(arrived, other_matrix.T)).reshape(EXP_DEV, 96, 2 * FFE)
    total_down = jnp.concatenate(
        [shard_weights[:, GU_ROWS + 32 * p : GU_ROWS + 32 * (p + 1)] for p in range(WIDTH // FFE)], axis=2
    ).astype(F32)

    exchanged, total_gu, total_down = lax.optimization_barrier((exchanged, total_gu, total_down))
    summed = jnp.sum(exchanged.astype(F32), axis=0).astype(BF)
    totals = to_all(summed, EXP, N_EXP)
    grad_normed_one = sum_finish(normed_rows, after(normed_arrived, summed))
    total_out, total_qkv, shared = arrange_call(totals)

    own_tokens = tokens[0].astype(F32)
    grad_in, _ = rms_backward(own_tokens, rms_inverse(own_tokens), gain_one, grad_normed_one)
    grad_tokens = (grad_resid + grad_in).astype(BF)

    return (
        output[None],
        grad_tokens[None],
        shared[:, SIDE - 1],
        total_qkv,
        total_out,
        shared[:, EXPERTS],
        shared[:, :EXPERTS],
        total_gu,
        total_down,
    )


def solution(mesh):
    fine = Mesh(mesh.devices.reshape(4, 2, 4, 2, 2), ("x", "zl", "y", "zh", "c"))
    rows = P(FSDP, EXP, None)
    weight = P(FSDP, None)
    expert_weight = P(EXP, FSDP, None)
    in_specs = (
        rows,
        P(FSDP, None),
        rows,
        P(FSDP),
        weight,
        weight,
        P(FSDP),
        weight,
        expert_weight,
        expert_weight,
        rows,
    )
    out_specs = (rows, rows, P(FSDP), weight, weight, P(FSDP), weight, expert_weight, expert_weight)
    return jax.shard_map(body, mesh=fine, in_specs=in_specs, out_specs=out_specs, check_vma=False)
```
